32 devices in a mesh: fluid: 2 (over core), zon: 8 (over z, x), mer: 2 (over y).
Axes of the slice: x: 2, y: 2, z: 4, core: 2. Of those that a mesh axis runs over, the one named last changes fastest.
Arguments:
- state: float32 [2, 2, 64, 128, 256], P('fluid', None, None, 'zon', 'mer'), may hold values from -6 to 6
- flow: bfloat16 [2, 2, 64, 128, 256], P('fluid', None, None, 'zon', 'mer'), may hold values from -0.5 to 0.5
- diffusion: float32 [2, 2, 64], P('fluid'), may hold values from 0.02 to 0.2
- column_solve: float32 [2, 64, 64], P('fluid'), may hold values from -1 to 1, as said below
- exchange_rate: float32 [2, 2], P('fluid'), may hold values from 0.2 to 0.6
- block_map: int32 [8], P('mer'), may hold values from 0 to 7, as said below
- ice_mask: int32 [8], P('mer'), may hold values from 0 to 1
Outputs:
- final_state: float32 [2, 2, 64, 128, 256], P('fluid', None, None, 'zon', 'mer')
The draws below stay inside these ranges and needn't reach their ends.
Inputs may be any that keep to these rules, and one draw needn't show every extreme that they name: `column_solve`: entries of the vertical inverses lie within this range; their diagonal is positive. `block_map`: each meridional section of 4 blocks, blocks k * 4 to (k + 1) * 4 - 1, is mapped onto itself by a permutation.
All inputs are finite; a program needn't handle non-finite values.
Results may differ from the reference program's by a relative error of at most 0.0003.
Values may be sent and summed in bfloat16 or wider, within the bound.
No kernel may reach another device: no remote copies, remote signals or barrier semaphores. Data moves between devices by JAX's collectives and lax.ppermute only.
A program may use at most 64 MiB of HBM per device.

```python
import math
import jax
import jax.numpy as jnp
from jax import lax

LEV = 64
TRACERS = 2
BLKW = 32
STEPS = 2
NXZ = 128
NY = 256
BPD = 4
NYB = 8


def draw_block_map(key, part):
    sections = NYB // BPD
    section_keys = jax.random.split(key, sections)
    shuffled = jax.vmap(lambda sub_key: jax.random.permutation(sub_key, BPD))(section_keys).astype(jnp.int32)
    offsets = (jnp.arange(sections, dtype=jnp.int32) * BPD)[:, None]
    return (shuffled + offsets).reshape(NYB).astype(jnp.int32)


def draw_column_solve(key, part):
    diag_key, scatter_key = jax.random.split(key)
    identity = jnp.eye(LEV, dtype=jnp.float32)
    diagonal = jax.random.uniform(diag_key, (2, LEV), jnp.float32, 0.7, 0.95)
    scatter_part = jnp.clip(jax.random.normal(scatter_key, (2, LEV, LEV), jnp.float32), -2.5, 2.5) * (0.35 * LEV ** (-0.5))
    return (scatter_part * (1.0 - identity) + diagonal[:, :, None] * identity).astype(jnp.float32)


def place_ends(drawn, stream_key, smallest, high):
    index_at = [jax.random.randint(jax.random.fold_in(stream_key, axis), (), 0, length) for axis, length in enumerate(drawn.shape)]
    longest = drawn.shape.index(max(drawn.shape))
    next_to = index_at[:longest] + [(index_at[longest] + 1) % drawn.shape[longest]] + index_at[longest + 1:]
    return drawn.at[tuple(index_at)].set(smallest).at[tuple(next_to)].set(high)


def block_scale(rng, dims, pieces, least, high):
    factor_of, own = 1.0, jax.random.fold_in(rng, 6)
    for dim, blocks in pieces:
        draws = jnp.exp(jax.random.uniform(jax.random.fold_in(own, dim), (blocks,), jnp.float32, least / len(pieces), high / len(pieces)))
        factor_of = factor_of * jnp.repeat(draws, dims[dim] // blocks).reshape([-1 if axis == dim else 1 for axis in range(len(dims))])
    return factor_of


def bell_draw(key, dims, scale, bound, cuts=(), kind=jnp.bfloat16):
    level = block_scale(key, dims, cuts, -0.22, 0.18) if cuts else 1.0
    result = jax.random.normal(key, dims, jnp.float32) * scale * level
    return jnp.minimum(jnp.maximum(result, -bound), bound).astype(kind)


def setup_inputs(seed: int = 0) -> dict:
    key_of = jax.random.split(jax.random.key(seed), 8)
    return {
        "state": bell_draw(key_of[0], (2, TRACERS, LEV, NXZ, NY), 1.0, 6.0, ((0, 2), (3, 8), (4, 2)), jnp.float32),
        "flow": jnp.clip(jax.random.uniform(key_of[1], (2, 2, LEV, NXZ, NY), jnp.float32, -0.5, 0.5) * block_scale(key_of[1], (2, 2, LEV, NXZ, NY), ((0, 2), (3, 8), (4, 2)), -0.4, 0.0), -0.5, 0.5).astype(jnp.bfloat16),
        "diffusion": jnp.clip(jnp.exp(math.log(0.2) - 2.3025851 * jax.random.uniform(key_of[2], (2, TRACERS, LEV), jnp.float32) ** block_scale(key_of[2], (2, TRACERS, LEV), ((0, 2),), -0.2, 0.2)), 0.02, 0.2),
        "column_solve": draw_column_solve(jax.random.fold_in(key_of[7], 71), 0),
        "exchange_rate": jnp.clip(jnp.exp(math.log(0.6) - 1.0986123 * jax.random.uniform(key_of[4], (2, TRACERS), jnp.float32) ** block_scale(key_of[4], (2, TRACERS), ((0, 2),), -0.2, 0.2)), 0.2, 0.6),
        "block_map": draw_block_map(jax.random.fold_in(key_of[7], 71), 0),
        "ice_mask": place_ends(jax.random.randint(key_of[6], (NYB,), 0, 2), jax.random.fold_in(key_of[6], 1), 0, 1).astype(jnp.int32),
    }


def reference(state, flow, diffusion, column_solve, exchange_rate, block_map, ice_mask):
    positions = jnp.arange(NYB, dtype=jnp.int32)
    inverse = jnp.sum(positions[:, None] * (block_map[:, None] == positions[None, :]).astype(jnp.int32), axis=0).astype(jnp.int32)
    open_cols = (1 - ice_mask).astype(jnp.float32)
    level_ids = jnp.arange(LEV, dtype=jnp.int32)
    tracer_field = state
    for step_index in range(STEPS):
        atm_rows = tracer_field[0, :, LEV - 1].reshape(TRACERS, NXZ, NYB, BLKW)
        ocean_rows = tracer_field[1, :, 0].reshape(TRACERS, NXZ, NYB, BLKW)
        mapped = jnp.take(atm_rows, block_map, axis=2)
        surface_flux = (mapped - ocean_rows) * open_cols[None, None, :, None]
        returned = jnp.take(surface_flux, inverse, axis=2)
        increment = jnp.stack([-exchange_rate[0][:, None, None, None] * returned,
                               exchange_rate[1][:, None, None, None] * surface_flux]).reshape(2, TRACERS, NXZ, NY)
        current = tracer_field

        def slab(slab_index):
            fluid_id = slab_index // TRACERS
            tracer_id = slab_index % TRACERS
            tracer_slab = current[fluid_id, tracer_id]
            zonal_flow = flow[fluid_id, 0].astype(jnp.float32)
            merid_flow = flow[fluid_id, 1].astype(jnp.float32)
            viscous = diffusion[fluid_id, tracer_id][:, None, None]
            east_cell = jnp.roll(tracer_slab, -1, axis=1)
            west_cell = jnp.roll(tracer_slab, 1, axis=1)
            padded = jnp.pad(tracer_slab, ((0, 0), (0, 0), (1, 1)))
            north_cell = padded[:, :, 2:]
            south_cell = padded[:, :, :-2]
            updated = (tracer_slab - 0.5 * zonal_flow * (east_cell - west_cell)
                       - 0.5 * merid_flow * (north_cell - south_cell)
                       + viscous * (east_cell + west_cell + north_cell + south_cell - 4.0 * tracer_slab))
            surface_level = jnp.where(fluid_id == 0, LEV - 1, 0).astype(jnp.int32)
            level_pick = (level_ids == surface_level).astype(jnp.float32)
            updated = updated + level_pick[:, None, None] * increment[fluid_id, tracer_id][None]
            solved = jnp.dot(column_solve[fluid_id], updated.reshape(LEV, NXZ * NY),
                             precision=lax.Precision.HIGHEST, preferred_element_type=jnp.float32)
            return solved.reshape(LEV, NXZ, NY)

        tracer_field = lax.map(slab, jnp.arange(2 * TRACERS, dtype=jnp.int32)).reshape(2, TRACERS, LEV, NXZ, NY)
    return tracer_field
```

```python
import functools

import jax
import jax.numpy as jnp
from jax import lax
from jax.experimental import pallas as pl
from jax.experimental.pallas import tpu as pltpu
from jax.sharding import PartitionSpec as P

STEPS = 2


def pair_route(count, odd):
    if odd:
        return [(i, ((i + 1) ^ 1) - 1 if i + 1 < count else 0) for i in range(count - 1)][1:] + [(0, count - 1), (count - 1, 0)]
    return [(i, i ^ 1) for i in range(count)]


def pair_swap(block, axis, odd):
    return lax.ppermute(block, axis, pair_route(lax.axis_size(axis), odd))


def even_flag(axis):
    return 1 - lax.rem(lax.axis_index(axis), 2)


def send_edges(column, zon_even, mer_even, send_odd, send_even, send_mer, levels, width, tracers):
    at_even = jnp.where(zon_even == 1, width - 1, 0)
    at_odd = jnp.where(zon_even == 1, 0, width - 1)
    lane = lax.broadcasted_iota(jnp.int32, (levels, 128), 1)
    acc = [jnp.zeros((levels, 128), jnp.float32) for _ in send_mer]
    for t in range(tracers):
        send_even[t * levels:(t + 1) * levels, :] = column(t, at_even)
        send_odd[t * levels:(t + 1) * levels, :] = column(t, at_odd)
        for x in range(width):
            j = 2 * (t * width + x)
            cells = column(t, x)
            for r in range(len(send_mer)):
                up = mer_even if r == 0 else 1 - mer_even
                acc[r] = jnp.where(lane == j + up, pltpu.roll(cells, j + 2 * up, 1), acc[r])
    for r, ref in enumerate(send_mer):
        ref[...] = acc[r]


def mer_halo(recv_mer, levels, mer_count):
    place = lax.axis_index("mer")
    even = even_flag("mer")
    lane = lax.broadcasted_iota(jnp.int32, (levels, 128), 1)
    total = jnp.zeros((levels, 128), jnp.float32)
    for r, ref in enumerate(recv_mer):
        north = even if r == 0 else 1 - even
        inside = jnp.where(north == 1, place + 1 < mer_count, place > 0)
        keep = jnp.logical_and(lax.rem(lane, 2) == 1 - north, inside)
        total = total + jnp.where(keep, ref[...], 0.0)
    return total


def increments(own, other, rate, block_map, ice_mask, tracers, width):
    fluid = lax.axis_index("fluid")
    blocks = block_map.shape[0]
    wide = own.shape[1] // blocks
    first = lax.axis_index("mer") * blocks
    is_atm = fluid == 0
    atm = jnp.where(is_atm, own, other)
    ocean = jnp.where(is_atm, other, own)
    block = lax.broadcasted_iota(jnp.int32, own.shape, 1) // wide
    flux = jnp.zeros_like(own)
    for b in range(blocks):
        a = block_map[b] - first
        moved = pltpu.roll(atm, lax.rem((b - a + blocks) * wide, 128), 1)
        flux = jnp.where(block == b, (moved - ocean) * (1 - ice_mask[b]).astype(jnp.float32), flux)
    returned = jnp.zeros_like(own)
    for b in range(blocks):
        a = block_map[b] - first
        moved = pltpu.roll(flux, lax.rem((a - b + blocks) * wide, 128), 1)
        returned = jnp.where(block == a, moved, returned)
    tracer = lax.broadcasted_iota(jnp.int32, own.shape, 0) // width
    scale = jnp.full(own.shape, rate[0])
    for t in range(1, tracers):
        scale = jnp.where(tracer == t, rate[t], scale)
    return jnp.where(is_atm, -returned, flux) * scale


def split3(matrix):
    high = matrix.astype(jnp.bfloat16)
    low = (matrix - high.astype(jnp.float32)).astype(jnp.bfloat16)
    return high, low


def step_body(column, store, east_halo, west_halo, halo, incr, zonal, merid, viscous, weights, levels, width, tracers):
    lane = lax.broadcasted_iota(jnp.int32, (levels, 128), 1)
    top = lane == 127
    bottom = lane == 0
    row = lax.broadcasted_iota(jnp.int32, (levels, 128), 0)
    fluid = lax.axis_index("fluid")
    at_surface = row == jnp.where(fluid == 0, levels - 1, 0)
    for t in range(tracers):
        nu = viscous[t]
        diag = 1.0 - 4.0 * nu
        for x0 in range(0, width, 2):
            parts = []
            for x in (x0, x0 + 1):
                j = t * width + x
                q = column(t, x)
                west = west_halo(t) if x == 0 else column(t, x - 1)
                east = east_halo(t) if x == width - 1 else column(t, x + 1)
                edge = pltpu.roll(halo, (127 - 2 * j) % 128, 1)
                north = jnp.where(top, edge, pltpu.roll(q, 127, 1))
                south = jnp.where(bottom, edge, pltpu.roll(q, 1, 1))
                c = zonal(x)
                d = merid(x)
                u = diag * q + (nu - c) * east + (nu + c) * west + (nu - d) * north + (nu + d) * south
                u = u + jnp.where(at_surface, jnp.broadcast_to(incr[j:j + 1, :], u.shape), 0.0)
                parts.append(u)
            u = jnp.concatenate(parts, axis=1)
            high, low = split3(u)
            solved = jnp.dot(weights, jnp.concatenate([high, low, high], axis=0), preferred_element_type=jnp.float32)
            store(t, x0, solved[:, :128])
            store(t, x0 + 1, solved[:, 128:])


def pack_kernel(dims, state, *outs):
    tracers, levels, width, rounds = dims
    send_odd, send_even, surface = outs[:3]
    column = lambda t, x: state[pl.ds(t * levels * width + x, levels, stride=width), :]
    send_edges(column, even_flag("zon"), even_flag("mer"), send_odd, send_even, outs[3:], levels, width, tracers)
    level = jnp.where(lax.axis_index("fluid") == 0, levels - 1, 0)
    for t in range(tracers):
        start = pl.multiple_of((t * levels + level) * width, 8)
        surface[t * width:(t + 1) * width, :] = state[pl.ds(start, width), :]


def prepare(diffusion, solve, levels, tracers):
    viscous = [jnp.transpose(jnp.broadcast_to(diffusion[t:t + 1, :], (128, levels))) for t in range(tracers)]
    high, low = split3(solve[...])
    return viscous, jnp.concatenate([high, high, low], axis=1)


def halos(recv_odd, recv_even, levels):
    even = even_flag("zon") == 1
    part = lambda ref, t: ref[t * levels:(t + 1) * levels, :]
    east = lambda t: jnp.where(even, part(recv_even, t), part(recv_odd, t))
    west = lambda t: jnp.where(even, part(recv_odd, t), part(recv_even, t))
    return east, west


def first_kernel(dims, mer_count, state, flow, diffusion, solve, rate, block_map, ice_mask, own, other, recv_odd, recv_even, *rest):
    tracers, levels, width, rounds = dims
    recv_mer, rest = rest[:rounds], rest[rounds:]
    fresh, frame, send_odd, send_even, surface = rest[:5]
    send_mer = rest[5:]
    size = levels * width
    for k in range(2):
        frame_k = flow[k * size:(k + 1) * size, :].astype(jnp.float32) * 0.5
        frame[k * size:(k + 1) * size, :] = frame_k
    viscous, weights = prepare(diffusion, solve, levels, tracers)
    east, west = halos(recv_odd, recv_even, levels)
    halo = mer_halo(recv_mer, levels, mer_count)
    incr = increments(own[...], other[...], rate, block_map, ice_mask, tracers, width)
    column = lambda t, x: state[pl.ds(t * size + x, levels, stride=width), :]
    strip = lambda k: lambda x: frame[pl.ds(k * size + x, levels, stride=width), :]

    def store(t, x, value):
        fresh[pl.ds((t * width + x) * levels, levels), :] = value

    step_body(column, store, east, west, halo, incr, strip(0), strip(1), viscous, weights, levels, width, tracers)
    fresh_column = lambda t, x: fresh[pl.ds(pl.multiple_of((t * width + x) * levels, 8), levels), :]
    send_edges(fresh_column, even_flag("zon"), even_flag("mer"), send_odd, send_even, send_mer, levels, width, tracers)
    level = jnp.where(lax.axis_index("fluid") == 0, levels - 1, 0)
    for j in range(tracers * width):
        surface[j:j + 1, :] = fresh[pl.ds(j * levels + level, 1), :]


def last_kernel(dims, mer_count, fresh, frame, diffusion, solve, rate, block_map, ice_mask, own, other, recv_odd, recv_even, *rest):
    tracers, levels, width, rounds = dims
    recv_mer, out = rest[:rounds], rest[rounds]
    size = levels * width
    viscous, weights = prepare(diffusion, solve, levels, tracers)
    east, west = halos(recv_odd, recv_even, levels)
    halo = mer_halo(recv_mer, levels, mer_count)
    incr = increments(own[...], other[...], rate, block_map, ice_mask, tracers, width)
    column = lambda t, x: fresh[pl.ds((t * width + x) * levels, levels), :]
    strip = lambda k: lambda x: frame[pl.ds(k * size + x, levels, stride=width), :]

    def store(t, x, value):
        out[pl.ds(t * size + x, levels, stride=width), :] = value

    step_body(column, store, east, west, halo, incr, strip(0), strip(1), viscous, weights, levels, width, tracers)


VM = pl.BlockSpec(memory_space=pltpu.VMEM)
SM = pl.BlockSpec(memory_space=pltpu.SMEM)


def call(body, name, in_specs, out_shape):
    many = isinstance(out_shape, list)
    return pl.pallas_call(
        body,
        out_shape=out_shape,
        in_specs=in_specs,
        out_specs=[VM] * len(out_shape) if many else VM,
        name=name,
        compiler_params=pltpu.CompilerParams(vmem_limit_bytes=32 * 1024 * 1024),
    )


def on_device(state, flow, diffusion, column_solve, exchange_rate, block_map, ice_mask):
    _, tracers, levels, width, wide = state.shape
    mer_count = lax.axis_size("mer")
    rounds = 1 if mer_count == 2 else 2
    dims = (tracers, levels, width, rounds)
    size = levels * width
    cells = state.reshape(tracers * size, wide)
    flow2 = flow.reshape(2 * size, wide)
    f32 = lambda *shape: jax.ShapeDtypeStruct(shape, jnp.float32)
    packs = [f32(tracers * levels, wide)] * 2 + [f32(tracers * width, wide)] + [f32(levels, 128)] * rounds
    fixed = (diffusion[0], column_solve[0], exchange_rate[0], block_map, ice_mask)
    fixed_specs = [VM, VM, SM, SM, SM]

    def swap(send_odd, send_even, surface, *send_mer):
        moved = [pair_swap(send_odd, "zon", True), pair_swap(send_even, "zon", False)]
        moved += [pair_swap(piece, "mer", r == 1) for r, piece in enumerate(send_mer)]
        return [surface, pair_swap(surface, "fluid", False)] + moved

    packed = call(functools.partial(pack_kernel, dims), "pack", [VM], packs)(cells)
    got = swap(*packed)
    fresh, frame, *packed = call(
        functools.partial(first_kernel, dims, mer_count), "first", [VM, VM] + fixed_specs + [VM] * len(got),
        [f32(tracers * size, wide), f32(2 * size, wide)] + packs,
    )(cells, flow2, *fixed, *got)
    got = swap(*packed)
    done = call(
        functools.partial(last_kernel, dims, mer_count), "last", [VM, VM] + fixed_specs + [VM] * len(got),
        f32(tracers * size, wide),
    )(fresh, frame, *fixed, *got)
    return done.reshape(state.shape)


def solution(mesh):
    return jax.shard_map(
        on_device,
        mesh=mesh,
        in_specs=(
            P("fluid", None, None, "zon", "mer"),
            P("fluid", None, None, "zon", "mer"),
            P("fluid", None, None),
            P("fluid", None, None),
            P("fluid", None),
            P("mer"),
            P("mer"),
        ),
        out_specs=P("fluid", None, None, "zon", "mer"),
        check_vma=False,
    )
```

```python
import functools

import jax
import jax.numpy as jnp
from jax import lax
from jax.experimental import pallas as pl
from jax.experimental.pallas import tpu as pltpu
from jax.sharding import PartitionSpec as P

f32, bf16 = jnp.float32, jnp.bfloat16


def ring(count, ahead):
    return [(i, (i + ahead) % count) for i in range(count)]


def pairs(count, odd):
    if odd:
        return [(i, ((i + 1) ^ 1) - 1) for i in range(1, count - 1)] + [(0, count - 1), (count - 1, 0)]
    return [(i, i ^ 1) for i in range(count)]


def mer_even():
    return 1 - lax.rem(lax.axis_index("mer"), 2)


def surface_level(levels):
    return jnp.where(lax.axis_index("fluid") == 0, levels - 1, 0)


def lanes_of(levels):
    return lax.broadcasted_iota(jnp.int32, (levels, 128), 1)


def split(value):
    high = value.astype(bf16)
    return high, (value - high.astype(f32)).astype(bf16)


def product(weights, value):
    high, low = split(value)
    return jnp.dot(weights, jnp.concatenate([high, low, high], axis=0), preferred_element_type=f32)


def part(ref, index, levels):
    return ref[index * levels:(index + 1) * levels, :]


def mer_halo(recv_mer, levels, mer_count):
    place, even = lax.axis_index("mer"), mer_even()
    lane = lanes_of(levels)
    total = jnp.zeros((levels, 128), f32)
    for r, ref in enumerate(recv_mer):
        north = even if r == 0 else 1 - even
        inside = jnp.where(north == 1, place + 1 < mer_count, place > 0)
        keep = jnp.logical_and(lax.rem(lane, 2) == 1 - north, inside)
        total = total + jnp.where(keep, ref[...], 0.0)
    return total


def pack_lanes(acc, cells, j, lane, even):
    for r in range(len(acc)):
        up = even if r == 0 else 1 - even
        acc[r] = jnp.where(lane == 2 * j + up, pltpu.roll(cells, 2 * j + 2 * up, 1), acc[r])


def both_edges(cells, j):
    return pltpu.roll(cells, (2 * j + 1) % 128, 1)


def at_edges(packed, j):
    return pltpu.roll(packed, (127 - 2 * j) % 128, 1)


def increments(own, other, rate, block_map, ice_mask, tracers, per_tracer):
    blocks = block_map.shape[0]
    wide = own.shape[1] // blocks
    first = lax.axis_index("mer") * blocks
    is_atm = lax.axis_index("fluid") == 0
    atm = jnp.where(is_atm, own, other)
    ocean = jnp.where(is_atm, other, own)
    block = lax.broadcasted_iota(jnp.int32, own.shape, 1) // wide
    flux = jnp.zeros_like(own)
    for b in range(blocks):
        a = block_map[b] - first
        moved = pltpu.roll(atm, lax.rem((b - a + blocks) * wide, 128), 1)
        flux = jnp.where(block == b, (moved - ocean) * (1 - ice_mask[b]).astype(f32), flux)
    returned = jnp.zeros_like(own)
    for b in range(blocks):
        a = block_map[b] - first
        moved = pltpu.roll(flux, lax.rem((a - b + blocks) * wide, 128), 1)
        returned = jnp.where(block == a, moved, returned)
    tracer = lax.broadcasted_iota(jnp.int32, own.shape, 0) // per_tracer
    scale = jnp.full(own.shape, rate[0])
    for t in range(1, tracers):
        scale = jnp.where(tracer == t, rate[t], scale)
    return jnp.where(is_atm, -returned, flux) * scale


def horizontal(q, east, west, c, d, nu, lane):
    north = jnp.where(lane == 127, 0.0, pltpu.roll(q, 127, 1))
    south = jnp.where(lane == 0, 0.0, pltpu.roll(q, 1, 1))
    return q - c * (east - west) - d * (north - south) + nu * ((east + west) + (north + south) - 4.0 * q)


def interior(column, strip, nu, weights, store, dims):
    tracers, levels, width = dims
    lane = lanes_of(levels)
    zero = jnp.zeros((levels, 128), f32)
    for x in range(width):
        c, d = strip(0, x), strip(1, x)
        terms = []
        for t in range(tracers):
            west = zero if x == 0 else column(t, x - 1)
            east = zero if x == width - 1 else column(t, x + 1)
            terms.append(horizontal(column(t, x), east, west, c, d, part(nu, t, levels), lane))
        solved = product(weights[...], jnp.concatenate(terms, axis=1))
        for t in range(tracers):
            store(t, x, solved[:, t * 128:(t + 1) * 128])


def pack_kernel(dims, cells, flow, diffusion, solve, rate, block_map, ice_mask, east_bound, west_bound, surface, frame, nu, weights, spread):
    tracers, levels, width = dims
    size = levels * width
    for k in range(2):
        frame[k * size:(k + 1) * size, :] = flow[k * size:(k + 1) * size, :].astype(f32) * 0.5
    for ref, edge, inner in ((east_bound, width - 1, width - 2), (west_bound, 0, 1)):
        for t in range(tracers):
            high, low = split(cells[pl.ds(t * size + edge, levels, stride=width), :])
            ref[t * levels:(t + 1) * levels, :] = high
            ref[(tracers + t) * levels:(tracers + t + 1) * levels, :] = low
            second = cells[pl.ds(t * size + inner, levels, stride=width), :].astype(bf16)
            ref[(2 * tracers + t) * levels:(2 * tracers + t + 1) * levels, :] = second
        for k in range(2):
            strip = frame[pl.ds(k * size + edge, levels, stride=width), :].astype(bf16)
            ref[(3 * tracers + k) * levels:(3 * tracers + k + 1) * levels, :] = strip
    level = surface_level(levels)
    for t in range(tracers):
        start = pl.multiple_of((t * levels + level) * width, 8)
        surface[t * width:(t + 1) * width, :] = cells[pl.ds(start, width), :]
        nu[t * levels:(t + 1) * levels, :] = jnp.transpose(jnp.broadcast_to(diffusion[t:t + 1, :], (128, levels)))
    high, low = split(solve[...])
    weights[...] = jnp.concatenate([high, high, low], axis=1)
    at_level = lax.broadcasted_iota(jnp.int32, (levels, levels), 1) == level
    spread[...] = jnp.broadcast_to(jnp.sum(jnp.where(at_level, solve[...], 0.0), axis=1, keepdims=True), (levels, 128))


def lanes_kernel(dims, cells, columns, *send_mer):
    tracers, levels, width = dims
    lane, even = lanes_of(levels), mer_even()
    acc = [jnp.zeros((levels, 128), f32) for _ in send_mer]
    for t in range(tracers):
        for x in range(width):
            j = t * width + x
            value = cells[pl.ds(t * levels * width + x, levels, stride=width), :]
            columns[j * levels:(j + 1) * levels, :] = value
            pack_lanes(acc, value, j, lane, even)
    for ref, value in zip(send_mer, acc):
        ref[...] = value


def inner_kernel(dims, columns, frame, nu, weights, partial, strips, mer_gain):
    tracers, levels, width = dims
    size = levels * width
    lane = lanes_of(levels)
    packed = jnp.zeros((levels, 128), f32)
    for k in range(2):
        for x in range(width):
            value = frame[pl.ds(k * size + x, levels, stride=width), :]
            strips[(k * width + x) * levels:(k * width + x + 1) * levels, :] = value
            if k == 1:
                packed = jnp.where(lane // 2 == x, both_edges(value, x), packed)
    gain = jnp.zeros((levels, 128), f32)
    for t in range(tracers):
        merid = packed if t == 0 else pltpu.roll(packed, 2 * t * width, 1)
        mine = part(nu, t, levels) + jnp.where(lane % 2 == 0, -merid, merid)
        gain = jnp.where(lane // (2 * width) == t, mine, gain)
    mer_gain[...] = gain

    def store(t, x, value):
        partial[pl.ds((t * width + x) * levels, levels), :] = value

    column = lambda t, x: part(columns, t * width + x, levels)
    strip = lambda k, x: part(strips, k * width + x, levels)
    interior(column, strip, nu, weights, store, dims)


def second_kernel(dims, columns, strips, nu, weights, partial):
    tracers, levels, width = dims

    def store(t, x, value):
        partial[pl.ds((t * width + x) * levels, levels), :] = value

    column = lambda t, x: part(columns, t * width + x, levels)
    strip = lambda k, x: part(strips, k * width + x, levels)
    interior(column, strip, nu, weights, store, dims)


def join_kernel(dims, mer_count, partial, strips, nu, weights, spread, mer_gain, rate, block_map, ice_mask, own, other, from_west, from_east, *rest):
    tracers, levels, width = dims
    rounds = 1 if mer_count == 2 else 2
    recv_mer = rest[:rounds]
    fresh, sides, surface = rest[rounds:rounds + 3]
    send_mer = rest[rounds + 3:]
    lane, even = lanes_of(levels), mer_even()
    incr = increments(own[...], other[...], rate, block_map, ice_mask, tracers, width)
    edges = []
    for s, ref in enumerate((from_west, from_east)):
        c = part(strips, 0 if s == 0 else width - 1, levels)
        for t in range(tracers):
            value = part(ref, t, levels).astype(f32) + part(ref, tracers + t, levels).astype(f32)
            sides[(2 * t + s) * levels:(2 * t + s + 1) * levels, :] = value
            edges.append((part(nu, t, levels) + (c if s == 0 else -c)) * value)
    solved = product(weights[...], jnp.concatenate(edges, axis=1))
    lanes = product(weights[...], mer_gain[...] * mer_halo(recv_mer, levels, mer_count))
    rim = jnp.logical_or(lane == 127, lane == 0)
    acc = [jnp.zeros((levels, 128), f32) for _ in send_mer]
    for t in range(tracers):
        for x in range(width):
            j = t * width + x
            value = part(partial, j, levels) + part(spread, 0, levels) * incr[j:j + 1, :]
            value = value + jnp.where(rim, at_edges(lanes, j), 0.0)
            if x in (0, width - 1):
                at = (0 if x == 0 else tracers) + t
                value = value + solved[:, at * 128:(at + 1) * 128]
            fresh[j * levels:(j + 1) * levels, :] = value
            pack_lanes(acc, value, j, lane, even)
        for s in range(2):
            pack_lanes(acc, part(sides, 2 * t + s, levels), tracers * width + 2 * t + s, lane, even)
    for ref, value in zip(send_mer, acc):
        ref[...] = value
    level = surface_level(levels)
    total = tracers * width
    surface[total:, :] = jnp.zeros((surface.shape[0] - total, 128), f32)
    for j in range(total):
        surface[j:j + 1, :] = fresh[pl.ds(j * levels + level, 1), :]
    for j in range(2 * tracers):
        surface[total + j:total + j + 1, :] = sides[pl.ds(j * levels + level, 1), :]


def sides_kernel(dims, columns, strips, nu, weights, sides, rate, block_map, ice_mask, own, other, from_west, from_east, edges, incr, inner_gain, outer_gain):
    tracers, levels, width = dims
    total = tracers * width
    lane = lanes_of(levels)
    incr[...] = increments(own[:total, :], other[:total, :], rate, block_map, ice_mask, tracers, width)
    extra = increments(own[total:, :], other[total:, :], rate, block_map, ice_mask, tracers, 2)
    at_level = lax.broadcasted_iota(jnp.int32, (levels, 128), 0) == surface_level(levels)
    terms, gains = [], []
    first = jnp.zeros((levels, 128), f32)
    later = jnp.zeros((levels, 128), f32)
    for s, ref in enumerate((from_west, from_east)):
        x = 0 if s == 0 else width - 1
        c, d = (part(ref, 3 * tracers + k, levels).astype(f32) for k in range(2))
        own_c = part(strips, x, levels)
        for t in range(tracers):
            mine, beyond = part(columns, t * width + x, levels), part(ref, 2 * tracers + t, levels).astype(f32)
            east, west = (mine, beyond) if s == 0 else (beyond, mine)
            value = horizontal(part(sides, 2 * t + s, levels), east, west, c, d, part(nu, t, levels), lane)
            value = value + jnp.where(at_level, jnp.broadcast_to(extra[2 * t + s:2 * t + s + 1, :], value.shape), 0.0)
            terms.append(value)
            gain = part(nu, t, levels) + (own_c if s == 0 else -own_c)
            gains.append(gain)
            j = t * width + x
            here = lane // 2 == j
            packed = both_edges(d, j)
            first = jnp.where(here, part(nu, t, levels) + jnp.where(lane % 2 == 0, -packed, packed), first)
            later = jnp.where(here, both_edges(gain, j), later)
    solved = product(weights[...], jnp.concatenate(terms, axis=1))
    solved = product(weights[...], solved * jnp.concatenate(gains, axis=1))
    for i in range(2 * tracers):
        edges[i * levels:(i + 1) * levels, :] = solved[:, i * 128:(i + 1) * 128]
    inner_gain[...] = first
    outer_gain[...] = later


def last_kernel(dims, mer_count, partial, edges, incr, weights, spread, mer_gain, inner_gain, outer_gain, *rest):
    tracers, levels, width = dims
    rounds = 1 if mer_count == 2 else 2
    recv_mer, (out, done, sems) = rest[:rounds], rest[rounds:]
    lane = lanes_of(levels)
    halo = mer_halo(recv_mer, levels, mer_count)
    corner = jnp.zeros((levels, 128), f32)
    for t in range(tracers):
        for s in range(2):
            j = t * width + (0 if s == 0 else width - 1)
            moved = pltpu.roll(halo, (2 * (j - tracers * width - 2 * t - s)) % 128, 1)
            corner = jnp.where(lane // 2 == j, moved, corner)
    corner = outer_gain[...] * product(weights[...], inner_gain[...] * corner)
    lanes = product(weights[...], mer_gain[...] * halo + corner)
    rim = jnp.logical_or(lane == 127, lane == 0)
    copies = []
    for t in range(tracers):
        for x in range(width):
            j = t * width + x
            value = part(partial, j, levels) + part(spread, 0, levels) * incr[j:j + 1, :]
            value = value + jnp.where(rim, at_edges(lanes, j), 0.0)
            if x in (0, width - 1):
                value = value + part(edges, (0 if x == 0 else tracers) + t, levels)
            done[j] = value
            copy = pltpu.make_async_copy(done.at[j], out.at[t, :, x, :], sems.at[j])
            copy.start()
            copies.append(copy)
    for copy in copies:
        copy.wait()


VM = pl.BlockSpec(memory_space=pltpu.VMEM)
SM = pl.BlockSpec(memory_space=pltpu.SMEM)


def call(body, name, in_specs, out_shape, flops, out_specs=None, scratch=()):
    many = isinstance(out_shape, list)
    return pl.pallas_call(
        body,
        out_shape=out_shape,
        in_specs=in_specs,
        out_specs=out_specs or ([VM] * len(out_shape) if many else VM),
        scratch_shapes=scratch,
        name=name,
        cost_estimate=pl.CostEstimate(flops=flops, bytes_accessed=2 << 20, transcendentals=0),
        compiler_params=pltpu.CompilerParams(vmem_limit_bytes=32 * 1024 * 1024),
    )


def on_device(state, flow, diffusion, column_solve, exchange_rate, block_map, ice_mask):
    _, tracers, levels, width, wide = state.shape
    mer_count, zon_count = lax.axis_size("mer"), lax.axis_size("zon")
    rounds = 1 if mer_count == 2 else 2
    dims = (tracers, levels, width)
    size, total = levels * width, tracers * width
    cells = state.reshape(tracers * size, wide)
    shape = lambda rows, dtype=f32: jax.ShapeDtypeStruct((rows, wide), dtype)
    small = (exchange_rate[0], block_map, ice_mask)
    small_specs = [SM] * 3
    message = shape((3 * tracers + 2) * levels, bf16)
    packed = shape(levels)

    def swap_mer(pieces):
        return [lax.ppermute(piece, "mer", pairs(mer_count, r == 1)) for r, piece in enumerate(pieces)]

    east_bound, west_bound, surface, frame, nu, weights, spread = call(
        functools.partial(pack_kernel, dims), "pack", [VM] * 4 + small_specs,
        [message, message, shape(total), shape(2 * size), shape(tracers * levels),
         jax.ShapeDtypeStruct((levels, 3 * levels), bf16), packed], 1 << 20,
    )(cells, flow.reshape(2 * size, wide), diffusion[0], column_solve[0], *small)
    from_west = lax.ppermute(east_bound, "zon", ring(zon_count, 1))
    columns, *send_mer = call(
        functools.partial(lanes_kernel, dims), "lanes", [VM], [shape(tracers * size)] + [packed] * rounds, 1 << 20,
    )(cells)
    recv_mer = swap_mer(send_mer)
    other = lax.ppermute(surface, "fluid", [(0, 1), (1, 0)])
    from_east = lax.ppermute(west_bound, "zon", ring(zon_count, -1))
    partial, strips, mer_gain = call(
        functools.partial(inner_kernel, dims), "inner", [VM] * 4,
        [shape(tracers * size), shape(2 * size), packed], 1 << 30,
    )(columns, frame, nu, weights)
    fresh, sides, fresh_surface, *send_mer = call(
        functools.partial(join_kernel, dims, mer_count), "join", [VM] * 6 + small_specs + [VM] * (4 + rounds),
        [shape(tracers * size), shape(2 * tracers * levels), shape(total + 8)] + [packed] * rounds, 1 << 26,
    )(partial, strips, nu, weights, spread, mer_gain, *small, surface, other, from_west, from_east, *recv_mer)
    recv_mer = swap_mer(send_mer)
    fresh_other = lax.ppermute(fresh_surface, "fluid", [(0, 1), (1, 0)])
    partial = call(
        functools.partial(second_kernel, dims), "second", [VM] * 4, shape(tracers * size), 1 << 30,
    )(fresh, strips, nu, weights)
    edges, incr, inner_gain, outer_gain = call(
        functools.partial(sides_kernel, dims), "sides", [VM] * 5 + small_specs + [VM] * 4,
        [shape(2 * tracers * levels), shape(total), packed, packed], 1 << 28,
    )(columns, strips, nu, weights, sides, *small, fresh_surface, fresh_other, from_west, from_east)
    done = call(
        functools.partial(last_kernel, dims, mer_count), "last", [VM] * (8 + rounds),
        jax.ShapeDtypeStruct(state.shape[1:], f32), 1 << 26,
        out_specs=pl.BlockSpec(memory_space=pl.ANY),
        scratch=[pltpu.VMEM((total, levels, wide), f32), pltpu.SemaphoreType.DMA((total,))],
    )(partial, edges, incr, weights, spread, mer_gain, inner_gain, outer_gain, *recv_mer)
    return done[None]


def solution(mesh):
    return jax.shard_map(
        on_device,
        mesh=mesh,
        in_specs=(
            P("fluid", None, None, "zon", "mer"),
            P("fluid", None, None, "zon", "mer"),
            P("fluid", None, None),
            P("fluid", None, None),
            P("fluid", None),
            P("mer"),
            P("mer"),
        ),
        out_specs=P("fluid", None, None, "zon", "mer"),
        check_vma=False,
    )
```

```python
import functools

import jax
import jax.numpy as jnp
from jax import lax
from jax.experimental import pallas as pl
from jax.experimental.pallas import tpu as pltpu
from jax.sharding import PartitionSpec as P

f32, bf16 = jnp.float32, jnp.bfloat16


def ring(count, ahead):
    return [(i, (i + ahead) % count) for i in range(count)]


def pairs(count, odd):
    if odd:
        return [(i, ((i + 1) ^ 1) - 1) for i in range(1, count - 1)] + [(0, count - 1), (count - 1, 0)]
    return [(i, i ^ 1) for i in range(count)]


def surface_level(levels):
    return jnp.where(lax.axis_index("fluid") == 0, levels - 1, 0)


def lanes_of(levels):
    return lax.broadcasted_iota(jnp.int32, (levels, 128), 1)


def split(value):
    high = value.astype(bf16)
    return high, (value - high.astype(f32)).astype(bf16)


def product(weights, value):
    high, low = split(value)
    return jnp.dot(weights, jnp.concatenate([high, low, high], axis=0), preferred_element_type=f32)


def part(ref, index, levels):
    return ref[index * levels:(index + 1) * levels, :]


def mer_halo(recv_mer, levels, mer_count):
    place = lax.axis_index("mer")
    even = 1 - lax.rem(place, 2)
    lane = lanes_of(levels)
    total = jnp.zeros((levels, 128), f32)
    for r, ref in enumerate(recv_mer):
        north = even if r == 0 else 1 - even
        inside = jnp.where(north == 1, place + 1 < mer_count, place > 0)
        keep = jnp.logical_and(lane % 2 == 1 - north, inside)
        moved = pltpu.roll(ref[...], jnp.where(north == 1, 127, 1), 1)
        total = total + jnp.where(keep, moved, 0.0)
    return total


def both_edges(cells, j):
    return pltpu.roll(cells, (2 * j + 1) % 128, 1)


def at_edges(packed, j):
    return pltpu.roll(packed, (127 - 2 * j) % 128, 1)


def increments(own, other, rate, block_map, ice_mask, tracers, per_tracer):
    blocks = block_map.shape[0]
    wide = own.shape[1] // blocks
    first = lax.axis_index("mer") * blocks
    is_atm = lax.axis_index("fluid") == 0
    atm = jnp.where(is_atm, own, other)
    ocean = jnp.where(is_atm, other, own)
    block = lax.broadcasted_iota(jnp.int32, own.shape, 1) // wide
    flux = jnp.zeros_like(own)
    for b in range(blocks):
        a = block_map[b] - first
        moved = pltpu.roll(atm, lax.rem((b - a + blocks) * wide, 128), 1)
        flux = jnp.where(block == b, (moved - ocean) * (1 - ice_mask[b]).astype(f32), flux)
    returned = jnp.zeros_like(own)
    for b in range(blocks):
        a = block_map[b] - first
        moved = pltpu.roll(flux, lax.rem((a - b + blocks) * wide, 128), 1)
        returned = jnp.where(block == a, moved, returned)
    tracer = lax.broadcasted_iota(jnp.int32, own.shape, 0) // per_tracer % tracers
    scale = jnp.full(own.shape, rate[0])
    for t in range(1, tracers):
        scale = jnp.where(tracer == t, rate[t], scale)
    return jnp.where(is_atm, -returned, flux) * scale


def horizontal(q, east, west, c, d, nu, lane):
    north = jnp.where(lane == 127, 0.0, pltpu.roll(q, 127, 1))
    south = jnp.where(lane == 0, 0.0, pltpu.roll(q, 1, 1))
    return q - c * (east - west) - d * (north - south) + nu * ((east + west) + (north + south) - 4.0 * q)


def interior(column, strip, nu, weights, store, dims):
    tracers, levels, width = dims
    lane = lanes_of(levels)
    zero = jnp.zeros((levels, 128), f32)
    for x in range(width):
        c, d = strip(0, x), strip(1, x)
        terms = []
        for t in range(tracers):
            west = zero if x == 0 else column(t, x - 1)
            east = zero if x == width - 1 else column(t, x + 1)
            terms.append(horizontal(column(t, x), east, west, c, d, part(nu, t, levels), lane))
        solved = product(weights[...], jnp.concatenate(terms, axis=1))
        for t in range(tracers):
            store(t, x, solved[:, t * 128:(t + 1) * 128])


def pack_kernel(dims, state, flow, east_bound, west_bound, surface, frame, columns, raw, sems):
    tracers, levels, width = dims
    size = levels * width
    level = surface_level(levels)
    places = ((east_bound, width - 1), (east_bound, width - 2), (west_bound, 0), (west_bound, 1))
    wait_columns, wait_flow, wait_rows = [], [], []
    for i, (_, x) in enumerate(places):
        for t in range(tracers):
            at = i * tracers + t
            wait_columns.append(pltpu.make_async_copy(state.at[t, :, x, :], columns.at[at], sems.at[at]))
    used = len(wait_columns)
    for k in range(2):
        wait_flow.append(pltpu.make_async_copy(flow.at[k], raw.at[k], sems.at[used + k]))
    for t in range(tracers):
        target = surface.at[pl.ds(t * width, width), :]
        wait_rows.append(pltpu.make_async_copy(state.at[t, level], target, sems.at[used + 2 + t]))
    for copy in wait_columns + wait_flow + wait_rows:
        copy.start()
    for copy in wait_columns:
        copy.wait()
    for i, (ref, _) in enumerate(places):
        for t in range(tracers):
            high, low = split(columns[i * tracers + t])
            if i % 2 == 0:
                ref[t * levels:(t + 1) * levels, :] = high
                ref[(tracers + t) * levels:(tracers + t + 1) * levels, :] = low
            else:
                ref[(2 * tracers + t) * levels:(2 * tracers + t + 1) * levels, :] = high
    for k, copy in enumerate(wait_flow):
        copy.wait()
        frame[k * size:(k + 1) * size, :] = raw[k].reshape(size, 128).astype(f32) * 0.5
        for ref, x in ((east_bound, width - 1), (west_bound, 0)):
            strip = frame[pl.ds(k * size + x, levels, stride=width), :].astype(bf16)
            ref[(3 * tracers + k) * levels:(3 * tracers + k + 1) * levels, :] = strip
    for copy in wait_rows:
        copy.wait()


def lanes_kernel(dims, cells, diffusion, solve, rate, block_map, ice_mask, columns, send_mer, nu, weights, spread):
    tracers, levels, width = dims
    lane = lanes_of(levels)
    packed = jnp.zeros((levels, 128), f32)
    for t in range(tracers):
        for x in range(width):
            j = t * width + x
            value = cells[pl.ds(t * levels * width + x, levels, stride=width), :]
            columns[j * levels:(j + 1) * levels, :] = value
            packed = jnp.where(lane // 2 == j, both_edges(value, j), packed)
        nu[t * levels:(t + 1) * levels, :] = jnp.transpose(jnp.broadcast_to(diffusion[t:t + 1, :], (128, levels)))
    send_mer[...] = packed
    high, low = split(solve[...])
    weights[...] = jnp.concatenate([high, high, low], axis=1)
    at_level = lax.broadcasted_iota(jnp.int32, (levels, levels), 1) == surface_level(levels)
    spread[...] = jnp.broadcast_to(jnp.sum(jnp.where(at_level, solve[...], 0.0), axis=1, keepdims=True), (levels, 128))


def inner_kernel(dims, columns, frame, nu, weights, partial, strips, mer_gain, edge_lanes, rows):
    tracers, levels, width = dims
    size = levels * width
    lane = lanes_of(levels)
    packed = jnp.zeros((levels, 128), f32)
    for k in range(2):
        for x in range(width):
            value = frame[pl.ds(k * size + x, levels, stride=width), :]
            strips[(k * width + x) * levels:(k * width + x + 1) * levels, :] = value
            if k == 1:
                packed = jnp.where(lane // 2 == x, both_edges(value, x), packed)
    gain = jnp.zeros((levels, 128), f32)
    for t in range(tracers):
        merid = packed if t == 0 else pltpu.roll(packed, 2 * t * width, 1)
        mine = part(nu, t, levels) + jnp.where(lane % 2 == 0, -merid, merid)
        gain = jnp.where(lane // (2 * width) == t, mine, gain)
    mer_gain[...] = gain
    found = [jnp.zeros((levels, 128), f32)]

    def store(t, x, value):
        j = t * width + x
        partial[j * levels:(j + 1) * levels, :] = value
        found[0] = jnp.where(lane // 2 == j, both_edges(value, j), found[0])

    column = lambda t, x: part(columns, t * width + x, levels)
    strip = lambda k, x: part(strips, k * width + x, levels)
    interior(column, strip, nu, weights, store, dims)
    edge_lanes[...] = found[0]
    level = surface_level(levels)
    for j in range(tracers * width):
        rows[j:j + 1, :] = partial[pl.ds(j * levels + level, 1), :]


def side_terms(ref, s, strips, nu, sides, dims):
    tracers, levels, width = dims
    c = part(strips, 0 if s == 0 else width - 1, levels)
    terms = []
    for t in range(tracers):
        value = part(ref, t, levels).astype(f32) + part(ref, tracers + t, levels).astype(f32)
        sides[t * levels:(t + 1) * levels, :] = value
        terms.append((part(nu, t, levels) + (c if s == 0 else -c)) * value)
    return terms


def side_lanes(packed, s, sides, solved, lane, dims):
    tracers, levels, width = dims
    for t in range(tracers):
        j = t * width + (0 if s == 0 else width - 1)
        packed = packed + jnp.where(lane // 2 == j, both_edges(part(solved, t, levels), j), 0.0)
        j = tracers * width + s * tracers + t
        packed = jnp.where(lane // 2 == j, both_edges(part(sides, t, levels), j), packed)
    return packed


def side_rows(fresh, surface, s, sides, solved, row, level, dims):
    tracers, levels, width = dims
    total = tracers * width
    for t in range(tracers):
        line = solved[pl.ds(t * levels + level, 1), :]
        fresh = fresh + jnp.where(row == t * width + (0 if s == 0 else width - 1), line, 0.0)
        at = total + s * tracers + t
        surface[at:at + 1, :] = sides[pl.ds(t * levels + level, 1), :]
    return fresh


def west_kernel(dims, mer_count, strips, nu, weights, spread, mer_gain, edge_lanes, rows, rate, block_map, ice_mask, own, other, from_west, *rest):
    tracers, levels, width = dims
    total = tracers * width
    rounds = len(rest) - 6
    recv_mer, (sides, solved, lanes, incr, half_lanes, surface) = rest[:rounds], rest[rounds:]
    lane = lanes_of(levels)
    terms = side_terms(from_west, 0, strips, nu, sides, dims)
    terms.append(mer_gain[...] * mer_halo(recv_mer, levels, mer_count))
    result = product(weights[...], jnp.concatenate(terms, axis=1))
    flux = increments(own[...], other[...], rate, block_map, ice_mask, tracers, width)
    incr[...] = flux
    for t in range(tracers):
        solved[t * levels:(t + 1) * levels, :] = result[:, t * 128:(t + 1) * 128]
    lanes[...] = result[:, tracers * 128:]
    row = lax.broadcasted_iota(jnp.int32, (total, 128), 0)
    rows_lane = lax.broadcasted_iota(jnp.int32, (total, 128), 1)
    turned = pltpu.roll(flux, 1, 1, stride=2, stride_axis=0)
    turned = jnp.sum(jnp.where(rows_lane // 2 == row, turned, 0.0), axis=0, keepdims=True)
    packed = edge_lanes[...] + lanes[...] + spread[...] * turned
    half_lanes[...] = side_lanes(packed, 0, sides, solved, lane, dims)
    level = surface_level(levels)
    fresh = rows[...] + spread[pl.ds(level, 1), :] * flux
    line = jnp.broadcast_to(lanes[pl.ds(level, 1), :], (total, 128))
    line = jnp.take_along_axis(line, 2 * row + (rows_lane == 0).astype(jnp.int32), axis=1)
    fresh = fresh + jnp.where(jnp.logical_or(rows_lane == 127, rows_lane == 0), line, 0.0)
    surface[total:, :] = jnp.zeros((surface.shape[0] - total, 128), f32)
    surface[:total, :] = side_rows(fresh, surface, 0, sides, solved, row, level, dims)


def east_kernel(dims, strips, nu, weights, half_lanes, half_surface, from_east, sides, solved, surface, send_mer):
    tracers, levels, width = dims
    total = tracers * width
    lane = lanes_of(levels)
    terms = side_terms(from_east, 1, strips, nu, sides, dims)
    result = product(weights[...], jnp.concatenate(terms, axis=1))
    for t in range(tracers):
        solved[t * levels:(t + 1) * levels, :] = result[:, t * 128:(t + 1) * 128]
    send_mer[...] = side_lanes(half_lanes[...], 1, sides, solved, lane, dims)
    surface[...] = half_surface[...]
    row = lax.broadcasted_iota(jnp.int32, (total, 128), 0)
    surface[:total, :] = side_rows(half_surface[:total, :], surface, 1, sides, solved, row, surface_level(levels), dims)


def middle_kernel(dims, partial, strips, nu, weights, spread, west_sides, east_sides, west_solved, east_solved, lanes, incr, columns, rate, block_map, ice_mask, own, other, from_west, from_east, again, edges, flux, inner_gain, outer_gain, fresh):
    tracers, levels, width = dims
    total = tracers * width
    lane = lanes_of(levels)
    flux[...] = increments(own[:total, :], other[:total, :], rate, block_map, ice_mask, tracers, width)
    extra = increments(own[total:, :], other[total:, :], rate, block_map, ice_mask, tracers, 1)
    at_level = lax.broadcasted_iota(jnp.int32, (levels, 128), 0) == surface_level(levels)
    terms, gains = [], []
    first = jnp.zeros((levels, 128), f32)
    later = jnp.zeros((levels, 128), f32)
    for s, (ref, sides) in enumerate(((from_west, west_sides), (from_east, east_sides))):
        x = 0 if s == 0 else width - 1
        c, d = (part(ref, 3 * tracers + k, levels).astype(f32) for k in range(2))
        own_c = part(strips, x, levels)
        for t in range(tracers):
            mine, beyond = part(columns, t * width + x, levels), part(ref, 2 * tracers + t, levels).astype(f32)
            east, west = (mine, beyond) if s == 0 else (beyond, mine)
            value = horizontal(part(sides, t, levels), east, west, c, d, part(nu, t, levels), lane)
            value = value + jnp.where(at_level, jnp.broadcast_to(extra[s * tracers + t:s * tracers + t + 1, :], value.shape), 0.0)
            terms.append(value)
            gain = part(nu, t, levels) + (own_c if s == 0 else -own_c)
            gains.append(gain)
            j = t * width + x
            here = lane // 2 == j
            packed = both_edges(d, j)
            first = jnp.where(here, part(nu, t, levels) + jnp.where(lane % 2 == 0, -packed, packed), first)
            later = jnp.where(here, both_edges(gain, j), later)
    inner_gain[...] = first
    outer_gain[...] = later
    result = product(weights[...], jnp.concatenate(terms, axis=1))
    result = product(weights[...], result * jnp.concatenate(gains, axis=1))
    for i in range(2 * tracers):
        edges[i * levels:(i + 1) * levels, :] = result[:, i * 128:(i + 1) * 128]
    rim = jnp.logical_or(lane == 127, lane == 0)
    for t in range(tracers):
        for x in range(width):
            j = t * width + x
            value = part(partial, j, levels) + spread[...] * incr[j:j + 1, :]
            value = value + jnp.where(rim, at_edges(lanes[...], j), 0.0)
            if x in (0, width - 1):
                value = value + part(west_solved if x == 0 else east_solved, t, levels)
            fresh[j * levels:(j + 1) * levels, :] = value

    def store(t, x, value):
        again[pl.ds((t * width + x) * levels, levels), :] = value

    column = lambda t, x: part(fresh, t * width + x, levels)
    strip = lambda k, x: part(strips, k * width + x, levels)
    interior(column, strip, nu, weights, store, dims)


def last_kernel(dims, mer_count, partial, edges, incr, weights, spread, mer_gain, inner_gain, outer_gain, *rest):
    tracers, levels, width = dims
    rounds = len(rest) - 3
    recv_mer, (out, done, sems) = rest[:rounds], rest[rounds:]
    lane = lanes_of(levels)
    halo = mer_halo(recv_mer, levels, mer_count)
    lanes = product(weights[...], mer_gain[...] * halo)
    corner = jnp.zeros((levels, 128), f32)
    for t in range(tracers):
        for s in range(2):
            j = t * width + (0 if s == 0 else width - 1)
            moved = pltpu.roll(halo, (2 * (j - tracers * width - s * tracers - t)) % 128, 1)
            corner = jnp.where(lane // 2 == j, moved, corner)
    corner = outer_gain[...] * product(weights[...], inner_gain[...] * corner)
    corner = product(weights[...], corner) + lanes
    rim = jnp.logical_or(lane == 127, lane == 0)
    copies = []
    for x in list(range(1, width - 1)) + [0, width - 1]:
        for t in range(tracers):
            j = t * width + x
            value = part(partial, j, levels) + spread[...] * incr[j:j + 1, :]
            value = value + jnp.where(rim, at_edges(corner if x in (0, width - 1) else lanes, j), 0.0)
            if x in (0, width - 1):
                value = value + part(edges, (0 if x == 0 else tracers) + t, levels)
            done[j] = value
            copy = pltpu.make_async_copy(done.at[j], out.at[t, :, x, :], sems.at[j])
            copy.start()
            copies.append(copy)
    for copy in copies:
        copy.wait()


VM = pl.BlockSpec(memory_space=pltpu.VMEM)
SM = pl.BlockSpec(memory_space=pltpu.SMEM)
HB = pl.BlockSpec(memory_space=pltpu.HBM)


def call(body, name, in_specs, out_shape, flops, out_specs=None, scratch=()):
    many = isinstance(out_shape, list)
    return pl.pallas_call(
        body,
        out_shape=out_shape,
        in_specs=in_specs,
        out_specs=out_specs or ([VM] * len(out_shape) if many else VM),
        scratch_shapes=scratch,
        name=name,
        cost_estimate=pl.CostEstimate(flops=flops, bytes_accessed=2 << 20, transcendentals=0),
        compiler_params=pltpu.CompilerParams(vmem_limit_bytes=32 * 1024 * 1024),
    )


def on_device(state, flow, diffusion, column_solve, exchange_rate, block_map, ice_mask):
    _, tracers, levels, width, wide = state.shape
    mer_count, zon_count = lax.axis_size("mer"), lax.axis_size("zon")
    rounds = 1 if mer_count == 2 else 2
    dims = (tracers, levels, width)
    size, total = levels * width, tracers * width
    shape = lambda rows, dtype=f32: jax.ShapeDtypeStruct((rows, wide), dtype)
    small = (exchange_rate[0], block_map, ice_mask)
    small_specs = [SM] * 3
    message = shape((3 * tracers + 2) * levels, bf16)
    packed = shape(levels)
    kept = shape(tracers * size)
    halved = shape(tracers * levels)
    sided = shape(2 * tracers * levels)

    def swap_mer(piece):
        return [lax.ppermute(piece, "mer", pairs(mer_count, r == 1)) for r in range(rounds)]

    def swap_fluid(piece):
        return lax.ppermute(piece, "fluid", [(0, 1), (1, 0)])

    east_bound, west_bound, surface, frame = call(
        functools.partial(pack_kernel, dims), "pack", [HB] * 2, [message, message, shape(total), shape(2 * size)], 1 << 20,
        scratch=[pltpu.VMEM((4 * tracers, levels, wide), f32), pltpu.VMEM((2, levels, width, wide), bf16),
                 pltpu.SemaphoreType.DMA((5 * tracers + 2,))],
    )(pltpu.with_memory_space_constraint(state[0], pltpu.HBM), pltpu.with_memory_space_constraint(flow[0], pltpu.HBM))
    from_west = lax.ppermute(east_bound, "zon", ring(zon_count, 1))
    columns, send_mer, nu, weights, spread = call(
        functools.partial(lanes_kernel, dims), "lanes", [VM] * 3 + small_specs,
        [kept, packed, shape(tracers * levels), jax.ShapeDtypeStruct((levels, 3 * levels), bf16), packed], 1 << 20,
    )(state.reshape(tracers * size, wide), diffusion[0], column_solve[0], *small)
    west_bound, send_mer, surface = lax.optimization_barrier((west_bound, send_mer, surface))
    recv_mer = swap_mer(send_mer)
    other = swap_fluid(surface)
    from_east = lax.ppermute(west_bound, "zon", ring(zon_count, -1))
    partial, strips, mer_gain, edge_lanes, rows = call(
        functools.partial(inner_kernel, dims), "inner", [VM] * 4, [kept, shape(2 * size), packed, packed, shape(total)], 1 << 30,
    )(columns, frame, nu, weights)
    west_sides, west_solved, lanes, incr, half_lanes, half_surface = call(
        functools.partial(west_kernel, dims, mer_count), "west", [VM] * 7 + small_specs + [VM] * (3 + rounds),
        [halved, halved, packed, shape(total), packed, shape(total + 8)], 1 << 33,
    )(strips, nu, weights, spread, mer_gain, edge_lanes, rows, *small, surface, other, from_west, *recv_mer)
    east_sides, east_solved, fresh_surface, send_mer = call(
        functools.partial(east_kernel, dims), "east", [VM] * 6, [halved, halved, shape(total + 8), packed], 1 << 26,
    )(strips, nu, weights, half_lanes, half_surface, from_east)
    recv_mer = swap_mer(send_mer)
    fresh_other = swap_fluid(fresh_surface)
    again, edges, flux, inner_gain, outer_gain = call(
        functools.partial(middle_kernel, dims), "middle", [VM] * 12 + small_specs + [VM] * 4,
        [kept, sided, shape(total), packed, packed], 1 << 30, scratch=[pltpu.VMEM((tracers * size, wide), f32)],
    )(partial, strips, nu, weights, spread, west_sides, east_sides, west_solved, east_solved, lanes, incr, columns, *small, fresh_surface, fresh_other, from_west, from_east)
    done = call(
        functools.partial(last_kernel, dims, mer_count), "last", [VM] * (8 + rounds),
        jax.ShapeDtypeStruct(state.shape[1:], f32), 1 << 26,
        out_specs=pl.BlockSpec(memory_space=pl.ANY),
        scratch=[pltpu.VMEM((total, levels, wide), f32), pltpu.SemaphoreType.DMA((total,))],
    )(again, edges, flux, weights, spread, mer_gain, inner_gain, outer_gain, *recv_mer)
    return done[None]


def solution(mesh):
    return jax.shard_map(
        on_device,
        mesh=mesh,
        in_specs=(
            P("fluid", None, None, "zon", "mer"),
            P("fluid", None, None, "zon", "mer"),
            P("fluid", None, None),
            P("fluid", None, None),
            P("fluid", None),
            P("mer"),
            P("mer"),
        ),
        out_specs=P("fluid", None, None, "zon", "mer"),
        check_vma=False,
    )
```

```python
import functools

import jax
import jax.numpy as jnp
from jax import lax
from jax.experimental import pallas as pl
from jax.experimental.pallas import tpu as pltpu
from jax.sharding import PartitionSpec as P

f32, bf16 = jnp.float32, jnp.bfloat16


def ring(count, ahead):
    return [(i, (i + ahead) % count) for i in range(count)]


def pairs(count, odd):
    if odd:
        return [(i, ((i + 1) ^ 1) - 1) for i in range(1, count - 1)] + [(0, count - 1), (count - 1, 0)]
    return [(i, i ^ 1) for i in range(count)]


def surface_level(levels):
    return jnp.where(lax.axis_index("fluid") == 0, levels - 1, 0)


def lanes_of(levels):
    return lax.broadcasted_iota(jnp.int32, (levels, 128), 1)


def split(value):
    high = value.astype(bf16)
    return high, (value - high.astype(f32)).astype(bf16)


def product(weights, value):
    high, low = split(value)
    return jnp.dot(weights, jnp.concatenate([high, low, high], axis=0), preferred_element_type=f32)


def part(ref, index, levels):
    return ref[index * levels:(index + 1) * levels, :]


def mer_halo(recv_mer, levels, mer_count):
    place = lax.axis_index("mer")
    even = 1 - lax.rem(place, 2)
    lane = lanes_of(levels)
    total = jnp.zeros((levels, 128), f32)
    for r, ref in enumerate(recv_mer):
        north = even if r == 0 else 1 - even
        inside = jnp.where(north == 1, place + 1 < mer_count, place > 0)
        keep = jnp.logical_and(lane % 2 == 1 - north, inside)
        moved = pltpu.roll(ref[...], jnp.where(north == 1, 127, 1), 1)
        total = total + jnp.where(keep, moved, 0.0)
    return total


def both_edges(cells, j):
    return pltpu.roll(cells, (2 * j + 1) % 128, 1)


def at_edges(packed, j):
    return pltpu.roll(packed, (127 - 2 * j) % 128, 1)


def increments(own, other, guide, tracers, per_tracer):
    is_atm = lax.axis_index("fluid") == 0
    pick = lambda row: jnp.broadcast_to(guide[row:row + 1, :].astype(jnp.int32), own.shape)
    atm = jnp.where(is_atm, own, other)
    ocean = jnp.where(is_atm, other, own)
    flux = (jnp.take_along_axis(atm, pick(0), axis=1) - ocean) * guide[2:3, :]
    returned = jnp.take_along_axis(flux, pick(1), axis=1)
    tracer = lax.broadcasted_iota(jnp.int32, own.shape, 0) // per_tracer % tracers
    scale = jnp.broadcast_to(guide[3:4, :], own.shape)
    for t in range(1, tracers):
        scale = jnp.where(tracer == t, guide[3 + t:4 + t, :], scale)
    return jnp.where(is_atm, -returned, flux) * scale


def fill_guide(guide, rate, block_map, ice_mask, tracers):
    blocks = block_map.shape[1]
    lane = lax.broadcasted_iota(jnp.int32, (1, 128), 1)
    wide = 128 // blocks
    block, within = lane // wide, lane % wide
    first = lax.axis_index("mer") * blocks
    mapped = jnp.zeros((1, 128), jnp.int32)
    returned = jnp.zeros((1, 128), jnp.int32)
    is_open = jnp.zeros((1, 128), jnp.int32)
    for b in range(blocks):
        above = block_map[:, b:b + 1] - first
        mapped = jnp.where(block == b, above, mapped)
        returned = jnp.where(block == above, b, returned)
        is_open = jnp.where(block == b, 1 - ice_mask[:, b:b + 1], is_open)
    guide[...] = jnp.zeros(guide.shape, f32)
    guide[0:1, :] = (mapped * wide + within).astype(f32)
    guide[1:2, :] = (returned * wide + within).astype(f32)
    guide[2:3, :] = is_open.astype(f32)
    for t in range(tracers):
        guide[3 + t:4 + t, :] = jnp.broadcast_to(rate[:, t:t + 1], (1, 128))


def horizontal(q, east, west, c, d, nu, lane):
    north = jnp.where(lane == 127, 0.0, pltpu.roll(q, 127, 1))
    south = jnp.where(lane == 0, 0.0, pltpu.roll(q, 1, 1))
    return q - c * (east - west) - d * (north - south) + nu * ((east + west) + (north + south) - 4.0 * q)


def interior(column, strip, nu, weights, store, dims):
    tracers, levels, width = dims
    lane = lanes_of(levels)
    zero = jnp.zeros((levels, 128), f32)
    for x in range(width):
        c, d = strip(0, x), strip(1, x)
        terms = []
        for t in range(tracers):
            west = zero if x == 0 else column(t, x - 1)
            east = zero if x == width - 1 else column(t, x + 1)
            terms.append(horizontal(column(t, x), east, west, c, d, part(nu, t, levels), lane))
        solved = product(weights[...], jnp.concatenate(terms, axis=1))
        for t in range(tracers):
            store(t, x, solved[:, t * 128:(t + 1) * 128])


def pack_kernel(dims, state, flow, *rest):
    tracers, levels, width = dims
    size = levels * width
    fixed = len(rest) - 7 >> 1
    east_bound, west_bound, surface, frame = rest[fixed:fixed + 4]
    columns, raw, sems = rest[2 * fixed + 4:]
    level = surface_level(levels)
    places = ((east_bound, width - 1), (east_bound, width - 2), (west_bound, 0), (west_bound, 1))
    wait_columns, wait_flow, wait_rows = [], [], []
    for i, (_, x) in enumerate(places):
        for t in range(tracers):
            at = i * tracers + t
            wait_columns.append(pltpu.make_async_copy(state.at[t, :, x, :], columns.at[at], sems.at[at]))
    used = len(wait_columns)
    for k in range(2):
        wait_flow.append(pltpu.make_async_copy(flow.at[k], raw.at[k], sems.at[used + k]))
    for t in range(tracers):
        target = surface.at[pl.ds(t * width, width), :]
        wait_rows.append(pltpu.make_async_copy(state.at[t, level], target, sems.at[used + 2 + t]))
    for i in range(fixed):
        wait_rows.append(pltpu.make_async_copy(rest[i], rest[fixed + 4 + i], sems.at[used + 2 + tracers + i]))
    for copy in wait_columns + wait_flow + wait_rows:
        copy.start()
    for copy in wait_columns:
        copy.wait()
    for i, (ref, _) in enumerate(places):
        for t in range(tracers):
            high, low = split(columns[i * tracers + t])
            if i % 2 == 0:
                ref[t * levels:(t + 1) * levels, :] = high
                ref[(tracers + t) * levels:(tracers + t + 1) * levels, :] = low
            else:
                ref[(2 * tracers + t) * levels:(2 * tracers + t + 1) * levels, :] = high
    for k, copy in enumerate(wait_flow):
        copy.wait()
        frame[k * size:(k + 1) * size, :] = raw[k].reshape(size, 128).astype(f32) * 0.5
        for ref, x in ((east_bound, width - 1), (west_bound, 0)):
            strip = frame[pl.ds(k * size + x, levels, stride=width), :].astype(bf16)
            ref[(3 * tracers + k) * levels:(3 * tracers + k + 1) * levels, :] = strip
    for copy in wait_rows:
        copy.wait()


def lanes_kernel(dims, cells, diffusion, solve, rate, block_map, ice_mask, columns, send_mer, nu, weights, spread, guide):
    tracers, levels, width = dims
    lane = lanes_of(levels)
    packed = jnp.zeros((levels, 128), f32)
    for t in range(tracers):
        for x in range(width):
            j = t * width + x
            value = cells[pl.ds(t * levels * width + x, levels, stride=width), :]
            columns[j * levels:(j + 1) * levels, :] = value
            packed = jnp.where(lane // 2 == j, both_edges(value, j), packed)
        nu[t * levels:(t + 1) * levels, :] = jnp.transpose(jnp.broadcast_to(diffusion[t:t + 1, :], (128, levels)))
    send_mer[...] = packed
    high, low = split(solve[...])
    weights[...] = jnp.concatenate([high, high, low], axis=1)
    at_level = lax.broadcasted_iota(jnp.int32, (levels, levels), 1) == surface_level(levels)
    fill_guide(guide, rate, block_map, ice_mask, tracers)
    spread[...] = jnp.broadcast_to(jnp.sum(jnp.where(at_level, solve[...], 0.0), axis=1, keepdims=True), (levels, 128))


def inner_kernel(dims, columns, frame, nu, weights, partial, strips, mer_gain, edge_lanes, rows):
    tracers, levels, width = dims
    size = levels * width
    lane = lanes_of(levels)
    packed = jnp.zeros((levels, 128), f32)
    for k in range(2):
        for x in range(width):
            value = frame[pl.ds(k * size + x, levels, stride=width), :]
            strips[(k * width + x) * levels:(k * width + x + 1) * levels, :] = value
            if k == 1:
                packed = jnp.where(lane // 2 == x, both_edges(value, x), packed)
    gain = jnp.zeros((levels, 128), f32)
    for t in range(tracers):
        merid = packed if t == 0 else pltpu.roll(packed, 2 * t * width, 1)
        mine = part(nu, t, levels) + jnp.where(lane % 2 == 0, -merid, merid)
        gain = jnp.where(lane // (2 * width) == t, mine, gain)
    mer_gain[...] = gain

    def store(t, x, value):
        j = t * width + x
        partial[j * levels:(j + 1) * levels, :] = value

    column = lambda t, x: part(columns, t * width + x, levels)
    strip = lambda k, x: part(strips, k * width + x, levels)
    interior(column, strip, nu, weights, store, dims)
    level = surface_level(levels)
    packed = jnp.zeros((levels, 128), f32)
    for j in range(tracers * width):
        packed = jnp.where(lane // 2 == j, both_edges(part(partial, j, levels), j), packed)
    edge_lanes[...] = packed
    for j in range(tracers * width):
        rows[j:j + 1, :] = partial[pl.ds(j * levels + level, 1), :]


def side_terms(ref, s, strips, nu, sides, dims):
    tracers, levels, width = dims
    c = part(strips, 0 if s == 0 else width - 1, levels)
    terms = []
    for t in range(tracers):
        value = part(ref, t, levels).astype(f32) + part(ref, tracers + t, levels).astype(f32)
        sides[t * levels:(t + 1) * levels, :] = value
        terms.append((part(nu, t, levels) + (c if s == 0 else -c)) * value)
    return terms


def side_lanes(packed, s, sides, solved, lane, dims):
    tracers, levels, width = dims
    for t in range(tracers):
        j = t * width + (0 if s == 0 else width - 1)
        packed = packed + jnp.where(lane // 2 == j, both_edges(part(solved, t, levels), j), 0.0)
        j = tracers * width + s * tracers + t
        packed = jnp.where(lane // 2 == j, both_edges(part(sides, t, levels), j), packed)
    return packed


def side_rows(fresh, surface, s, sides, solved, row, level, dims):
    tracers, levels, width = dims
    total = tracers * width
    for t in range(tracers):
        line = solved[pl.ds(t * levels + level, 1), :]
        fresh = fresh + jnp.where(row == t * width + (0 if s == 0 else width - 1), line, 0.0)
        at = total + s * tracers + t
        surface[at:at + 1, :] = sides[pl.ds(t * levels + level, 1), :]
    return fresh


def west_kernel(dims, mer_count, strips, nu, weights, spread, mer_gain, edge_lanes, rows, guide, own, other, from_west, *rest):
    tracers, levels, width = dims
    total = tracers * width
    rounds = len(rest) - 6
    recv_mer, (sides, solved, lanes, incr, half_lanes, surface) = rest[:rounds], rest[rounds:]
    lane = lanes_of(levels)
    terms = side_terms(from_west, 0, strips, nu, sides, dims)
    terms.append(mer_gain[...] * mer_halo(recv_mer, levels, mer_count))
    result = product(weights[...], jnp.concatenate(terms, axis=1))
    flux = increments(own[...], other[...], guide, tracers, width)
    incr[...] = flux
    for t in range(tracers):
        solved[t * levels:(t + 1) * levels, :] = result[:, t * 128:(t + 1) * 128]
    lanes[...] = result[:, tracers * 128:]
    row = lax.broadcasted_iota(jnp.int32, (total, 128), 0)
    rows_lane = lax.broadcasted_iota(jnp.int32, (total, 128), 1)
    turned = pltpu.roll(flux, 1, 1, stride=2, stride_axis=0)
    turned = jnp.sum(jnp.where(rows_lane // 2 == row, turned, 0.0), axis=0, keepdims=True)
    packed = edge_lanes[...] + lanes[...] + spread[...] * turned
    half_lanes[...] = side_lanes(packed, 0, sides, solved, lane, dims)
    level = surface_level(levels)
    fresh = rows[...] + spread[pl.ds(level, 1), :] * flux
    line = jnp.broadcast_to(lanes[pl.ds(level, 1), :], (total, 128))
    line = jnp.take_along_axis(line, 2 * row + (rows_lane == 0).astype(jnp.int32), axis=1)
    fresh = fresh + jnp.where(jnp.logical_or(rows_lane == 127, rows_lane == 0), line, 0.0)
    surface[total:, :] = jnp.zeros((surface.shape[0] - total, 128), f32)
    surface[:total, :] = side_rows(fresh, surface, 0, sides, solved, row, level, dims)


def east_kernel(dims, strips, nu, weights, half_lanes, half_surface, from_east, sides, solved, surface, send_mer):
    tracers, levels, width = dims
    total = tracers * width
    lane = lanes_of(levels)
    terms = side_terms(from_east, 1, strips, nu, sides, dims)
    result = product(weights[...], jnp.concatenate(terms, axis=1))
    for t in range(tracers):
        solved[t * levels:(t + 1) * levels, :] = result[:, t * 128:(t + 1) * 128]
    send_mer[...] = side_lanes(half_lanes[...], 1, sides, solved, lane, dims)
    surface[...] = half_surface[...]
    row = lax.broadcasted_iota(jnp.int32, (total, 128), 0)
    surface[:total, :] = side_rows(half_surface[:total, :], surface, 1, sides, solved, row, surface_level(levels), dims)


def middle_kernel(dims, partial, strips, nu, weights, spread, west_sides, east_sides, west_solved, east_solved, lanes, incr, columns, guide, own, other, from_west, from_east, again, edges, flux, inner_gain, outer_gain, fresh):
    tracers, levels, width = dims
    total = tracers * width
    lane = lanes_of(levels)
    flux[...] = increments(own[:total, :], other[:total, :], guide, tracers, width)
    extra = increments(own[total:, :], other[total:, :], guide, tracers, 1)
    at_level = lax.broadcasted_iota(jnp.int32, (levels, 128), 0) == surface_level(levels)
    terms, gains = [], []
    first = jnp.zeros((levels, 128), f32)
    later = jnp.zeros((levels, 128), f32)
    for s, (ref, sides) in enumerate(((from_west, west_sides), (from_east, east_sides))):
        x = 0 if s == 0 else width - 1
        c, d = (part(ref, 3 * tracers + k, levels).astype(f32) for k in range(2))
        own_c = part(strips, x, levels)
        for t in range(tracers):
            mine, beyond = part(columns, t * width + x, levels), part(ref, 2 * tracers + t, levels).astype(f32)
            east, west = (mine, beyond) if s == 0 else (beyond, mine)
            value = horizontal(part(sides, t, levels), east, west, c, d, part(nu, t, levels), lane)
            value = value + jnp.where(at_level, jnp.broadcast_to(extra[s * tracers + t:s * tracers + t + 1, :], value.shape), 0.0)
            terms.append(value)
            gain = part(nu, t, levels) + (own_c if s == 0 else -own_c)
            gains.append(gain)
            j = t * width + x
            here = lane // 2 == j
            packed = both_edges(d, j)
            first = jnp.where(here, part(nu, t, levels) + jnp.where(lane % 2 == 0, -packed, packed), first)
            later = jnp.where(here, both_edges(gain, j), later)
    inner_gain[...] = first
    outer_gain[...] = later
    result = product(weights[...], jnp.concatenate(terms, axis=1))
    result = product(weights[...], result * jnp.concatenate(gains, axis=1))
    for i in range(2 * tracers):
        edges[i * levels:(i + 1) * levels, :] = result[:, i * 128:(i + 1) * 128]
    rim = jnp.logical_or(lane == 127, lane == 0)
    for t in range(tracers):
        for x in range(width):
            j = t * width + x
            value = part(partial, j, levels) + spread[...] * incr[j:j + 1, :]
            value = value + jnp.where(rim, at_edges(lanes[...], j), 0.0)
            if x in (0, width - 1):
                value = value + part(west_solved if x == 0 else east_solved, t, levels)
            fresh[j * levels:(j + 1) * levels, :] = value

    def store(t, x, value):
        again[pl.ds((t * width + x) * levels, levels), :] = value

    column = lambda t, x: part(fresh, t * width + x, levels)
    strip = lambda k, x: part(strips, k * width + x, levels)
    interior(column, strip, nu, weights, store, dims)


def last_kernel(dims, mer_count, partial, edges, incr, weights, spread, mer_gain, inner_gain, outer_gain, *rest):
    tracers, levels, width = dims
    rounds = len(rest) - 3
    recv_mer, (out, done, sems) = rest[:rounds], rest[rounds:]
    lane = lanes_of(levels)
    halo = mer_halo(recv_mer, levels, mer_count)
    lanes = product(weights[...], mer_gain[...] * halo)
    corner = jnp.zeros((levels, 128), f32)
    for t in range(tracers):
        for s in range(2):
            j = t * width + (0 if s == 0 else width - 1)
            moved = pltpu.roll(halo, (2 * (j - tracers * width - s * tracers - t)) % 128, 1)
            corner = jnp.where(lane // 2 == j, moved, corner)
    corner = outer_gain[...] * product(weights[...], inner_gain[...] * corner)
    corner = product(weights[...], corner) + lanes
    rim = jnp.logical_or(lane == 127, lane == 0)
    copies = []
    for x in list(range(1, width - 1)) + [0, width - 1]:
        for t in range(tracers):
            j = t * width + x
            value = part(partial, j, levels) + spread[...] * incr[j:j + 1, :]
            value = value + jnp.where(rim, at_edges(corner if x in (0, width - 1) else lanes, j), 0.0)
            if x in (0, width - 1):
                value = value + part(edges, (0 if x == 0 else tracers) + t, levels)
            done[j] = value
            copy = pltpu.make_async_copy(done.at[j], out.at[t, :, x, :], sems.at[j])
            copy.start()
            copies.append(copy)
    for copy in copies:
        copy.wait()


VM = pl.BlockSpec(memory_space=pltpu.VMEM)
HB = pl.BlockSpec(memory_space=pltpu.HBM)


def call(body, name, in_specs, out_shape, flops, out_specs=None, scratch=()):
    many = isinstance(out_shape, list)
    return pl.pallas_call(
        body,
        out_shape=out_shape,
        in_specs=in_specs,
        out_specs=out_specs or ([VM] * len(out_shape) if many else VM),
        scratch_shapes=scratch,
        name=name,
        cost_estimate=pl.CostEstimate(flops=flops, bytes_accessed=2 << 20, transcendentals=0),
        compiler_params=pltpu.CompilerParams(vmem_limit_bytes=32 * 1024 * 1024),
    )


def on_device(state, flow, diffusion, column_solve, exchange_rate, block_map, ice_mask):
    _, tracers, levels, width, wide = state.shape
    mer_count, zon_count = lax.axis_size("mer"), lax.axis_size("zon")
    rounds = 1 if mer_count == 2 else 2
    dims = (tracers, levels, width)
    size, total = levels * width, tracers * width
    shape = lambda rows, dtype=f32: jax.ShapeDtypeStruct((rows, wide), dtype)
    message = shape((3 * tracers + 2) * levels, bf16)
    packed = shape(levels)
    kept = shape(tracers * size)
    halved = shape(tracers * levels)
    sided = shape(2 * tracers * levels)

    def swap_mer(piece):
        return [lax.ppermute(piece, "mer", pairs(mer_count, r == 1)) for r in range(rounds)]

    def swap_fluid(piece):
        return lax.ppermute(piece, "fluid", [(0, 1), (1, 0)])

    params = (diffusion[0], column_solve[0], exchange_rate, block_map[None], ice_mask[None])
    in_hbm = [pltpu.with_memory_space_constraint(value, pltpu.HBM) for value in (state[0], flow[0]) + params]
    east_bound, west_bound, surface, frame, *params = call(
        functools.partial(pack_kernel, dims), "pack", [HB] * len(in_hbm),
        [message, message, shape(total), shape(2 * size)] + [jax.ShapeDtypeStruct(p.shape, p.dtype) for p in params], 1 << 20,
        scratch=[pltpu.VMEM((4 * tracers, levels, wide), f32), pltpu.VMEM((2, levels, width, wide), bf16),
                 pltpu.SemaphoreType.DMA((5 * tracers + 2 + len(params),))],
    )(*in_hbm)
    from_west = lax.ppermute(east_bound, "zon", ring(zon_count, 1))
    columns, send_mer, nu, weights, spread, guide = call(
        functools.partial(lanes_kernel, dims), "lanes", [VM] * 6,
        [kept, packed, shape(tracers * levels), jax.ShapeDtypeStruct((levels, 3 * levels), bf16), packed, shape(8)], 1 << 20,
    )(state.reshape(tracers * size, wide), *params)
    west_bound, send_mer, surface = lax.optimization_barrier((west_bound, send_mer, surface))
    recv_mer = swap_mer(send_mer)
    other = swap_fluid(surface)
    from_east = lax.ppermute(west_bound, "zon", ring(zon_count, -1))
    partial, strips, mer_gain, edge_lanes, rows = call(
        functools.partial(inner_kernel, dims), "inner", [VM] * 4, [kept, shape(2 * size), packed, packed, shape(total)], 1 << 30,
    )(columns, frame, nu, weights)
    west_sides, west_solved, lanes, incr, half_lanes, half_surface = call(
        functools.partial(west_kernel, dims, mer_count), "west", [VM] * (11 + rounds),
        [halved, halved, packed, shape(total), packed, shape(total + 8)], 1 << 33,
    )(strips, nu, weights, spread, mer_gain, edge_lanes, rows, guide, surface, other, from_west, *recv_mer)
    east_sides, east_solved, fresh_surface, send_mer = call(
        functools.partial(east_kernel, dims), "east", [VM] * 6, [halved, halved, shape(total + 8), packed], 1 << 26,
    )(strips, nu, weights, half_lanes, half_surface, from_east)
    recv_mer = swap_mer(send_mer)
    fresh_other = swap_fluid(fresh_surface)
    again, edges, flux, inner_gain, outer_gain = call(
        functools.partial(middle_kernel, dims), "middle", [VM] * 17,
        [kept, sided, shape(total), packed, packed], 1 << 30, scratch=[pltpu.VMEM((tracers * size, wide), f32)],
    )(partial, strips, nu, weights, spread, west_sides, east_sides, west_solved, east_solved, lanes, incr, columns, guide, fresh_surface, fresh_other, from_west, from_east)
    done = call(
        functools.partial(last_kernel, dims, mer_count), "last", [VM] * (8 + rounds),
        jax.ShapeDtypeStruct(state.shape[1:], f32), 1 << 26,
        out_specs=pl.BlockSpec(memory_space=pl.ANY),
        scratch=[pltpu.VMEM((total, levels, wide), f32), pltpu.SemaphoreType.DMA((total,))],
    )(again, edges, flux, weights, spread, mer_gain, inner_gain, outer_gain, *recv_mer)
    return done[None]


def solution(mesh):
    return jax.shard_map(
        on_device,
        mesh=mesh,
        in_specs=(
            P("fluid", None, None, "zon", "mer"),
            P("fluid", None, None, "zon", "mer"),
            P("fluid", None, None),
            P("fluid", None, None),
            P("fluid", None),
            P("mer"),
            P("mer"),
        ),
        out_specs=P("fluid", None, None, "zon", "mer"),
        check_vma=False,
    )
```

```python
import functools

import jax
import jax.numpy as jnp
from jax import lax
from jax.experimental import pallas as pl
from jax.experimental.pallas import tpu as pltpu
from jax.sharding import PartitionSpec as P

f32, bf16 = jnp.float32, jnp.bfloat16


def ring(count, ahead):
    return [(i, (i + ahead) % count) for i in range(count)]


def pairs(count, odd):
    if odd:
        return [(i, ((i + 1) ^ 1) - 1) for i in range(1, count - 1)] + [(0, count - 1), (count - 1, 0)]
    return [(i, i ^ 1) for i in range(count)]


def surface_level(levels):
    return jnp.where(lax.axis_index("fluid") == 0, levels - 1, 0)


def lanes_of(levels):
    return lax.broadcasted_iota(jnp.int32, (levels, 128), 1)


def split(value):
    high = value.astype(bf16)
    return high, (value - high.astype(f32)).astype(bf16)


def product(weights, value):
    high, low = split(value)
    return jnp.dot(weights, jnp.concatenate([high, low, high], axis=0), preferred_element_type=f32)


def part(ref, index, levels):
    return ref[index * levels:(index + 1) * levels, :]


def mer_halo(recv_mer, levels, mer_count):
    place = lax.axis_index("mer")
    even = 1 - lax.rem(place, 2)
    lane = lanes_of(levels)
    total = jnp.zeros((levels, 128), f32)
    for r, ref in enumerate(recv_mer):
        north = even if r == 0 else 1 - even
        inside = jnp.where(north == 1, place + 1 < mer_count, place > 0)
        keep = jnp.logical_and(lane % 2 == 1 - north, inside)
        moved = pltpu.roll(ref[...], jnp.where(north == 1, 127, 1), 1)
        total = total + jnp.where(keep, moved, 0.0)
    return total


def both_edges(cells, j):
    return pltpu.roll(cells, (2 * j + 1) % 128, 1)


def at_edges(packed, j):
    return pltpu.roll(packed, (127 - 2 * j) % 128, 1)


def increments(own, other, guide, tracers, per_tracer):
    is_atm = lax.axis_index("fluid") == 0
    pick = lambda row: jnp.broadcast_to(guide[row:row + 1, :].astype(jnp.int32), own.shape)
    atm = jnp.where(is_atm, own, other)
    ocean = jnp.where(is_atm, other, own)
    flux = (jnp.take_along_axis(atm, pick(0), axis=1) - ocean) * guide[2:3, :]
    returned = jnp.take_along_axis(flux, pick(1), axis=1)
    tracer = lax.broadcasted_iota(jnp.int32, own.shape, 0) // per_tracer % tracers
    scale = jnp.broadcast_to(guide[3:4, :], own.shape)
    for t in range(1, tracers):
        scale = jnp.where(tracer == t, guide[3 + t:4 + t, :], scale)
    return jnp.where(is_atm, -returned, flux) * scale


def fill_guide(guide, rate, block_map, ice_mask, tracers):
    blocks = block_map.shape[1]
    lane = lax.broadcasted_iota(jnp.int32, (1, 128), 1)
    wide = 128 // blocks
    block, within = lane // wide, lane % wide
    first = lax.axis_index("mer") * blocks
    mapped = jnp.zeros((1, 128), jnp.int32)
    returned = jnp.zeros((1, 128), jnp.int32)
    is_open = jnp.zeros((1, 128), jnp.int32)
    for b in range(blocks):
        above = block_map[:, b:b + 1] - first
        mapped = jnp.where(block == b, above, mapped)
        returned = jnp.where(block == above, b, returned)
        is_open = jnp.where(block == b, 1 - ice_mask[:, b:b + 1], is_open)
    guide[...] = jnp.zeros(guide.shape, f32)
    guide[0:1, :] = (mapped * wide + within).astype(f32)
    guide[1:2, :] = (returned * wide + within).astype(f32)
    guide[2:3, :] = is_open.astype(f32)
    for t in range(tracers):
        guide[3 + t:4 + t, :] = jnp.broadcast_to(rate[:, t:t + 1], (1, 128))


def horizontal(q, east, west, c, d, nu, lane):
    north = jnp.where(lane == 127, 0.0, pltpu.roll(q, 127, 1))
    south = jnp.where(lane == 0, 0.0, pltpu.roll(q, 1, 1))
    return q - c * (east - west) - d * (north - south) + nu * ((east + west) + (north + south) - 4.0 * q)


def interior(column, strip, nu, weights, store, dims):
    tracers, levels, width = dims
    lane = lanes_of(levels)
    zero = jnp.zeros((levels, 128), f32)
    for x in range(width):
        c, d = strip(0, x), strip(1, x)
        terms = []
        for t in range(tracers):
            west = zero if x == 0 else column(t, x - 1)
            east = zero if x == width - 1 else column(t, x + 1)
            terms.append(horizontal(column(t, x), east, west, c, d, part(nu, t, levels), lane))
        solved = product(weights[...], jnp.concatenate(terms, axis=1))
        for t in range(tracers):
            store(t, x, solved[:, t * 128:(t + 1) * 128])


def pack_kernel(dims, state, flow, *rest):
    tracers, levels, width = dims
    size = levels * width
    fixed = len(rest) - 7 >> 1
    east_bound, west_bound, surface, frame = rest[fixed:fixed + 4]
    columns, raw, sems = rest[2 * fixed + 4:]
    level = surface_level(levels)
    places = ((east_bound, width - 1), (east_bound, width - 2), (west_bound, 0), (west_bound, 1))
    wait_columns, wait_flow, wait_rows = [], [], []
    for i, (_, x) in enumerate(places):
        for t in range(tracers):
            at = i * tracers + t
            wait_columns.append(pltpu.make_async_copy(state.at[t, :, x, :], columns.at[at], sems.at[at]))
    used = len(wait_columns)
    for k in range(2):
        wait_flow.append(pltpu.make_async_copy(flow.at[k], raw.at[k], sems.at[used + k]))
    for t in range(tracers):
        target = surface.at[pl.ds(t * width, width), :]
        wait_rows.append(pltpu.make_async_copy(state.at[t, level], target, sems.at[used + 2 + t]))
    for i in range(fixed):
        wait_rows.append(pltpu.make_async_copy(rest[i], rest[fixed + 4 + i], sems.at[used + 2 + tracers + i]))
    for copy in wait_columns + wait_flow + wait_rows:
        copy.start()
    for copy in wait_columns:
        copy.wait()
    for i, (ref, _) in enumerate(places):
        for t in range(tracers):
            high, low = split(columns[i * tracers + t])
            if i % 2 == 0:
                ref[t * levels:(t + 1) * levels, :] = high
                ref[(tracers + t) * levels:(tracers + t + 1) * levels, :] = low
            else:
                ref[(2 * tracers + t) * levels:(2 * tracers + t + 1) * levels, :] = high
    for k, copy in enumerate(wait_flow):
        copy.wait()
        frame[k * size:(k + 1) * size, :] = raw[k].reshape(size, 128).astype(f32) * 0.5
        for ref, x in ((east_bound, width - 1), (west_bound, 0)):
            strip = frame[pl.ds(k * size + x, levels, stride=width), :].astype(bf16)
            ref[(3 * tracers + k) * levels:(3 * tracers + k + 1) * levels, :] = strip
    for copy in wait_rows:
        copy.wait()


def lanes_kernel(dims, cells, diffusion, solve, rate, block_map, ice_mask, columns, send_mer, nu, weights, spread, guide):
    tracers, levels, width = dims
    lane = lanes_of(levels)
    packed = jnp.zeros((levels, 128), f32)
    for t in range(tracers):
        for x in range(width):
            j = t * width + x
            value = cells[pl.ds(t * levels * width + x, levels, stride=width), :]
            columns[j * levels:(j + 1) * levels, :] = value
            packed = jnp.where(lane // 2 == j, both_edges(value, j), packed)
        nu[t * levels:(t + 1) * levels, :] = jnp.transpose(jnp.broadcast_to(diffusion[t:t + 1, :], (128, levels)))
    send_mer[...] = packed
    high, low = split(solve[...])
    weights[...] = jnp.concatenate([high, high, low], axis=1)
    at_level = lax.broadcasted_iota(jnp.int32, (levels, levels), 1) == surface_level(levels)
    fill_guide(guide, rate, block_map, ice_mask, tracers)
    spread[...] = jnp.broadcast_to(jnp.sum(jnp.where(at_level, solve[...], 0.0), axis=1, keepdims=True), (levels, 128))


def inner_kernel(dims, columns, frame, nu, weights, partial, strips, mer_gain, edge_lanes, rows):
    tracers, levels, width = dims
    size = levels * width
    lane = lanes_of(levels)
    packed = jnp.zeros((levels, 128), f32)
    for k in range(2):
        for x in range(width):
            value = frame[pl.ds(k * size + x, levels, stride=width), :]
            strips[(k * width + x) * levels:(k * width + x + 1) * levels, :] = value
            if k == 1:
                packed = jnp.where(lane // 2 == x, both_edges(value, x), packed)
    gain = jnp.zeros((levels, 128), f32)
    for t in range(tracers):
        merid = packed if t == 0 else pltpu.roll(packed, 2 * t * width, 1)
        mine = part(nu, t, levels) + jnp.where(lane % 2 == 0, -merid, merid)
        gain = jnp.where(lane // (2 * width) == t, mine, gain)
    mer_gain[...] = gain

    def store(t, x, value):
        j = t * width + x
        partial[j * levels:(j + 1) * levels, :] = value

    column = lambda t, x: part(columns, t * width + x, levels)
    strip = lambda k, x: part(strips, k * width + x, levels)
    interior(column, strip, nu, weights, store, dims)
    level = surface_level(levels)
    packed = jnp.zeros((levels, 128), f32)
    for j in range(tracers * width):
        packed = jnp.where(lane // 2 == j, both_edges(part(partial, j, levels), j), packed)
    edge_lanes[...] = packed
    for j in range(tracers * width):
        rows[j:j + 1, :] = partial[pl.ds(j * levels + level, 1), :]


def side_terms(ref, s, strips, nu, sides, dims):
    tracers, levels, width = dims
    c = part(strips, 0 if s == 0 else width - 1, levels)
    terms = []
    for t in range(tracers):
        value = part(ref, t, levels).astype(f32) + part(ref, tracers + t, levels).astype(f32)
        sides[t * levels:(t + 1) * levels, :] = value
        terms.append((part(nu, t, levels) + (c if s == 0 else -c)) * value)
    return terms


def side_lanes(packed, s, sides, solved, lane, dims):
    tracers, levels, width = dims
    for t in range(tracers):
        j = t * width + (0 if s == 0 else width - 1)
        packed = packed + jnp.where(lane // 2 == j, both_edges(part(solved, t, levels), j), 0.0)
        j = tracers * width + s * tracers + t
        packed = jnp.where(lane // 2 == j, both_edges(part(sides, t, levels), j), packed)
    return packed


def side_rows(fresh, surface, s, sides, solved, row, level, dims):
    tracers, levels, width = dims
    total = tracers * width
    for t in range(tracers):
        line = solved[pl.ds(t * levels + level, 1), :]
        fresh = fresh + jnp.where(row == t * width + (0 if s == 0 else width - 1), line, 0.0)
        at = total + s * tracers + t
        surface[at:at + 1, :] = sides[pl.ds(t * levels + level, 1), :]
    return fresh


def west_kernel(dims, strips, nu, weights, spread, edge_lanes, rows, guide, own, other, from_west, sides, solved, incr, half_lanes, surface):
    tracers, levels, width = dims
    total = tracers * width
    lane = lanes_of(levels)
    terms = side_terms(from_west, 0, strips, nu, sides, dims)
    result = product(weights[...], jnp.concatenate(terms, axis=1))
    flux = increments(own[...], other[...], guide, tracers, width)
    incr[...] = flux
    for t in range(tracers):
        solved[t * levels:(t + 1) * levels, :] = result[:, t * 128:(t + 1) * 128]
    row = lax.broadcasted_iota(jnp.int32, (total, 128), 0)
    rows_lane = lax.broadcasted_iota(jnp.int32, (total, 128), 1)
    turned = pltpu.roll(flux, 1, 1, stride=2, stride_axis=0)
    turned = jnp.sum(jnp.where(rows_lane // 2 == row, turned, 0.0), axis=0, keepdims=True)
    half_lanes[...] = side_lanes(edge_lanes[...] + spread[...] * turned, 0, sides, solved, lane, dims)
    level = surface_level(levels)
    surface[total:, :] = jnp.zeros((surface.shape[0] - total, 128), f32)
    fresh = rows[...] + spread[pl.ds(level, 1), :] * flux
    surface[:total, :] = side_rows(fresh, surface, 0, sides, solved, row, level, dims)


def east_kernel(dims, mer_count, strips, nu, weights, mer_gain, half_lanes, half_surface, from_east, *rest):
    tracers, levels, width = dims
    total = tracers * width
    rounds = len(rest) - 5
    recv_mer, (sides, solved, lanes, surface, send_mer) = rest[:rounds], rest[rounds:]
    lane = lanes_of(levels)
    terms = side_terms(from_east, 1, strips, nu, sides, dims)
    terms.append(mer_gain[...] * mer_halo(recv_mer, levels, mer_count))
    result = product(weights[...], jnp.concatenate(terms, axis=1))
    for t in range(tracers):
        solved[t * levels:(t + 1) * levels, :] = result[:, t * 128:(t + 1) * 128]
    lanes[...] = result[:, tracers * 128:]
    send_mer[...] = side_lanes(half_lanes[...] + lanes[...], 1, sides, solved, lane, dims)
    row = lax.broadcasted_iota(jnp.int32, (total, 128), 0)
    rows_lane = lax.broadcasted_iota(jnp.int32, (total, 128), 1)
    level = surface_level(levels)
    line = jnp.broadcast_to(lanes[pl.ds(level, 1), :], (total, 128))
    line = jnp.take_along_axis(line, 2 * row + (rows_lane == 0).astype(jnp.int32), axis=1)
    fresh = half_surface[:total, :] + jnp.where(jnp.logical_or(rows_lane == 127, rows_lane == 0), line, 0.0)
    surface[total:, :] = half_surface[total:, :]
    surface[:total, :] = side_rows(fresh, surface, 1, sides, solved, row, level, dims)


def middle_kernel(dims, partial, strips, nu, weights, spread, west_sides, east_sides, west_solved, east_solved, lanes, incr, columns, guide, own, other, from_west, from_east, again, edges, flux, inner_gain, outer_gain, fresh):
    tracers, levels, width = dims
    total = tracers * width
    lane = lanes_of(levels)
    flux[...] = increments(own[:total, :], other[:total, :], guide, tracers, width)
    extra = increments(own[total:, :], other[total:, :], guide, tracers, 1)
    at_level = lax.broadcasted_iota(jnp.int32, (levels, 128), 0) == surface_level(levels)
    terms, gains = [], []
    first = jnp.zeros((levels, 128), f32)
    later = jnp.zeros((levels, 128), f32)
    for s, (ref, sides) in enumerate(((from_west, west_sides), (from_east, east_sides))):
        x = 0 if s == 0 else width - 1
        c, d = (part(ref, 3 * tracers + k, levels).astype(f32) for k in range(2))
        own_c = part(strips, x, levels)
        for t in range(tracers):
            mine, beyond = part(columns, t * width + x, levels), part(ref, 2 * tracers + t, levels).astype(f32)
            east, west = (mine, beyond) if s == 0 else (beyond, mine)
            value = horizontal(part(sides, t, levels), east, west, c, d, part(nu, t, levels), lane)
            value = value + jnp.where(at_level, jnp.broadcast_to(extra[s * tracers + t:s * tracers + t + 1, :], value.shape), 0.0)
            terms.append(value)
            gain = part(nu, t, levels) + (own_c if s == 0 else -own_c)
            gains.append(gain)
            j = t * width + x
            here = lane // 2 == j
            packed = both_edges(d, j)
            first = jnp.where(here, part(nu, t, levels) + jnp.where(lane % 2 == 0, -packed, packed), first)
            later = jnp.where(here, both_edges(gain, j), later)
    inner_gain[...] = first
    outer_gain[...] = later
    result = product(weights[...], jnp.concatenate(terms, axis=1))
    result = product(weights[...], result * jnp.concatenate(gains, axis=1))
    for i in range(2 * tracers):
        edges[i * levels:(i + 1) * levels, :] = result[:, i * 128:(i + 1) * 128]
    rim = jnp.logical_or(lane == 127, lane == 0)
    for t in range(tracers):
        for x in range(width):
            j = t * width + x
            value = part(partial, j, levels) + spread[...] * incr[j:j + 1, :]
            value = value + jnp.where(rim, at_edges(lanes[...], j), 0.0)
            if x in (0, width - 1):
                value = value + part(west_solved if x == 0 else east_solved, t, levels)
            fresh[j * levels:(j + 1) * levels, :] = value

    def store(t, x, value):
        again[pl.ds((t * width + x) * levels, levels), :] = value

    column = lambda t, x: part(fresh, t * width + x, levels)
    strip = lambda k, x: part(strips, k * width + x, levels)
    interior(column, strip, nu, weights, store, dims)


def last_kernel(dims, mer_count, partial, edges, incr, weights, spread, mer_gain, inner_gain, outer_gain, *rest):
    tracers, levels, width = dims
    rounds = len(rest) - 3
    recv_mer, (out, done, sems) = rest[:rounds], rest[rounds:]
    lane = lanes_of(levels)
    halo = mer_halo(recv_mer, levels, mer_count)
    lanes = product(weights[...], mer_gain[...] * halo)
    corner = jnp.zeros((levels, 128), f32)
    for t in range(tracers):
        for s in range(2):
            j = t * width + (0 if s == 0 else width - 1)
            moved = pltpu.roll(halo, (2 * (j - tracers * width - s * tracers - t)) % 128, 1)
            corner = jnp.where(lane // 2 == j, moved, corner)
    corner = outer_gain[...] * product(weights[...], inner_gain[...] * corner)
    corner = product(weights[...], corner) + lanes
    rim = jnp.logical_or(lane == 127, lane == 0)
    copies = []
    for x in list(range(1, width - 1)) + [0, width - 1]:
        for t in range(tracers):
            j = t * width + x
            value = part(partial, j, levels) + spread[...] * incr[j:j + 1, :]
            value = value + jnp.where(rim, at_edges(corner if x in (0, width - 1) else lanes, j), 0.0)
            if x in (0, width - 1):
                value = value + part(edges, (0 if x == 0 else tracers) + t, levels)
            done[j] = value
            copy = pltpu.make_async_copy(done.at[j], out.at[t, :, x, :], sems.at[j])
            copy.start()
            copies.append(copy)
    for copy in copies:
        copy.wait()


VM = pl.BlockSpec(memory_space=pltpu.VMEM)
HB = pl.BlockSpec(memory_space=pltpu.HBM)


def call(body, name, in_specs, out_shape, flops, out_specs=None, scratch=()):
    many = isinstance(out_shape, list)
    return pl.pallas_call(
        body,
        out_shape=out_shape,
        in_specs=in_specs,
        out_specs=out_specs or ([VM] * len(out_shape) if many else VM),
        scratch_shapes=scratch,
        name=name,
        cost_estimate=pl.CostEstimate(flops=flops, bytes_accessed=2 << 20, transcendentals=0),
        compiler_params=pltpu.CompilerParams(vmem_limit_bytes=32 * 1024 * 1024),
    )


def on_device(state, flow, diffusion, column_solve, exchange_rate, block_map, ice_mask):
    _, tracers, levels, width, wide = state.shape
    mer_count, zon_count = lax.axis_size("mer"), lax.axis_size("zon")
    rounds = 1 if mer_count == 2 else 2
    dims = (tracers, levels, width)
    size, total = levels * width, tracers * width
    shape = lambda rows, dtype=f32: jax.ShapeDtypeStruct((rows, wide), dtype)
    message = shape((3 * tracers + 2) * levels, bf16)
    packed = shape(levels)
    kept = shape(tracers * size)
    halved = shape(tracers * levels)
    sided = shape(2 * tracers * levels)

    def swap_mer(piece):
        return [lax.ppermute(piece, "mer", pairs(mer_count, r == 1)) for r in range(rounds)]

    def swap_fluid(piece):
        return lax.ppermute(piece, "fluid", [(0, 1), (1, 0)])

    params = (diffusion[0], column_solve[0], exchange_rate, block_map[None], ice_mask[None])
    in_hbm = [pltpu.with_memory_space_constraint(value, pltpu.HBM) for value in (state[0], flow[0]) + params]
    east_bound, west_bound, surface, frame, *params = call(
        functools.partial(pack_kernel, dims), "pack", [HB] * len(in_hbm),
        [message, message, shape(total), shape(2 * size)] + [jax.ShapeDtypeStruct(p.shape, p.dtype) for p in params], 1 << 20,
        scratch=[pltpu.VMEM((4 * tracers, levels, wide), f32), pltpu.VMEM((2, levels, width, wide), bf16),
                 pltpu.SemaphoreType.DMA((5 * tracers + 2 + len(params),))],
    )(*in_hbm)
    from_west = lax.ppermute(east_bound, "zon", ring(zon_count, 1))
    columns, send_mer, nu, weights, spread, guide = call(
        functools.partial(lanes_kernel, dims), "lanes", [VM] * 6,
        [kept, packed, shape(tracers * levels), jax.ShapeDtypeStruct((levels, 3 * levels), bf16), packed, shape(8)], 1 << 20,
    )(state.reshape(tracers * size, wide), *params)
    recv_mer = swap_mer(send_mer)
    other = swap_fluid(surface)
    from_east = lax.ppermute(west_bound, "zon", ring(zon_count, -1))
    partial, strips, mer_gain, edge_lanes, rows = call(
        functools.partial(inner_kernel, dims), "inner", [VM] * 4, [kept, shape(2 * size), packed, packed, shape(total)], 1 << 30,
    )(columns, frame, nu, weights)
    west_sides, west_solved, incr, half_lanes, half_surface = call(
        functools.partial(west_kernel, dims), "west", [VM] * 10,
        [halved, halved, shape(total), packed, shape(total + 8)], 1 << 33,
    )(strips, nu, weights, spread, edge_lanes, rows, guide, surface, other, from_west)
    east_sides, east_solved, lanes, fresh_surface, send_mer = call(
        functools.partial(east_kernel, dims, mer_count), "east", [VM] * (7 + rounds),
        [halved, halved, packed, shape(total + 8), packed], 1 << 26,
    )(strips, nu, weights, mer_gain, half_lanes, half_surface, from_east, *recv_mer)
    recv_mer = swap_mer(send_mer)
    fresh_other = swap_fluid(fresh_surface)
    again, edges, flux, inner_gain, outer_gain = call(
        functools.partial(middle_kernel, dims), "middle", [VM] * 17,
        [kept, sided, shape(total), packed, packed], 1 << 30, scratch=[pltpu.VMEM((tracers * size, wide), f32)],
    )(partial, strips, nu, weights, spread, west_sides, east_sides, west_solved, east_solved, lanes, incr, columns, guide, fresh_surface, fresh_other, from_west, from_east)
    done = call(
        functools.partial(last_kernel, dims, mer_count), "last", [VM] * (8 + rounds),
        jax.ShapeDtypeStruct(state.shape[1:], f32), 1 << 26,
        out_specs=pl.BlockSpec(memory_space=pl.ANY),
        scratch=[pltpu.VMEM((total, levels, wide), f32), pltpu.SemaphoreType.DMA((total,))],
    )(again, edges, flux, weights, spread, mer_gain, inner_gain, outer_gain, *recv_mer)
    return done[None]


def solution(mesh):
    return jax.shard_map(
        on_device,
        mesh=mesh,
        in_specs=(
            P("fluid", None, None, "zon", "mer"),
            P("fluid", None, None, "zon", "mer"),
            P("fluid", None, None),
            P("fluid", None, None),
            P("fluid", None),
            P("mer"),
            P("mer"),
        ),
        out_specs=P("fluid", None, None, "zon", "mer"),
        check_vma=False,
    )
```

```python
import functools

import jax
import jax.numpy as jnp
from jax import lax
from jax.experimental import pallas as pl
from jax.experimental.pallas import tpu as pltpu
from jax.sharding import PartitionSpec as P

f32, bf16 = jnp.float32, jnp.bfloat16


def pairs(count, odd):
    if odd:
        return [(i, ((i + 1) ^ 1) - 1) for i in range(1, count - 1)] + [(0, count - 1), (count - 1, 0)]
    return [(i, i ^ 1) for i in range(count)]


def side_of(odd, width):
    east = lax.rem(lax.axis_index("zon") + (0 if odd else 1), 2)
    return east * (width - 1), east


def surface_level(levels):
    return jnp.where(lax.axis_index("fluid") == 0, levels - 1, 0)


def lanes_of(levels):
    return lax.broadcasted_iota(jnp.int32, (levels, 128), 1)


def split(value):
    high = value.astype(bf16)
    return high, (value - high.astype(f32)).astype(bf16)


def product(weights, value):
    high, low = split(value)
    return jnp.dot(weights, jnp.concatenate([high, low, high], axis=0), preferred_element_type=f32)


def part(ref, index, levels):
    return ref[index * levels:(index + 1) * levels, :]


def fold(value):
    half = value.shape[0] // 2
    lane = lanes_of(half)
    return jnp.where(lane < 64, value[:half], pltpu.roll(value[half:], 64, 1))


def unfold(value):
    return jnp.concatenate([value, pltpu.roll(value, 64, 1)], axis=0)


def mer_sides(recv_mer, mer_count):
    place = lax.axis_index("mer")
    even = 1 - lax.rem(place, 2)
    for r, ref in enumerate(recv_mer):
        north = even if r == 0 else 1 - even
        yield unfold(ref[...]), north, jnp.where(north == 1, place + 1 < mer_count, place > 0)


def mer_halo(recv_mer, levels, mer_count):
    lane = lanes_of(levels)
    total = jnp.zeros((levels, 128), f32)
    for value, north, inside in mer_sides(recv_mer, mer_count):
        keep = jnp.logical_and(jnp.logical_and(lane % 2 == 1 - north, lane < 64), inside)
        total = total + jnp.where(keep, pltpu.roll(value, jnp.where(north == 1, 127, 1), 1), 0.0)
    return total


def both_edges(cells, j):
    return pltpu.roll(cells, 2 * j + 1, 1)


def at_edges(packed, j):
    return pltpu.roll(packed, (127 - 2 * j) % 128, 1)


def increments(own, other, guide, tracers, per_tracer):
    is_atm = lax.axis_index("fluid") == 0
    pick = lambda row: jnp.broadcast_to(guide[row:row + 1, :].astype(jnp.int32), own.shape)
    atm = jnp.where(is_atm, own, other)
    ocean = jnp.where(is_atm, other, own)
    flux = (jnp.take_along_axis(atm, pick(0), axis=1) - ocean) * guide[2:3, :]
    returned = jnp.take_along_axis(flux, pick(1), axis=1)
    tracer = lax.broadcasted_iota(jnp.int32, own.shape, 0) // per_tracer % tracers
    scale = jnp.broadcast_to(guide[3:4, :], own.shape)
    for t in range(1, tracers):
        scale = jnp.where(tracer == t, guide[3 + t:4 + t, :], scale)
    return jnp.where(is_atm, -returned, flux) * scale


def fill_guide(guide, rate, block_map, ice_mask, tracers):
    blocks = block_map.shape[1]
    lane = lax.broadcasted_iota(jnp.int32, (1, 128), 1)
    wide = 128 // blocks
    block, within = lane // wide, lane % wide
    first = lax.axis_index("mer") * blocks
    mapped = jnp.zeros((1, 128), jnp.int32)
    returned = jnp.zeros((1, 128), jnp.int32)
    is_open = jnp.zeros((1, 128), jnp.int32)
    for b in range(blocks):
        above = block_map[:, b:b + 1] - first
        mapped = jnp.where(block == b, above, mapped)
        returned = jnp.where(block == above, b, returned)
        is_open = jnp.where(block == b, 1 - ice_mask[:, b:b + 1], is_open)
    guide[...] = jnp.zeros(guide.shape, f32)
    guide[0:1, :] = (mapped * wide + within).astype(f32)
    guide[1:2, :] = (returned * wide + within).astype(f32)
    guide[2:3, :] = is_open.astype(f32)
    for t in range(tracers):
        guide[3 + t:4 + t, :] = jnp.broadcast_to(rate[:, t:t + 1], (1, 128))


def horizontal(q, east, west, c, d, nu, lane):
    north = jnp.where(lane == 127, 0.0, pltpu.roll(q, 127, 1))
    south = jnp.where(lane == 0, 0.0, pltpu.roll(q, 1, 1))
    return q - c * (east - west) - d * (north - south) + nu * ((east + west) + (north + south) - 4.0 * q)


def interior(column, strip, nu, weights, store, dims):
    tracers, levels, width = dims
    lane = lanes_of(levels)
    zero = jnp.zeros((levels, 128), f32)
    for x in range(width):
        c, d = strip(0, x), strip(1, x)
        terms = []
        for t in range(tracers):
            west = zero if x == 0 else column(t, x - 1)
            east = zero if x == width - 1 else column(t, x + 1)
            terms.append(horizontal(column(t, x), east, west, c, d, part(nu, t, levels), lane))
        solved = product(weights[...], jnp.concatenate(terms, axis=1))
        for t in range(tracers):
            store(t, x, solved[:, t * 128:(t + 1) * 128])


def pack_kernel(dims, state, flow, *rest):
    tracers, levels, width = dims
    size = levels * width
    fixed = len(rest) - 7 >> 1
    even_bound, odd_bound, surface, frame = rest[fixed:fixed + 4]
    columns, raw, sems = rest[2 * fixed + 4:]
    level = surface_level(levels)
    places = (width - 1, width - 2, 0, 1)
    wait_columns, wait_flow, wait_rows = [], [], []
    for i, x in enumerate(places):
        for t in range(tracers):
            at = i * tracers + t
            wait_columns.append(pltpu.make_async_copy(state.at[t, :, x, :], columns.at[at], sems.at[at]))
    used = len(wait_columns)
    for k in range(2):
        wait_flow.append(pltpu.make_async_copy(flow.at[k], raw.at[k], sems.at[used + k]))
    for t in range(tracers):
        target = surface.at[pl.ds(t * width, width), :]
        wait_rows.append(pltpu.make_async_copy(state.at[t, level], target, sems.at[used + 2 + t]))
    for i in range(fixed):
        wait_rows.append(pltpu.make_async_copy(rest[i], rest[fixed + 4 + i], sems.at[used + 2 + tracers + i]))
    for copy in wait_columns + wait_flow + wait_rows:
        copy.start()
    for copy in wait_columns:
        copy.wait()
    for ref, odd in ((even_bound, False), (odd_bound, True)):
        first = 2 * tracers * (1 - side_of(odd, width)[1])
        for t in range(tracers):
            high, low = split(columns[first + t])
            ref[t * levels:(t + 1) * levels, :] = high
            ref[(tracers + t) * levels:(tracers + t + 1) * levels, :] = low
            ref[(2 * tracers + t) * levels:(2 * tracers + t + 1) * levels, :] = columns[first + tracers + t].astype(bf16)
    for k, copy in enumerate(wait_flow):
        copy.wait()
        frame[k * size:(k + 1) * size, :] = raw[k].reshape(size, 128).astype(f32) * 0.5
        for ref, odd in ((even_bound, False), (odd_bound, True)):
            strip = frame[pl.ds(k * size + side_of(odd, width)[0], levels, stride=width), :].astype(bf16)
            ref[(3 * tracers + k) * levels:(3 * tracers + k + 1) * levels, :] = strip
    for copy in wait_rows:
        copy.wait()


def lanes_kernel(dims, cells, diffusion, solve, rate, block_map, ice_mask, columns, send_mer, nu, weights, spread, guide):
    tracers, levels, width = dims
    lane = lanes_of(levels)
    packed = jnp.zeros((levels, 128), f32)
    for t in range(tracers):
        for x in range(width):
            j = t * width + x
            value = cells[pl.ds(t * levels * width + x, levels, stride=width), :]
            columns[j * levels:(j + 1) * levels, :] = value
            packed = jnp.where(lane // 2 == j, both_edges(value, j), packed)
        nu[t * levels:(t + 1) * levels, :] = jnp.transpose(jnp.broadcast_to(diffusion[t:t + 1, :], (128, levels)))
    send_mer[...] = fold(packed)
    high, low = split(solve[...])
    weights[...] = jnp.concatenate([high, high, low], axis=1)
    at_level = lax.broadcasted_iota(jnp.int32, (levels, levels), 1) == surface_level(levels)
    fill_guide(guide, rate, block_map, ice_mask, tracers)
    spread[...] = jnp.broadcast_to(jnp.sum(jnp.where(at_level, solve[...], 0.0), axis=1, keepdims=True), (levels, 128))


def inner_kernel(dims, columns, frame, nu, weights, partial, strips, mer_gain, edge_lanes, rows):
    tracers, levels, width = dims
    size = levels * width
    lane = lanes_of(levels)
    packed = jnp.zeros((levels, 128), f32)
    for k in range(2):
        for x in range(width):
            value = frame[pl.ds(k * size + x, levels, stride=width), :]
            strips[(k * width + x) * levels:(k * width + x + 1) * levels, :] = value
            if k == 1:
                packed = jnp.where(lane // 2 == x, both_edges(value, x), packed)
    gain = jnp.zeros((levels, 128), f32)
    for t in range(tracers):
        merid = packed if t == 0 else pltpu.roll(packed, 2 * t * width, 1)
        mine = part(nu, t, levels) + jnp.where(lane % 2 == 0, -merid, merid)
        gain = jnp.where(lane // (2 * width) == t, mine, gain)
    mer_gain[...] = gain

    def store(t, x, value):
        j = t * width + x
        partial[j * levels:(j + 1) * levels, :] = value

    column = lambda t, x: part(columns, t * width + x, levels)
    strip = lambda k, x: part(strips, k * width + x, levels)
    interior(column, strip, nu, weights, store, dims)
    level = surface_level(levels)
    packed = jnp.zeros((levels, 128), f32)
    for j in range(tracers * width):
        packed = jnp.where(lane // 2 == j, both_edges(part(partial, j, levels), j), packed)
    edge_lanes[...] = packed
    for j in range(tracers * width):
        rows[j:j + 1, :] = partial[pl.ds(j * levels + level, 1), :]


def column_at(ref, index, levels):
    return ref[pl.ds(pl.multiple_of(index * levels, 8), levels), :]


def side_terms(ref, odd, strips, nu, sides, dims):
    tracers, levels, width = dims
    x, east = side_of(odd, width)
    c = column_at(strips, x, levels) * (1 - 2 * east).astype(f32)
    terms = []
    for t in range(tracers):
        value = part(ref, t, levels).astype(f32) + part(ref, tracers + t, levels).astype(f32)
        sides[t * levels:(t + 1) * levels, :] = value
        terms.append((part(nu, t, levels) + c) * value)
    return terms


def side_lanes(packed, odd, solved, lane, dims):
    tracers, levels, width = dims
    for t in range(tracers):
        j = t * width + side_of(odd, width)[0]
        packed = packed + jnp.where(lane // 2 == j, both_edges(part(solved, t, levels), j), 0.0)
    return packed


def side_rows(fresh, surface, odd, sides, solved, row, level, dims):
    tracers, levels, width = dims
    total = tracers * width
    for t in range(tracers):
        line = solved[pl.ds(t * levels + level, 1), :]
        fresh = fresh + jnp.where(row == t * width + side_of(odd, width)[0], line, 0.0)
        at = total + int(odd) * tracers + t
        surface[at:at + 1, :] = sides[pl.ds(t * levels + level, 1), :]
    return fresh


def even_kernel(dims, strips, nu, weights, spread, edge_lanes, rows, guide, own, other, from_even, sides, solved, incr, half_lanes, surface):
    tracers, levels, width = dims
    total = tracers * width
    lane = lanes_of(levels)
    terms = side_terms(from_even, False, strips, nu, sides, dims)
    result = product(weights[...], jnp.concatenate(terms, axis=1))
    flux = increments(own[...], other[...], guide, tracers, width)
    incr[...] = flux
    for t in range(tracers):
        solved[t * levels:(t + 1) * levels, :] = result[:, t * 128:(t + 1) * 128]
    row = lax.broadcasted_iota(jnp.int32, (total, 128), 0)
    rows_lane = lax.broadcasted_iota(jnp.int32, (total, 128), 1)
    turned = pltpu.roll(flux, 1, 1, stride=2, stride_axis=0)
    turned = jnp.sum(jnp.where(rows_lane // 2 == row, turned, 0.0), axis=0, keepdims=True)
    half_lanes[...] = side_lanes(edge_lanes[...] + spread[...] * turned, False, solved, lane, dims)
    level = surface_level(levels)
    surface[total:, :] = jnp.zeros((surface.shape[0] - total, 128), f32)
    fresh = rows[...] + spread[pl.ds(level, 1), :] * flux
    surface[:total, :] = side_rows(fresh, surface, False, sides, solved, row, level, dims)


def odd_kernel(dims, mer_count, strips, nu, weights, mer_gain, half_lanes, half_surface, even_sides, from_odd, *rest):
    tracers, levels, width = dims
    total = tracers * width
    rounds = (len(rest) - 4) // 2
    recv_mer, (sides, solved, lanes, surface), send_mer = rest[:rounds], rest[rounds:rounds + 4], rest[rounds + 4:]
    lane = lanes_of(levels)
    terms = side_terms(from_odd, True, strips, nu, sides, dims)
    terms.append(mer_gain[...] * mer_halo(recv_mer, levels, mer_count))
    result = product(weights[...], jnp.concatenate(terms, axis=1))
    for t in range(tracers):
        solved[t * levels:(t + 1) * levels, :] = result[:, t * 128:(t + 1) * 128]
    lanes[...] = result[:, tracers * 128:]
    packed = side_lanes(half_lanes[...] + lanes[...], True, solved, lane, dims)
    place = lax.axis_index("mer")
    for r, ref in enumerate(send_mer):
        up = lax.rem(place + 1 + r, 2)
        message = packed
        for s, cells in enumerate((even_sides, sides)):
            for t in range(tracers):
                at = s * tracers + t
                moved = pltpu.roll(part(cells, t, levels), 2 * at + 2 * up, 1)
                message = jnp.where(lane == 2 * at + up, moved, message)
        ref[...] = fold(message)
    row = lax.broadcasted_iota(jnp.int32, (total, 128), 0)
    rows_lane = lax.broadcasted_iota(jnp.int32, (total, 128), 1)
    level = surface_level(levels)
    line = jnp.broadcast_to(lanes[pl.ds(level, 1), :], (total, 128))
    line = jnp.take_along_axis(line, 2 * row + (rows_lane == 0).astype(jnp.int32), axis=1)
    fresh = half_surface[:total, :] + jnp.where(jnp.logical_or(rows_lane == 127, rows_lane == 0), line, 0.0)
    surface[total:, :] = half_surface[total:, :]
    surface[:total, :] = side_rows(fresh, surface, True, sides, solved, row, level, dims)


def middle_kernel(dims, partial, strips, nu, weights, spread, even_sides, odd_sides, even_solved, odd_solved, lanes, incr, columns, guide, own, other, from_even, from_odd, again, edges, flux, inner_gain, outer_gain, fresh):
    tracers, levels, width = dims
    total = tracers * width
    lane = lanes_of(levels)
    flux[...] = increments(own[:total, :], other[:total, :], guide, tracers, width)
    extra = increments(own[total:, :], other[total:, :], guide, tracers, 1)
    at_level = lax.broadcasted_iota(jnp.int32, (levels, 128), 0) == surface_level(levels)
    terms, gains = [], []
    first = jnp.zeros((levels, 128), f32)
    later = jnp.zeros((levels, 128), f32)
    for s, (ref, sides) in enumerate(((from_even, even_sides), (from_odd, odd_sides))):
        x, east = side_of(s == 1, width)
        ahead = (2 * east - 1).astype(f32)
        c, d = (part(ref, 3 * tracers + k, levels).astype(f32) for k in range(2))
        own_c = column_at(strips, x, levels) * ahead
        for t in range(tracers):
            mine, beyond = column_at(columns, t * width + x, levels), part(ref, 2 * tracers + t, levels).astype(f32)
            value = horizontal(part(sides, t, levels), beyond, mine, c * ahead, d, part(nu, t, levels), lane)
            value = value + jnp.where(at_level, jnp.broadcast_to(extra[s * tracers + t:s * tracers + t + 1, :], value.shape), 0.0)
            terms.append(value)
            gain = part(nu, t, levels) - own_c
            gains.append(gain)
            j = t * width + x
            here = lane // 2 == j
            packed = both_edges(d, j)
            first = jnp.where(here, part(nu, t, levels) + jnp.where(lane % 2 == 0, -packed, packed), first)
            later = jnp.where(here, both_edges(gain, j), later)
    inner_gain[...] = first
    outer_gain[...] = later
    result = product(weights[...], jnp.concatenate(terms, axis=1))
    result = product(weights[...], result * jnp.concatenate(gains, axis=1))
    for s in range(2):
        for t in range(tracers):
            at, i = side_of(s == 1, width)[1] * tracers + t, s * tracers + t
            edges[pl.ds(pl.multiple_of(at * levels, 8), levels), :] = result[:, i * 128:(i + 1) * 128]
    rim = jnp.logical_or(lane == 127, lane == 0)
    for t in range(tracers):
        for x in range(width):
            j = t * width + x
            value = part(partial, j, levels) + spread[...] * incr[j:j + 1, :]
            value = value + jnp.where(rim, at_edges(lanes[...], j), 0.0)
            if x in (0, width - 1):
                by_even = side_of(False, width)[0] == x
                value = value + jnp.where(by_even, part(even_solved, t, levels), part(odd_solved, t, levels))
            fresh[j * levels:(j + 1) * levels, :] = value

    def store(t, x, value):
        again[pl.ds((t * width + x) * levels, levels), :] = value

    column = lambda t, x: part(fresh, t * width + x, levels)
    strip = lambda k, x: part(strips, k * width + x, levels)
    interior(column, strip, nu, weights, store, dims)


def last_kernel(dims, mer_count, partial, edges, incr, weights, spread, mer_gain, inner_gain, outer_gain, *rest):
    tracers, levels, width = dims
    rounds = len(rest) - 3
    recv_mer, (out, done, sems) = rest[:rounds], rest[rounds:]
    lane = lanes_of(levels)
    halo = mer_halo(recv_mer, levels, mer_count)
    lanes = product(weights[...], mer_gain[...] * halo)
    corner = jnp.zeros((levels, 128), f32)
    for value, north, inside in mer_sides(recv_mer, mer_count):
        for s in range(2):
            for t in range(tracers):
                j = t * width + side_of(s == 1, width)[0]
                moved = pltpu.roll(value, lax.rem(2 * (j - s * tracers - t) + 128, 128), 1)
                corner = jnp.where(jnp.logical_and(lane == 2 * j + 1 - north, inside), moved, corner)
    corner = outer_gain[...] * product(weights[...], inner_gain[...] * corner)
    corner = product(weights[...], corner) + lanes
    rim = jnp.logical_or(lane == 127, lane == 0)
    copies = []
    for x in list(range(1, width - 1)) + [0, width - 1]:
        for t in range(tracers):
            j = t * width + x
            value = part(partial, j, levels) + spread[...] * incr[j:j + 1, :]
            value = value + jnp.where(rim, at_edges(corner if x in (0, width - 1) else lanes, j), 0.0)
            if x in (0, width - 1):
                value = value + part(edges, (0 if x == 0 else tracers) + t, levels)
            done[j] = value
            copy = pltpu.make_async_copy(done.at[j], out.at[t, :, x, :], sems.at[j])
            copy.start()
            copies.append(copy)
    for copy in copies:
        copy.wait()


VM = pl.BlockSpec(memory_space=pltpu.VMEM)
HB = pl.BlockSpec(memory_space=pltpu.HBM)


def call(body, name, in_specs, out_shape, flops, out_specs=None, scratch=()):
    many = isinstance(out_shape, list)
    return pl.pallas_call(
        body,
        out_shape=out_shape,
        in_specs=in_specs,
        out_specs=out_specs or ([VM] * len(out_shape) if many else VM),
        scratch_shapes=scratch,
        name=name,
        cost_estimate=pl.CostEstimate(flops=flops, bytes_accessed=2 << 20, transcendentals=0),
        compiler_params=pltpu.CompilerParams(vmem_limit_bytes=32 * 1024 * 1024),
    )


def on_device(state, flow, diffusion, column_solve, exchange_rate, block_map, ice_mask):
    _, tracers, levels, width, wide = state.shape
    mer_count, zon_count = lax.axis_size("mer"), lax.axis_size("zon")
    rounds = 1 if mer_count == 2 else 2
    dims = (tracers, levels, width)
    size, total = levels * width, tracers * width
    shape = lambda rows, dtype=f32: jax.ShapeDtypeStruct((rows, wide), dtype)
    message = shape((3 * tracers + 2) * levels, bf16)
    packed = shape(levels)
    folded = shape(levels // 2)
    kept = shape(tracers * size)
    halved = shape(tracers * levels)
    sided = shape(2 * tracers * levels)

    def swap_mer(pieces):
        return [lax.ppermute(piece, "mer", pairs(mer_count, r == 1)) for r, piece in enumerate(pieces)]

    def swap_fluid(piece):
        return lax.ppermute(piece, "fluid", [(0, 1), (1, 0)])

    params = (diffusion[0], column_solve[0], exchange_rate, block_map[None], ice_mask[None])
    in_hbm = [pltpu.with_memory_space_constraint(value, pltpu.HBM) for value in (state[0], flow[0]) + params]
    even_bound, odd_bound, surface, frame, *params = call(
        functools.partial(pack_kernel, dims), "pack", [HB] * len(in_hbm),
        [message, message, shape(total), shape(2 * size)] + [jax.ShapeDtypeStruct(p.shape, p.dtype) for p in params], 1 << 20,
        scratch=[pltpu.VMEM((4 * tracers, levels, wide), f32), pltpu.VMEM((2, levels, width, wide), bf16),
                 pltpu.SemaphoreType.DMA((5 * tracers + 2 + len(params),))],
    )(*in_hbm)
    from_even = lax.ppermute(even_bound, "zon", pairs(zon_count, False))
    columns, send_mer, nu, weights, spread, guide = call(
        functools.partial(lanes_kernel, dims), "lanes", [VM] * 6,
        [kept, folded, shape(tracers * levels), jax.ShapeDtypeStruct((levels, 3 * levels), bf16), packed, shape(8)], 1 << 20,
    )(state.reshape(tracers * size, wide), *params)
    recv_mer = swap_mer([send_mer] * rounds)
    other = swap_fluid(surface)
    from_odd = lax.ppermute(odd_bound, "zon", pairs(zon_count, True))
    partial, strips, mer_gain, edge_lanes, rows = call(
        functools.partial(inner_kernel, dims), "inner", [VM] * 4, [kept, shape(2 * size), packed, packed, shape(total)], 1 << 30,
    )(columns, frame, nu, weights)
    even_sides, even_solved, incr, half_lanes, half_surface = call(
        functools.partial(even_kernel, dims), "even", [VM] * 10,
        [halved, halved, shape(total), packed, shape(total + 8)], 1 << 33,
    )(strips, nu, weights, spread, edge_lanes, rows, guide, surface, other, from_even)
    odd_sides, odd_solved, lanes, fresh_surface, *send_mer = call(
        functools.partial(odd_kernel, dims, mer_count), "odd", [VM] * (8 + rounds),
        [halved, halved, packed, shape(total + 8)] + [folded] * rounds, 1 << 26,
    )(strips, nu, weights, mer_gain, half_lanes, half_surface, even_sides, from_odd, *recv_mer)
    recv_mer = swap_mer(send_mer)
    fresh_other = swap_fluid(fresh_surface)
    again, edges, flux, inner_gain, outer_gain = call(
        functools.partial(middle_kernel, dims), "middle", [VM] * 17,
        [kept, sided, shape(total), packed, packed], 1 << 30, scratch=[pltpu.VMEM((tracers * size, wide), f32)],
    )(partial, strips, nu, weights, spread, even_sides, odd_sides, even_solved, odd_solved, lanes, incr, columns, guide, fresh_surface, fresh_other, from_even, from_odd)
    done = call(
        functools.partial(last_kernel, dims, mer_count), "last", [VM] * (8 + rounds),
        jax.ShapeDtypeStruct(state.shape[1:], f32), 1 << 26,
        out_specs=pl.BlockSpec(memory_space=pl.ANY),
        scratch=[pltpu.VMEM((total, levels, wide), f32), pltpu.SemaphoreType.DMA((total,))],
    )(again, edges, flux, weights, spread, mer_gain, inner_gain, outer_gain, *recv_mer)
    return done[None]


def solution(mesh):
    return jax.shard_map(
        on_device,
        mesh=mesh,
        in_specs=(
            P("fluid", None, None, "zon", "mer"),
            P("fluid", None, None, "zon", "mer"),
            P("fluid", None, None),
            P("fluid", None, None),
            P("fluid", None),
            P("mer"),
            P("mer"),
        ),
        out_specs=P("fluid", None, None, "zon", "mer"),
        check_vma=False,
    )
```

```python
import functools

import jax
import jax.numpy as jnp
from jax import lax
from jax.experimental import pallas as pl
from jax.experimental.pallas import tpu as pltpu
from jax.sharding import PartitionSpec as P

f32, bf16 = jnp.float32, jnp.bfloat16


SCALE = 8192.0


def ring(count, ahead):
    return [(i, (i + ahead) % count) for i in range(count)]


def pairs(count, odd):
    if odd:
        return [(i, ((i + 1) ^ 1) - 1) for i in range(1, count - 1)] + [(0, count - 1), (count - 1, 0)]
    return [(i, i ^ 1) for i in range(count)]


def side_of(east, width):
    return width - 1 if east else 0


def surface_level(levels):
    return jnp.where(lax.axis_index("fluid") == 0, levels - 1, 0)


def lanes_of(levels):
    return lax.broadcasted_iota(jnp.int32, (levels, 128), 1)


def split(value):
    high = value.astype(bf16)
    return high, (value - high.astype(f32)).astype(bf16)


def product(weights, value):
    high, low = split(value)
    return jnp.dot(weights, jnp.concatenate([high, low, high], axis=0), preferred_element_type=f32)


def part(ref, index, levels):
    return ref[index * levels:(index + 1) * levels, :]


def fold(value):
    half = value.shape[0] // 2
    lane = lanes_of(half)
    return jnp.where(lane < 64, value[:half], pltpu.roll(value[half:], 64, 1))


def unfold(value):
    return jnp.concatenate([value, pltpu.roll(value, 64, 1)], axis=0)


def mer_sides(recv_mer, mer_count):
    place = lax.axis_index("mer")
    even = 1 - lax.rem(place, 2)
    for r, ref in enumerate(recv_mer):
        north = even if r == 0 else 1 - even
        yield unfold(ref[...]), north, jnp.where(north == 1, place + 1 < mer_count, place > 0)


def mer_halo(recv_mer, levels, mer_count):
    lane = lanes_of(levels)
    total = jnp.zeros((levels, 128), f32)
    for value, north, inside in mer_sides(recv_mer, mer_count):
        keep = jnp.logical_and(jnp.logical_and(lane % 2 == 1 - north, lane < 64), inside)
        total = total + jnp.where(keep, pltpu.roll(value, jnp.where(north == 1, 127, 1), 1), 0.0)
    return total


def both_edges(cells, j):
    return pltpu.roll(cells, 2 * j + 1, 1)


def at_edges(packed, j):
    return pltpu.roll(packed, (127 - 2 * j) % 128, 1)


def increments(own, other, guide, tracers, per_tracer):
    is_atm = lax.axis_index("fluid") == 0
    pick = lambda row: jnp.broadcast_to(guide[row:row + 1, :].astype(jnp.int32), own.shape)
    atm = jnp.where(is_atm, own, other)
    ocean = jnp.where(is_atm, other, own)
    flux = (jnp.take_along_axis(atm, pick(0), axis=1) - ocean) * guide[2:3, :]
    returned = jnp.take_along_axis(flux, pick(1), axis=1)
    tracer = lax.broadcasted_iota(jnp.int32, own.shape, 0) // per_tracer % tracers
    scale = jnp.broadcast_to(guide[3:4, :], own.shape)
    for t in range(1, tracers):
        scale = jnp.where(tracer == t, guide[3 + t:4 + t, :], scale)
    return jnp.where(is_atm, -returned, flux) * scale


def fill_guide(guide, rate, block_map, ice_mask, tracers):
    blocks = block_map.shape[1]
    lane = lax.broadcasted_iota(jnp.int32, (1, 128), 1)
    wide = 128 // blocks
    block, within = lane // wide, lane % wide
    first = lax.axis_index("mer") * blocks
    mapped = jnp.zeros((1, 128), jnp.int32)
    returned = jnp.zeros((1, 128), jnp.int32)
    is_open = jnp.zeros((1, 128), jnp.int32)
    for b in range(blocks):
        above = block_map[:, b:b + 1] - first
        mapped = jnp.where(block == b, above, mapped)
        returned = jnp.where(block == above, b, returned)
        is_open = jnp.where(block == b, 1 - ice_mask[:, b:b + 1], is_open)
    guide[...] = jnp.zeros(guide.shape, f32)
    guide[0:1, :] = (mapped * wide + within).astype(f32)
    guide[1:2, :] = (returned * wide + within).astype(f32)
    guide[2:3, :] = is_open.astype(f32)
    for t in range(tracers):
        guide[3 + t:4 + t, :] = jnp.broadcast_to(rate[:, t:t + 1], (1, 128))


def horizontal(q, east, west, c, d, nu, lane):
    north = jnp.where(lane == 127, 0.0, pltpu.roll(q, 127, 1))
    south = jnp.where(lane == 0, 0.0, pltpu.roll(q, 1, 1))
    return q - c * (east - west) - d * (north - south) + nu * ((east + west) + (north + south) - 4.0 * q)


def interior(column, strip, nu, weights, store, dims):
    tracers, levels, width = dims
    lane = lanes_of(levels)
    zero = jnp.zeros((levels, 128), f32)
    for x in range(width):
        c, d = strip(0, x), strip(1, x)
        terms = []
        for t in range(tracers):
            west = zero if x == 0 else column(t, x - 1)
            east = zero if x == width - 1 else column(t, x + 1)
            terms.append(horizontal(column(t, x), east, west, c, d, part(nu, t, levels), lane))
        solved = product(weights[...], jnp.concatenate(terms, axis=1))
        for t in range(tracers):
            store(t, x, solved[:, t * 128:(t + 1) * 128])


def pack_kernel(dims, state, flow, *rest):
    tracers, levels, width = dims
    size = levels * width
    fixed = len(rest) - 6 >> 1
    east_bound, west_bound, surface, frame = rest[fixed:fixed + 4]
    raw, sems = rest[2 * fixed + 4:]
    level = surface_level(levels)
    wait_flow, copies = [], []
    for k in range(2):
        wait_flow.append(pltpu.make_async_copy(flow.at[k], raw.at[k], sems.at[k]))
    for ref, places in ((east_bound, (width - 1, width - 2)), (west_bound, (0, 1))):
        for i, x in enumerate(places):
            for t in range(tracers):
                target = ref.at[pl.ds((i * tracers + t) * levels, levels), :]
                copies.append(pltpu.make_async_copy(state.at[t, :, x, :], target, sems.at[2 + len(copies)]))
    for t in range(tracers):
        target = surface.at[pl.ds(t * width, width), :]
        copies.append(pltpu.make_async_copy(state.at[t, level], target, sems.at[2 + len(copies)]))
    for i in range(fixed):
        copies.append(pltpu.make_async_copy(rest[i], rest[fixed + 4 + i], sems.at[2 + len(copies)]))
    for copy in wait_flow + copies:
        copy.start()
    for k, copy in enumerate(wait_flow):
        copy.wait()
        frame[k * size:(k + 1) * size, :] = raw[k].reshape(size, 128).astype(f32) * 0.5
        for ref, x in ((east_bound, width - 1), (west_bound, 0)):
            strip = frame[pl.ds(k * size + x, levels, stride=width), :]
            ref[(2 * tracers + k) * levels:(2 * tracers + k + 1) * levels, :] = strip
    for copy in copies:
        copy.wait()


def lanes_kernel(dims, cells, diffusion, solve, rate, block_map, ice_mask, columns, send_mer, nu, weights, spread, guide):
    tracers, levels, width = dims
    lane = lanes_of(levels)
    packed = jnp.zeros((levels, 128), f32)
    for t in range(tracers):
        for x in range(width):
            j = t * width + x
            value = cells[pl.ds(t * levels * width + x, levels, stride=width), :]
            columns[j * levels:(j + 1) * levels, :] = value
            packed = jnp.where(lane // 2 == j, both_edges(value, j), packed)
        nu[t * levels:(t + 1) * levels, :] = jnp.transpose(jnp.broadcast_to(diffusion[t:t + 1, :], (128, levels)))
    send_mer[...] = fold(packed)
    high, low = split(solve[...])
    weights[...] = jnp.concatenate([high, high, low], axis=1)
    at_level = lax.broadcasted_iota(jnp.int32, (levels, levels), 1) == surface_level(levels)
    fill_guide(guide, rate, block_map, ice_mask, tracers)
    spread[...] = jnp.broadcast_to(jnp.sum(jnp.where(at_level, solve[...], 0.0), axis=1, keepdims=True), (levels, 128))


def inner_kernel(dims, columns, frame, nu, weights, partial, strips, mer_gain, edge_lanes, rows):
    tracers, levels, width = dims
    size = levels * width
    lane = lanes_of(levels)
    packed = jnp.zeros((levels, 128), f32)
    for k in range(2):
        for x in range(width):
            value = frame[pl.ds(k * size + x, levels, stride=width), :]
            strips[(k * width + x) * levels:(k * width + x + 1) * levels, :] = value
            if k == 1:
                packed = jnp.where(lane // 2 == x, both_edges(value, x), packed)
    gain = jnp.zeros((levels, 128), f32)
    for t in range(tracers):
        merid = packed if t == 0 else pltpu.roll(packed, 2 * t * width, 1)
        mine = part(nu, t, levels) + jnp.where(lane % 2 == 0, -merid, merid)
        gain = jnp.where(lane // (2 * width) == t, mine, gain)
    mer_gain[...] = gain

    def store(t, x, value):
        j = t * width + x
        partial[j * levels:(j + 1) * levels, :] = value

    column = lambda t, x: part(columns, t * width + x, levels)
    strip = lambda k, x: part(strips, k * width + x, levels)
    interior(column, strip, nu, weights, store, dims)
    level = surface_level(levels)
    packed = jnp.zeros((levels, 128), f32)
    for j in range(tracers * width):
        packed = jnp.where(lane // 2 == j, both_edges(part(partial, j, levels), j), packed)
    edge_lanes[...] = packed
    for j in range(tracers * width):
        rows[j:j + 1, :] = partial[pl.ds(j * levels + level, 1), :]


def side_terms(ref, east, strips, nu, dims):
    tracers, levels, width = dims
    c = part(strips, side_of(east, width), levels)
    return [(part(nu, t, levels) + (-c if east else c)) * part(ref, t, levels) for t in range(tracers)]


def side_lanes(packed, east, solved, lane, dims):
    tracers, levels, width = dims
    for t in range(tracers):
        j = t * width + side_of(east, width)
        packed = packed + jnp.where(lane // 2 == j, both_edges(part(solved, t, levels), j), 0.0)
    return packed


def side_rows(fresh, surface, east, sides, solved, row, level, dims):
    tracers, levels, width = dims
    total = tracers * width
    for t in range(tracers):
        line = solved[pl.ds(t * levels + level, 1), :]
        fresh = fresh + jnp.where(row == t * width + side_of(east, width), line, 0.0)
        at = total + int(east) * tracers + t
        surface[at:at + 1, :] = sides[pl.ds(t * levels + level, 1), :]
    return fresh


def west_kernel(dims, strips, nu, weights, spread, edge_lanes, rows, guide, own, other, from_west, solved, incr, half_lanes, surface):
    tracers, levels, width = dims
    total = tracers * width
    lane = lanes_of(levels)
    terms = side_terms(from_west, False, strips, nu, dims)
    result = product(weights[...], jnp.concatenate(terms, axis=1))
    flux = increments(own[...], other[...], guide, tracers, width)
    incr[...] = flux
    for t in range(tracers):
        solved[t * levels:(t + 1) * levels, :] = result[:, t * 128:(t + 1) * 128]
    row = lax.broadcasted_iota(jnp.int32, (total, 128), 0)
    rows_lane = lax.broadcasted_iota(jnp.int32, (total, 128), 1)
    turned = pltpu.roll(flux, 1, 1, stride=2, stride_axis=0)
    turned = jnp.sum(jnp.where(rows_lane // 2 == row, turned, 0.0), axis=0, keepdims=True)
    half_lanes[...] = side_lanes(edge_lanes[...] + spread[...] * turned, False, solved, lane, dims)
    level = surface_level(levels)
    surface[total:, :] = jnp.zeros((surface.shape[0] - total, 128), f32)
    fresh = rows[...] + spread[pl.ds(level, 1), :] * flux
    surface[:total, :] = side_rows(fresh, surface, False, from_west, solved, row, level, dims)


def east_kernel(dims, mer_count, strips, nu, weights, mer_gain, half_lanes, half_surface, from_west, from_east, *rest):
    tracers, levels, width = dims
    total = tracers * width
    rounds = (len(rest) - 3) // 2
    recv_mer, (solved, lanes, surface), send_mer = rest[:rounds], rest[rounds:rounds + 3], rest[rounds + 3:]
    lane = lanes_of(levels)
    terms = side_terms(from_east, True, strips, nu, dims)
    terms.append(mer_gain[...] * mer_halo(recv_mer, levels, mer_count))
    result = product(weights[...], jnp.concatenate(terms, axis=1))
    for t in range(tracers):
        solved[t * levels:(t + 1) * levels, :] = result[:, t * 128:(t + 1) * 128]
    lanes[...] = result[:, tracers * 128:]
    packed = side_lanes(half_lanes[...] + lanes[...], True, solved, lane, dims)
    place = lax.axis_index("mer")
    for r, ref in enumerate(send_mer):
        up = lax.rem(place + 1 + r, 2)
        message = packed
        for s, cells in enumerate((from_west, from_east)):
            for t in range(tracers):
                at = s * tracers + t
                moved = pltpu.roll(part(cells, t, levels), 2 * at + 2 * up, 1)
                message = jnp.where(lane == 2 * at + up, moved, message)
        ref[...] = fold(message)
    row = lax.broadcasted_iota(jnp.int32, (total, 128), 0)
    rows_lane = lax.broadcasted_iota(jnp.int32, (total, 128), 1)
    level = surface_level(levels)
    line = jnp.broadcast_to(lanes[pl.ds(level, 1), :], (total, 128))
    line = jnp.take_along_axis(line, 2 * row + (rows_lane == 0).astype(jnp.int32), axis=1)
    fresh = half_surface[:total, :] + jnp.where(jnp.logical_or(rows_lane == 127, rows_lane == 0), line, 0.0)
    surface[total:, :] = half_surface[total:, :]
    surface[:total, :] = side_rows(fresh, surface, True, from_east, solved, row, level, dims)


def middle_kernel(dims, partial, strips, nu, weights, spread, west_solved, east_solved, lanes, incr, columns, guide, own, other, from_west, from_east, again, edges, flux, inner_gain, outer_gain, fresh):
    tracers, levels, width = dims
    total = tracers * width
    lane = lanes_of(levels)
    flux[...] = increments(own[:total, :], other[:total, :], guide, tracers, width)
    extra = increments(own[total:, :], other[total:, :], guide, tracers, 1)
    at_level = lax.broadcasted_iota(jnp.int32, (levels, 128), 0) == surface_level(levels)
    terms, gains = [], []
    first = jnp.zeros((levels, 128), f32)
    later = jnp.zeros((levels, 128), f32)
    for s, ref in enumerate((from_west, from_east)):
        x = side_of(s == 1, width)
        c, d = (part(ref, 2 * tracers + k, levels) for k in range(2))
        own_c = part(strips, x, levels)
        for t in range(tracers):
            mine, beyond = part(columns, t * width + x, levels), part(ref, tracers + t, levels)
            west, east = (mine, beyond) if s == 1 else (beyond, mine)
            value = horizontal(part(ref, t, levels), east, west, c, d, part(nu, t, levels), lane)
            value = value + jnp.where(at_level, jnp.broadcast_to(extra[s * tracers + t:s * tracers + t + 1, :], value.shape), 0.0)
            terms.append(value)
            gain = part(nu, t, levels) + (-own_c if s == 1 else own_c)
            gains.append(gain)
            j = t * width + x
            here = lane // 2 == j
            packed = both_edges(d, j)
            first = jnp.where(here, part(nu, t, levels) + jnp.where(lane % 2 == 0, -packed, packed), first)
            later = jnp.where(here, both_edges(gain, j), later)
    inner_gain[...] = first
    outer_gain[...] = later
    result = product(weights[...], jnp.concatenate(terms, axis=1))
    result = product(weights[...], result * jnp.concatenate(gains, axis=1))
    for i in range(2 * tracers):
        edges[i * levels:(i + 1) * levels, :] = result[:, i * 128:(i + 1) * 128]
    rim = jnp.logical_or(lane == 127, lane == 0)
    for t in range(tracers):
        for x in range(width):
            j = t * width + x
            value = part(partial, j, levels) + spread[...] * incr[j:j + 1, :]
            value = value + jnp.where(rim, at_edges(lanes[...], j), 0.0)
            if x in (0, width - 1):
                value = value + part(west_solved if x == 0 else east_solved, t, levels)
            fresh[j * levels:(j + 1) * levels, :] = value

    def store(t, x, value):
        again[pl.ds((t * width + x) * levels, levels), :] = value

    column = lambda t, x: part(fresh, t * width + x, levels)
    strip = lambda k, x: part(strips, k * width + x, levels)
    interior(column, strip, nu, weights, store, dims)


def last_kernel(dims, mer_count, partial, edges, incr, weights, spread, mer_gain, inner_gain, outer_gain, *rest):
    tracers, levels, width = dims
    rounds = len(rest) - 3
    recv_mer, (out, done, sems) = rest[:rounds], rest[rounds:]
    lane = lanes_of(levels)
    halo = mer_halo(recv_mer, levels, mer_count)
    lanes = product(weights[...], mer_gain[...] * halo)
    corner = jnp.zeros((levels, 128), f32)
    for value, north, inside in mer_sides(recv_mer, mer_count):
        for s in range(2):
            for t in range(tracers):
                j = t * width + side_of(s == 1, width)
                moved = pltpu.roll(value, 2 * (j - s * tracers - t) % 128, 1)
                corner = jnp.where(jnp.logical_and(lane == 2 * j + 1 - north, inside), moved, corner)
    corner = outer_gain[...] * product(weights[...], inner_gain[...] * corner)
    corner = product(weights[...], corner) + lanes
    rim = jnp.logical_or(lane == 127, lane == 0)
    copies = []
    for x in list(range(1, width - 1)) + [0, width - 1]:
        for t in range(tracers):
            j = t * width + x
            value = part(partial, j, levels) + spread[...] * incr[j:j + 1, :]
            value = value + jnp.where(rim, at_edges(corner if x in (0, width - 1) else lanes, j), 0.0)
            if x in (0, width - 1):
                value = value + part(edges, (0 if x == 0 else tracers) + t, levels)
            done[j] = value
            copy = pltpu.make_async_copy(done.at[j], out.at[t, :, x, :], sems.at[j])
            copy.start()
            copies.append(copy)
    for copy in copies:
        copy.wait()


VM = pl.BlockSpec(memory_space=pltpu.VMEM)
HB = pl.BlockSpec(memory_space=pltpu.HBM)


def call(body, name, in_specs, out_shape, flops, out_specs=None, scratch=()):
    many = isinstance(out_shape, list)
    return pl.pallas_call(
        body,
        out_shape=out_shape,
        in_specs=in_specs,
        out_specs=out_specs or ([VM] * len(out_shape) if many else VM),
        scratch_shapes=scratch,
        name=name,
        cost_estimate=pl.CostEstimate(flops=flops, bytes_accessed=2 << 20, transcendentals=0),
        compiler_params=pltpu.CompilerParams(vmem_limit_bytes=32 * 1024 * 1024),
    )


def on_device(state, flow, diffusion, column_solve, exchange_rate, block_map, ice_mask):
    _, tracers, levels, width, wide = state.shape
    mer_count, zon_count = lax.axis_size("mer"), lax.axis_size("zon")
    rounds = 1 if mer_count == 2 else 2
    dims = (tracers, levels, width)
    size, total = levels * width, tracers * width
    shape = lambda rows, dtype=f32: jax.ShapeDtypeStruct((rows, wide), dtype)
    message = shape((2 * tracers + 2) * levels)
    packed = shape(levels)
    folded = shape(levels // 2)
    kept = shape(tracers * size)
    halved = shape(tracers * levels)
    sided = shape(2 * tracers * levels)

    def swap_mer(pieces):
        return [lax.ppermute(piece, "mer", pairs(mer_count, r == 1)) for r, piece in enumerate(pieces)]

    def shift_zonal(piece, ahead):
        moved = lax.ppermute(piece, "zon", ring(zon_count, ahead))
        return moved.astype(f32) * (1.0 / SCALE)

    def swap_fluid(piece):
        return lax.ppermute(piece, "fluid", [(0, 1), (1, 0)])

    params = (diffusion[0], column_solve[0], exchange_rate, block_map[None], ice_mask[None])
    in_hbm = [pltpu.with_memory_space_constraint(value, pltpu.HBM) for value in (state[0], flow[0]) + params]
    east_bound, west_bound, surface, frame, *params = call(
        functools.partial(pack_kernel, dims), "pack", [HB] * len(in_hbm),
        [message, message, shape(total), shape(2 * size)] + [jax.ShapeDtypeStruct(p.shape, p.dtype) for p in params], 1 << 20,
        scratch=[pltpu.VMEM((2, levels, width, wide), bf16),
                 pltpu.SemaphoreType.DMA((5 * tracers + 2 + len(params),))],
    )(*in_hbm)
    east_bound, west_bound = lax.optimization_barrier(((east_bound * SCALE).astype(jnp.float16), (west_bound * SCALE).astype(jnp.float16)))
    from_west = shift_zonal(east_bound, 1)
    columns, send_mer, nu, weights, spread, guide = call(
        functools.partial(lanes_kernel, dims), "lanes", [VM] * 6,
        [kept, folded, shape(tracers * levels), jax.ShapeDtypeStruct((levels, 3 * levels), bf16), packed, shape(8)], 1 << 20,
    )(state.reshape(tracers * size, wide), *params)
    recv_mer = swap_mer([send_mer] * rounds)
    other = swap_fluid(surface)
    from_east = shift_zonal(west_bound, -1)
    partial, strips, mer_gain, edge_lanes, rows = call(
        functools.partial(inner_kernel, dims), "inner", [VM] * 4, [kept, shape(2 * size), packed, packed, shape(total)], 1 << 30,
    )(columns, frame, nu, weights)
    west_solved, incr, half_lanes, half_surface = call(
        functools.partial(west_kernel, dims), "west", [VM] * 10,
        [halved, shape(total), packed, shape(total + 8)], 1 << 33,
    )(strips, nu, weights, spread, edge_lanes, rows, guide, surface, other, from_west)
    east_solved, lanes, fresh_surface, *send_mer = call(
        functools.partial(east_kernel, dims, mer_count), "east", [VM] * (8 + rounds),
        [halved, packed, shape(total + 8)] + [folded] * rounds, 1 << 26,
    )(strips, nu, weights, mer_gain, half_lanes, half_surface, from_west, from_east, *recv_mer)
    recv_mer = swap_mer(send_mer)
    fresh_other = swap_fluid(fresh_surface)
    again, edges, flux, inner_gain, outer_gain = call(
        functools.partial(middle_kernel, dims), "middle", [VM] * 15,
        [kept, sided, shape(total), packed, packed], 1 << 30, scratch=[pltpu.VMEM((tracers * size, wide), f32)],
    )(partial, strips, nu, weights, spread, west_solved, east_solved, lanes, incr, columns, guide, fresh_surface, fresh_other, from_west, from_east)
    done = call(
        functools.partial(last_kernel, dims, mer_count), "last", [VM] * (8 + rounds),
        jax.ShapeDtypeStruct(state.shape[1:], f32), 1 << 26,
        out_specs=pl.BlockSpec(memory_space=pl.ANY),
        scratch=[pltpu.VMEM((total, levels, wide), f32), pltpu.SemaphoreType.DMA((total,))],
    )(again, edges, flux, weights, spread, mer_gain, inner_gain, outer_gain, *recv_mer)
    return done[None]


def solution(mesh):
    return jax.shard_map(
        on_device,
        mesh=mesh,
        in_specs=(
            P("fluid", None, None, "zon", "mer"),
            P("fluid", None, None, "zon", "mer"),
            P("fluid", None, None),
            P("fluid", None, None),
            P("fluid", None),
            P("mer"),
            P("mer"),
        ),
        out_specs=P("fluid", None, None, "zon", "mer"),
        check_vma=False,
    )
```

```python
import functools

import jax
import jax.numpy as jnp
from jax import lax
from jax.experimental import pallas as pl
from jax.experimental.pallas import tpu as pltpu
from jax.sharding import PartitionSpec as P

f32, bf16 = jnp.float32, jnp.bfloat16


SCALE = 8192.0


def ring(count, ahead):
    return [(i, (i + ahead) % count) for i in range(count)]


def pairs(count, odd):
    if odd:
        return [(i, ((i + 1) ^ 1) - 1) for i in range(1, count - 1)] + [(0, count - 1), (count - 1, 0)]
    return [(i, i ^ 1) for i in range(count)]


def side_of(east, width):
    return width - 1 if east else 0


def surface_level(levels):
    return jnp.where(lax.axis_index("fluid") == 0, levels - 1, 0)


def lanes_of(levels):
    return lax.broadcasted_iota(jnp.int32, (levels, 128), 1)


def split(value):
    high = value.astype(bf16)
    return high, (value - high.astype(f32)).astype(bf16)


def product(weights, value):
    high, low = split(value)
    return jnp.dot(weights, jnp.concatenate([high, low, high], axis=0), preferred_element_type=f32)


def part(ref, index, levels):
    return ref[index * levels:(index + 1) * levels, :]


def fold(value):
    half = value.shape[0] // 2
    lane = lanes_of(half)
    return jnp.where(lane < 64, value[:half], pltpu.roll(value[half:], 64, 1))


def unfold(value):
    return jnp.concatenate([value, pltpu.roll(value, 64, 1)], axis=0)


def mer_sides(recv_mer, mer_count):
    place = lax.axis_index("mer")
    even = 1 - lax.rem(place, 2)
    for r, ref in enumerate(recv_mer):
        north = even if r == 0 else 1 - even
        yield unfold(ref[...]), north, jnp.where(north == 1, place + 1 < mer_count, place > 0)


def mer_halo(recv_mer, levels, mer_count):
    lane = lanes_of(levels)
    total = jnp.zeros((levels, 128), f32)
    for value, north, inside in mer_sides(recv_mer, mer_count):
        keep = jnp.logical_and(jnp.logical_and(lane % 2 == 1 - north, lane < 64), inside)
        total = total + jnp.where(keep, pltpu.roll(value, jnp.where(north == 1, 127, 1), 1), 0.0)
    return total


def both_edges(cells, j):
    return pltpu.roll(cells, 2 * j + 1, 1)


def at_edges(packed, j):
    return pltpu.roll(packed, (127 - 2 * j) % 128, 1)


def increments(own, other, guide, tracers, per_tracer):
    is_atm = lax.axis_index("fluid") == 0
    pick = lambda row: jnp.broadcast_to(guide[row:row + 1, :].astype(jnp.int32), own.shape)
    atm = jnp.where(is_atm, own, other)
    ocean = jnp.where(is_atm, other, own)
    flux = (jnp.take_along_axis(atm, pick(0), axis=1) - ocean) * guide[2:3, :]
    returned = jnp.take_along_axis(flux, pick(1), axis=1)
    tracer = lax.broadcasted_iota(jnp.int32, own.shape, 0) // per_tracer % tracers
    scale = jnp.broadcast_to(guide[3:4, :], own.shape)
    for t in range(1, tracers):
        scale = jnp.where(tracer == t, guide[3 + t:4 + t, :], scale)
    return jnp.where(is_atm, -returned, flux) * scale


def fill_guide(guide, rate, block_map, ice_mask, tracers):
    blocks = block_map.shape[1]
    lane = lax.broadcasted_iota(jnp.int32, (1, 128), 1)
    wide = 128 // blocks
    block, within = lane // wide, lane % wide
    first = lax.axis_index("mer") * blocks
    mapped = jnp.zeros((1, 128), jnp.int32)
    returned = jnp.zeros((1, 128), jnp.int32)
    is_open = jnp.zeros((1, 128), jnp.int32)
    for b in range(blocks):
        above = block_map[:, b:b + 1] - first
        mapped = jnp.where(block == b, above, mapped)
        returned = jnp.where(block == above, b, returned)
        is_open = jnp.where(block == b, 1 - ice_mask[:, b:b + 1], is_open)
    guide[...] = jnp.zeros(guide.shape, f32)
    guide[0:1, :] = (mapped * wide + within).astype(f32)
    guide[1:2, :] = (returned * wide + within).astype(f32)
    guide[2:3, :] = is_open.astype(f32)
    for t in range(tracers):
        guide[3 + t:4 + t, :] = jnp.broadcast_to(rate[:, t:t + 1], (1, 128))


def horizontal(q, east, west, north, south, c, d, nu):
    return q - c * (east - west) - d * (north - south) + nu * ((east + west) + (north + south) - 4.0 * q)


def swapped(packed, lane):
    return jnp.where(lane % 2 == 0, pltpu.roll(packed, 127, 1), pltpu.roll(packed, 1, 1))


def interior(column, strip, nu, weights, store, dims):
    tracers, levels, width = dims
    zero = jnp.zeros((levels, 128), f32)
    for x in range(width):
        c, d = strip(0, x), strip(1, x)
        terms = []
        for t in range(tracers):
            west = zero if x == 0 else column(t, x - 1)
            east = zero if x == width - 1 else column(t, x + 1)
            q = column(t, x)
            terms.append(horizontal(q, east, west, pltpu.roll(q, 127, 1), pltpu.roll(q, 1, 1), c, d, part(nu, t, levels)))
        solved = product(weights[...], jnp.concatenate(terms, axis=1))
        for t in range(tracers):
            store(t, x, solved[:, t * 128:(t + 1) * 128])


def pack_kernel(dims, state, flow, *rest):
    tracers, levels, width = dims
    size = levels * width
    fixed = len(rest) - 6 >> 1
    east_bound, west_bound, surface, frame = rest[fixed:fixed + 4]
    raw, sems = rest[2 * fixed + 4:]
    level = surface_level(levels)
    wait_flow, copies = [], []
    for k in range(2):
        wait_flow.append(pltpu.make_async_copy(flow.at[k], raw.at[k], sems.at[k]))
    for ref, places in ((east_bound, (width - 1, width - 2)), (west_bound, (0, 1))):
        for i, x in enumerate(places):
            for t in range(tracers):
                target = ref.at[pl.ds((i * tracers + t) * levels, levels), :]
                copies.append(pltpu.make_async_copy(state.at[t, :, x, :], target, sems.at[2 + len(copies)]))
    for t in range(tracers):
        target = surface.at[pl.ds(t * width, width), :]
        copies.append(pltpu.make_async_copy(state.at[t, level], target, sems.at[2 + len(copies)]))
    for i in range(fixed):
        copies.append(pltpu.make_async_copy(rest[i], rest[fixed + 4 + i], sems.at[2 + len(copies)]))
    for copy in wait_flow + copies:
        copy.start()
    for k, copy in enumerate(wait_flow):
        copy.wait()
        frame[k * size:(k + 1) * size, :] = raw[k].reshape(size, 128).astype(f32) * 0.5
        for ref, x in ((east_bound, width - 1), (west_bound, 0)):
            strip = frame[pl.ds(k * size + x, levels, stride=width), :]
            ref[(2 * tracers + k) * levels:(2 * tracers + k + 1) * levels, :] = strip
    for copy in copies:
        copy.wait()


def lanes_kernel(dims, cells, diffusion, solve, rate, block_map, ice_mask, columns, send_mer, nu, weights, spread, guide):
    tracers, levels, width = dims
    lane = lanes_of(levels)
    packed = jnp.zeros((levels, 128), f32)
    for t in range(tracers):
        for x in range(width):
            j = t * width + x
            value = cells[pl.ds(t * levels * width + x, levels, stride=width), :]
            columns[j * levels:(j + 1) * levels, :] = value
            packed = jnp.where(lane // 2 == j, both_edges(value, j), packed)
        nu[t * levels:(t + 1) * levels, :] = jnp.transpose(jnp.broadcast_to(diffusion[t:t + 1, :], (128, levels)))
    send_mer[...] = fold(packed)
    high, low = split(solve[...])
    weights[...] = jnp.concatenate([high, high, low], axis=1)
    at_level = lax.broadcasted_iota(jnp.int32, (levels, levels), 1) == surface_level(levels)
    fill_guide(guide, rate, block_map, ice_mask, tracers)
    spread[...] = jnp.broadcast_to(jnp.sum(jnp.where(at_level, solve[...], 0.0), axis=1, keepdims=True), (levels, 128))


def inner_kernel(dims, columns, frame, nu, weights, partial, strips, mer_gain, edge_lanes, rows):
    tracers, levels, width = dims
    lane = lanes_of(levels)

    def store(t, x, value):
        j = t * width + x
        partial[j * levels:(j + 1) * levels, :] = value

    def strip(k, x):
        value = frame[pl.ds(k * levels * width + x, levels, stride=width), :]
        strips[(k * width + x) * levels:(k * width + x + 1) * levels, :] = value
        return value

    column = lambda t, x: part(columns, t * width + x, levels)
    interior(column, strip, nu, weights, store, dims)
    packed = jnp.zeros((levels, 128), f32)
    for j in range(tracers * width):
        packed = jnp.where(lane // 2 == j, both_edges(part(partial, j, levels), j), packed)
    edge_lanes[...] = packed
    packed = jnp.zeros((levels, 128), f32)
    for x in range(width):
        packed = jnp.where(lane // 2 == x, both_edges(part(strips, width + x, levels), x), packed)
    gain = jnp.zeros((levels, 128), f32)
    for t in range(tracers):
        merid = packed if t == 0 else pltpu.roll(packed, 2 * t * width, 1)
        mine = part(nu, t, levels) + jnp.where(lane % 2 == 0, -merid, merid)
        gain = jnp.where(lane // (2 * width) == t, mine, gain)
    mer_gain[...] = gain
    rows[...] = partial[pl.ds(surface_level(levels), tracers * width, stride=levels), :]


def side_terms(ref, east, strips, nu, dims):
    tracers, levels, width = dims
    c = part(strips, side_of(east, width), levels)
    return [(part(nu, t, levels) + (-c if east else c)) * part(ref, t, levels) for t in range(tracers)]


def side_lanes(packed, east, solved, lane, dims):
    tracers, levels, width = dims
    for t in range(tracers):
        j = t * width + side_of(east, width)
        packed = packed + jnp.where(lane // 2 == j, both_edges(part(solved, t, levels), j), 0.0)
    return packed


def side_rows(fresh, surface, east, sides, solved, row, level, dims):
    tracers, levels, width = dims
    total = tracers * width
    for t in range(tracers):
        line = solved[pl.ds(t * levels + level, 1), :]
        fresh = fresh + jnp.where(row == t * width + side_of(east, width), line, 0.0)
        at = total + int(east) * tracers + t
        surface[at:at + 1, :] = sides[pl.ds(t * levels + level, 1), :]
    return fresh


def west_kernel(dims, mer_count, strips, nu, weights, spread, mer_gain, edge_lanes, rows, guide, own, other, own_mer, from_west, *rest):
    tracers, levels, width = dims
    total = tracers * width
    rounds = len(rest) - 5
    recv_mer, (solved, lanes, incr, half_lanes, surface) = rest[:rounds], rest[rounds:]
    lane = lanes_of(levels)
    terms = side_terms(from_west, False, strips, nu, dims)
    terms.append(mer_gain[...] * (mer_halo(recv_mer, levels, mer_count) - swapped(unfold(own_mer[...]), lane)))
    result = product(weights[...], jnp.concatenate(terms, axis=1))
    flux = increments(own[...], other[...], guide, tracers, width)
    incr[...] = flux
    for t in range(tracers):
        solved[t * levels:(t + 1) * levels, :] = result[:, t * 128:(t + 1) * 128]
    lanes[...] = result[:, tracers * 128:]
    row = lax.broadcasted_iota(jnp.int32, (total, 128), 0)
    rows_lane = lax.broadcasted_iota(jnp.int32, (total, 128), 1)
    turned = pltpu.roll(flux, 1, 1, stride=2, stride_axis=0)
    turned = jnp.sum(jnp.where(rows_lane // 2 == row, turned, 0.0), axis=0, keepdims=True)
    half_lanes[...] = side_lanes(edge_lanes[...] + lanes[...] + spread[...] * turned, False, solved, lane, dims)
    level = surface_level(levels)
    fresh = rows[...] + spread[pl.ds(level, 1), :] * flux
    line = jnp.broadcast_to(lanes[pl.ds(level, 1), :], (total, 128))
    line = jnp.take_along_axis(line, 2 * row + (rows_lane == 0).astype(jnp.int32), axis=1)
    fresh = fresh + jnp.where(jnp.logical_or(rows_lane == 127, rows_lane == 0), line, 0.0)
    surface[total:, :] = jnp.zeros((surface.shape[0] - total, 128), f32)
    surface[:total, :] = side_rows(fresh, surface, False, from_west, solved, row, level, dims)


def east_kernel(dims, strips, nu, weights, half_lanes, half_surface, from_west, from_east, solved, surface, own_lanes, *send_mer):
    tracers, levels, width = dims
    total = tracers * width
    lane = lanes_of(levels)
    result = product(weights[...], jnp.concatenate(side_terms(from_east, True, strips, nu, dims), axis=1))
    for t in range(tracers):
        solved[t * levels:(t + 1) * levels, :] = result[:, t * 128:(t + 1) * 128]
    packed = side_lanes(half_lanes[...], True, solved, lane, dims)
    own_lanes[...] = packed
    place = lax.axis_index("mer")
    for r, ref in enumerate(send_mer):
        up = lax.rem(place + 1 + r, 2)
        message = packed
        for s, cells in enumerate((from_west, from_east)):
            for t in range(tracers):
                at = s * tracers + t
                moved = pltpu.roll(part(cells, t, levels), 2 * at + 2 * up, 1)
                message = jnp.where(lane == 2 * at + up, moved, message)
        ref[...] = fold(message)
    row = lax.broadcasted_iota(jnp.int32, (total, 128), 0)
    surface[total:, :] = half_surface[total:, :]
    surface[:total, :] = side_rows(half_surface[:total, :], surface, True, from_east, solved, row, surface_level(levels), dims)


def middle_kernel(dims, partial, strips, nu, weights, spread, west_solved, east_solved, lanes, incr, columns, guide, own, other, from_west, from_east, again, inner_gain, outer_gain, fresh):
    tracers, levels, width = dims
    total = tracers * width
    lane = lanes_of(levels)
    flux = increments(own[:total, :], other[:total, :], guide, tracers, width)
    extra = increments(own[total:, :], other[total:, :], guide, tracers, 1)
    at_level = lax.broadcasted_iota(jnp.int32, (levels, 128), 0) == surface_level(levels)
    terms, gains = [], []
    first = jnp.zeros((levels, 128), f32)
    later = jnp.zeros((levels, 128), f32)
    for s, ref in enumerate((from_west, from_east)):
        x = side_of(s == 1, width)
        c, d = (part(ref, 2 * tracers + k, levels) for k in range(2))
        own_c = part(strips, x, levels)
        for t in range(tracers):
            mine, beyond = part(columns, t * width + x, levels), part(ref, tracers + t, levels)
            west, east = (mine, beyond) if s == 1 else (beyond, mine)
            q = part(ref, t, levels)
            north = jnp.where(lane == 127, 0.0, pltpu.roll(q, 127, 1))
            south = jnp.where(lane == 0, 0.0, pltpu.roll(q, 1, 1))
            value = horizontal(q, east, west, north, south, c, d, part(nu, t, levels))
            value = value + jnp.where(at_level, jnp.broadcast_to(extra[s * tracers + t:s * tracers + t + 1, :], value.shape), 0.0)
            terms.append(value)
            gain = part(nu, t, levels) + (-own_c if s == 1 else own_c)
            gains.append(gain)
            j = t * width + x
            here = lane // 2 == j
            packed = both_edges(d, j)
            first = jnp.where(here, part(nu, t, levels) + jnp.where(lane % 2 == 0, -packed, packed), first)
            later = jnp.where(here, both_edges(gain, j), later)
    inner_gain[...] = first
    outer_gain[...] = later
    result = product(weights[...], jnp.concatenate(terms, axis=1))
    result = product(weights[...], result * jnp.concatenate(gains, axis=1))
    rim = jnp.logical_or(lane == 127, lane == 0)
    for t in range(tracers):
        for x in range(width):
            j = t * width + x
            value = part(partial, j, levels) + spread[...] * incr[j:j + 1, :]
            value = value + jnp.where(rim, at_edges(lanes[...], j), 0.0)
            if x in (0, width - 1):
                value = value + part(west_solved if x == 0 else east_solved, t, levels)
            fresh[j * levels:(j + 1) * levels, :] = value

    def store(t, x, value):
        j = t * width + x
        value = value + spread[...] * flux[j:j + 1, :]
        if x in (0, width - 1):
            at = (0 if x == 0 else tracers) + t
            value = value + result[:, at * 128:(at + 1) * 128]
        again[j * levels:(j + 1) * levels, :] = value

    column = lambda t, x: part(fresh, t * width + x, levels)
    strip = lambda k, x: part(strips, k * width + x, levels)
    interior(column, strip, nu, weights, store, dims)


def last_kernel(dims, mer_count, partial, weights, mer_gain, own_lanes, inner_gain, outer_gain, *rest):
    tracers, levels, width = dims
    rounds = len(rest) - 3
    recv_mer, (out, done, sems) = rest[:rounds], rest[rounds:]
    lane = lanes_of(levels)
    halo = mer_halo(recv_mer, levels, mer_count)
    lanes = product(weights[...], mer_gain[...] * (halo - swapped(own_lanes[...], lane)))
    corner = jnp.zeros((levels, 128), f32)
    for value, north, inside in mer_sides(recv_mer, mer_count):
        for s in range(2):
            for t in range(tracers):
                j = t * width + side_of(s == 1, width)
                moved = pltpu.roll(value, 2 * (j - s * tracers - t) % 128, 1)
                corner = jnp.where(jnp.logical_and(lane == 2 * j + 1 - north, inside), moved, corner)
    corner = outer_gain[...] * product(weights[...], inner_gain[...] * corner)
    corner = product(weights[...], corner) + lanes
    rim = jnp.logical_or(lane == 127, lane == 0)
    copies = []
    for x in list(range(1, width - 1)) + [0, width - 1]:
        for t in range(tracers):
            j = t * width + x
            edge = at_edges(corner if x in (0, width - 1) else lanes, j)
            done[j] = part(partial, j, levels) + jnp.where(rim, edge, 0.0)
            copy = pltpu.make_async_copy(done.at[j], out.at[t, :, x, :], sems.at[j])
            copy.start()
            copies.append(copy)
    for copy in copies:
        copy.wait()


VM = pl.BlockSpec(memory_space=pltpu.VMEM)
HB = pl.BlockSpec(memory_space=pltpu.HBM)


def call(body, name, in_specs, out_shape, flops, out_specs=None, scratch=()):
    many = isinstance(out_shape, list)
    return pl.pallas_call(
        body,
        out_shape=out_shape,
        in_specs=in_specs,
        out_specs=out_specs or ([VM] * len(out_shape) if many else VM),
        scratch_shapes=scratch,
        name=name,
        cost_estimate=pl.CostEstimate(flops=flops, bytes_accessed=2 << 20, transcendentals=0),
        compiler_params=pltpu.CompilerParams(vmem_limit_bytes=32 * 1024 * 1024),
    )


def on_device(state, flow, diffusion, column_solve, exchange_rate, block_map, ice_mask):
    _, tracers, levels, width, wide = state.shape
    mer_count, zon_count = lax.axis_size("mer"), lax.axis_size("zon")
    rounds = 1 if mer_count == 2 else 2
    dims = (tracers, levels, width)
    size, total = levels * width, tracers * width
    shape = lambda rows, dtype=f32: jax.ShapeDtypeStruct((rows, wide), dtype)
    message = shape((2 * tracers + 2) * levels)
    packed = shape(levels)
    folded = shape(levels // 2)
    kept = shape(tracers * size)
    halved = shape(tracers * levels)

    def swap_mer(pieces):
        return [lax.ppermute(piece, "mer", pairs(mer_count, r == 1)) for r, piece in enumerate(pieces)]

    def shift_zonal(piece, ahead):
        return lax.ppermute(piece, "zon", ring(zon_count, ahead))

    def widen(piece):
        return piece.astype(f32) * (1.0 / SCALE)

    def swap_fluid(piece):
        return lax.ppermute(piece, "fluid", [(0, 1), (1, 0)])

    params = (diffusion[0], column_solve[0], exchange_rate, block_map[None], ice_mask[None])
    in_hbm = [pltpu.with_memory_space_constraint(value, pltpu.HBM) for value in (state[0], flow[0]) + params]
    east_bound, west_bound, surface, frame, *params = call(
        functools.partial(pack_kernel, dims), "pack", [HB] * len(in_hbm),
        [message, message, shape(total), shape(2 * size)] + [jax.ShapeDtypeStruct(p.shape, p.dtype) for p in params], 1 << 20,
        scratch=[pltpu.VMEM((2, levels, width, wide), bf16),
                 pltpu.SemaphoreType.DMA((5 * tracers + 2 + len(params),))],
    )(*in_hbm)
    east_bound, west_bound = lax.optimization_barrier(((east_bound * SCALE).astype(jnp.float16), (west_bound * SCALE).astype(jnp.float16)))
    from_west = widen(shift_zonal(east_bound, 1))
    columns, send_mer, nu, weights, spread, guide = call(
        functools.partial(lanes_kernel, dims), "lanes", [VM] * 6,
        [kept, folded, shape(tracers * levels), jax.ShapeDtypeStruct((levels, 3 * levels), bf16), packed, shape(8)], 1 << 20,
    )(state.reshape(tracers * size, wide), *params)
    west_bound, send_mer = lax.optimization_barrier((west_bound, send_mer))
    recv_mer = swap_mer([send_mer] * rounds)
    other = swap_fluid(surface)
    from_east = shift_zonal(west_bound, -1)
    partial, strips, mer_gain, edge_lanes, rows = call(
        functools.partial(inner_kernel, dims), "inner", [VM] * 4, [kept, shape(2 * size), packed, packed, shape(total)], 1 << 30,
    )(columns, frame, nu, weights)
    west_solved, lanes, incr, half_lanes, half_surface = call(
        functools.partial(west_kernel, dims, mer_count), "west", [VM] * (12 + rounds),
        [halved, packed, shape(total), packed, shape(total + 8)], 1 << 33,
    )(strips, nu, weights, spread, mer_gain, edge_lanes, rows, guide, surface, other, send_mer, from_west, *recv_mer)
    from_east, half_lanes = lax.optimization_barrier((from_east, half_lanes))
    from_east = widen(from_east)
    east_solved, fresh_surface, own_lanes, *send_mer = call(
        functools.partial(east_kernel, dims), "east", [VM] * 7,
        [halved, shape(total + 8), packed] + [folded] * rounds, 1 << 26,
    )(strips, nu, weights, half_lanes, half_surface, from_west, from_east)
    recv_mer = swap_mer(send_mer)
    fresh_other = swap_fluid(fresh_surface)
    again, inner_gain, outer_gain = call(
        functools.partial(middle_kernel, dims), "middle", [VM] * 15,
        [kept, packed, packed], 1 << 30, scratch=[pltpu.VMEM((tracers * size, wide), f32)],
    )(partial, strips, nu, weights, spread, west_solved, east_solved, lanes, incr, columns, guide, fresh_surface, fresh_other, from_west, from_east)
    done = call(
        functools.partial(last_kernel, dims, mer_count), "last", [VM] * (6 + rounds),
        jax.ShapeDtypeStruct(state.shape[1:], f32), 1 << 26,
        out_specs=pl.BlockSpec(memory_space=pl.ANY),
        scratch=[pltpu.VMEM((total, levels, wide), f32), pltpu.SemaphoreType.DMA((total,))],
    )(again, weights, mer_gain, own_lanes, inner_gain, outer_gain, *recv_mer)
    return done[None]


def solution(mesh):
    return jax.shard_map(
        on_device,
        mesh=mesh,
        in_specs=(
            P("fluid", None, None, "zon", "mer"),
            P("fluid", None, None, "zon", "mer"),
            P("fluid", None, None),
            P("fluid", None, None),
            P("fluid", None),
            P("mer"),
            P("mer"),
        ),
        out_specs=P("fluid", None, None, "zon", "mer"),
        check_vma=False,
    )
```

```python
import functools

import jax
import jax.numpy as jnp
from jax import lax
from jax.experimental import pallas as pl
from jax.experimental.pallas import tpu as pltpu
from jax.sharding import PartitionSpec as P

f32, bf16 = jnp.float32, jnp.bfloat16


SCALE = 8192.0


def ring(count, ahead):
    return [(i, (i + ahead) % count) for i in range(count)]


def pairs(count, odd):
    if odd:
        return [(i, ((i + 1) ^ 1) - 1) for i in range(1, count - 1)] + [(0, count - 1), (count - 1, 0)]
    return [(i, i ^ 1) for i in range(count)]


def side_of(east, width):
    return width - 1 if east else 0


def surface_level(levels):
    return jnp.where(lax.axis_index("fluid") == 0, levels - 1, 0)


def lanes_of(levels):
    return lax.broadcasted_iota(jnp.int32, (levels, 128), 1)


def split(value):
    high = value.astype(bf16)
    return high, (value - high.astype(f32)).astype(bf16)


def product(weights, value):
    high, low = split(value)
    return jnp.dot(weights, jnp.concatenate([high, low, high], axis=0), preferred_element_type=f32)


def part(ref, index, levels):
    return ref[index * levels:(index + 1) * levels, :]


def fold(value):
    half = value.shape[0] // 2
    lane = lanes_of(half)
    return jnp.where(lane < 64, value[:half], pltpu.roll(value[half:], 64, 1))


def unfold(value):
    return jnp.concatenate([value, pltpu.roll(value, 64, 1)], axis=0)


def mer_sides(recv_mer, mer_count):
    place = lax.axis_index("mer")
    even = 1 - lax.rem(place, 2)
    for r, value in enumerate(recv_mer):
        north = even if r == 0 else 1 - even
        yield value, north, jnp.where(north == 1, place + 1 < mer_count, place > 0)


def mer_halo(recv_mer, levels, mer_count):
    lane = lanes_of(levels)
    total = jnp.zeros((levels, 128), f32)
    for value, north, inside in mer_sides(recv_mer, mer_count):
        keep = jnp.logical_and(jnp.logical_and(lane % 2 == 1 - north, lane < 64), inside)
        total = total + jnp.where(keep, pltpu.roll(value, jnp.where(north == 1, 127, 1), 1), 0.0)
    return total


def both_edges(cells, j):
    return pltpu.roll(cells, 2 * j + 1, 1)


def at_edges(packed, j):
    return pltpu.roll(packed, (127 - 2 * j) % 128, 1)


def increments(own, other, guide, tracers, per_tracer):
    is_atm = lax.axis_index("fluid") == 0
    pick = lambda row: jnp.broadcast_to(guide[row:row + 1, :].astype(jnp.int32), own.shape)
    atm = jnp.where(is_atm, own, other)
    ocean = jnp.where(is_atm, other, own)
    flux = (jnp.take_along_axis(atm, pick(0), axis=1) - ocean) * guide[2:3, :]
    returned = jnp.take_along_axis(flux, pick(1), axis=1)
    tracer = lax.broadcasted_iota(jnp.int32, own.shape, 0) // per_tracer % tracers
    scale = jnp.broadcast_to(guide[3:4, :], own.shape)
    for t in range(1, tracers):
        scale = jnp.where(tracer == t, guide[3 + t:4 + t, :], scale)
    return jnp.where(is_atm, -returned, flux) * scale


def fill_guide(guide, rate, block_map, ice_mask, tracers):
    blocks = block_map.shape[1]
    lane = lax.broadcasted_iota(jnp.int32, (1, 128), 1)
    wide = 128 // blocks
    block, within = lane // wide, lane % wide
    first = lax.axis_index("mer") * blocks
    mapped = jnp.zeros((1, 128), jnp.int32)
    returned = jnp.zeros((1, 128), jnp.int32)
    is_open = jnp.zeros((1, 128), jnp.int32)
    for b in range(blocks):
        above = block_map[:, b:b + 1] - first
        mapped = jnp.where(block == b, above, mapped)
        returned = jnp.where(block == above, b, returned)
        is_open = jnp.where(block == b, 1 - ice_mask[:, b:b + 1], is_open)
    guide[...] = jnp.zeros(guide.shape, f32)
    guide[0:1, :] = (mapped * wide + within).astype(f32)
    guide[1:2, :] = (returned * wide + within).astype(f32)
    guide[2:3, :] = is_open.astype(f32)
    for t in range(tracers):
        guide[3 + t:4 + t, :] = jnp.broadcast_to(rate[:, t:t + 1], (1, 128))


def horizontal(q, east, west, c, d, nu, lane):
    north = jnp.where(lane == 127, 0.0, pltpu.roll(q, 127, 1))
    south = jnp.where(lane == 0, 0.0, pltpu.roll(q, 1, 1))
    return q - c * (east - west) - d * (north - south) + nu * ((east + west) + (north + south) - 4.0 * q)


def interior(column, strip, nu, weights, store, dims):
    tracers, levels, width = dims
    lane = lanes_of(levels)
    zero = jnp.zeros((levels, 128), f32)
    for x in range(width):
        c, d = strip(0, x), strip(1, x)
        terms = []
        for t in range(tracers):
            west = zero if x == 0 else column(t, x - 1)
            east = zero if x == width - 1 else column(t, x + 1)
            terms.append(horizontal(column(t, x), east, west, c, d, part(nu, t, levels), lane))
        solved = product(weights[...], jnp.concatenate(terms, axis=1))
        for t in range(tracers):
            store(t, x, solved[:, t * 128:(t + 1) * 128])


def pack_kernel(dims, state, flow, *rest):
    tracers, levels, width = dims
    size = levels * width
    fixed = len(rest) - 6 >> 1
    east_bound, west_bound, surface, frame = rest[fixed:fixed + 4]
    raw, sems = rest[2 * fixed + 4:]
    level = surface_level(levels)
    wait_flow, copies = [], []
    for k in range(2):
        wait_flow.append(pltpu.make_async_copy(flow.at[k], raw.at[k], sems.at[k]))
    for ref, places in ((east_bound, (width - 1, width - 2)), (west_bound, (0, 1))):
        for i, x in enumerate(places):
            for t in range(tracers):
                target = ref.at[pl.ds((i * tracers + t) * levels, levels), :]
                copies.append(pltpu.make_async_copy(state.at[t, :, x, :], target, sems.at[2 + len(copies)]))
    for t in range(tracers):
        target = surface.at[pl.ds(t * width, width), :]
        copies.append(pltpu.make_async_copy(state.at[t, level], target, sems.at[2 + len(copies)]))
    for i in range(fixed):
        copies.append(pltpu.make_async_copy(rest[i], rest[fixed + 4 + i], sems.at[2 + len(copies)]))
    for copy in wait_flow + copies:
        copy.start()
    for k, copy in enumerate(wait_flow):
        copy.wait()
        frame[k * size:(k + 1) * size, :] = raw[k].reshape(size, 128).astype(f32) * 0.5
        for ref, x in ((east_bound, width - 1), (west_bound, 0)):
            strip = frame[pl.ds(k * size + x, levels, stride=width), :]
            ref[(2 * tracers + k) * levels:(2 * tracers + k + 1) * levels, :] = strip
    for copy in copies:
        copy.wait()


def lanes_kernel(dims, cells, frame, diffusion, solve, rate, block_map, ice_mask, columns, send_mer, nu, weights, spread, guide):
    tracers, levels, width = dims
    size = levels * width
    lane = lanes_of(levels)
    packed = jnp.zeros((levels, 128), f32)
    merid = jnp.zeros((levels, 128), f32)
    gain = jnp.zeros((levels, 128), f32)
    for x in range(width):
        strip = frame[pl.ds(size + x, levels, stride=width), :]
        merid = jnp.where(lane // 2 == x, both_edges(strip, x), merid)
    for t in range(tracers):
        for x in range(width):
            j = t * width + x
            value = cells[pl.ds(t * size + x, levels, stride=width), :]
            columns[j * levels:(j + 1) * levels, :] = value
            packed = jnp.where(lane // 2 == j, both_edges(value, j), packed)
        mine = jnp.transpose(jnp.broadcast_to(diffusion[t:t + 1, :], (128, levels)))
        nu[t * levels:(t + 1) * levels, :] = mine
        turned = merid if t == 0 else pltpu.roll(merid, 2 * t * width, 1)
        mine = mine + jnp.where(lane % 2 == 0, -turned, turned)
        gain = jnp.where(lane // (2 * width) == t, mine, gain)
    send_mer[...] = jnp.where(lane < 64, packed, pltpu.roll(gain, 64, 1))
    high, low = split(solve[...])
    weights[...] = jnp.concatenate([high, high, low], axis=1)
    at_level = lax.broadcasted_iota(jnp.int32, (levels, levels), 1) == surface_level(levels)
    fill_guide(guide, rate, block_map, ice_mask, tracers)
    spread[...] = jnp.broadcast_to(jnp.sum(jnp.where(at_level, solve[...], 0.0), axis=1, keepdims=True), (levels, 128))


def inner_kernel(dims, columns, frame, nu, weights, partial, strips, edge_lanes, rows):
    tracers, levels, width = dims
    lane = lanes_of(levels)
    for k in range(2):
        for x in range(width):
            value = frame[pl.ds((k * levels * width) + x, levels, stride=width), :]
            strips[(k * width + x) * levels:(k * width + x + 1) * levels, :] = value

    def store(t, x, value):
        j = t * width + x
        partial[j * levels:(j + 1) * levels, :] = value

    column = lambda t, x: part(columns, t * width + x, levels)
    strip = lambda k, x: part(strips, k * width + x, levels)
    interior(column, strip, nu, weights, store, dims)
    packed = jnp.zeros((levels, 128), f32)
    for j in range(tracers * width):
        packed = jnp.where(lane // 2 == j, both_edges(part(partial, j, levels), j), packed)
    edge_lanes[...] = packed
    rows[...] = partial[pl.ds(surface_level(levels), tracers * width, stride=levels), :]


def side_terms(ref, east, strips, nu, dims):
    tracers, levels, width = dims
    c = part(strips, side_of(east, width), levels)
    return [(part(nu, t, levels) + (-c if east else c)) * part(ref, t, levels) for t in range(tracers)]


def side_lanes(packed, east, solved, lane, dims):
    tracers, levels, width = dims
    for t in range(tracers):
        j = t * width + side_of(east, width)
        packed = packed + jnp.where(lane // 2 == j, both_edges(part(solved, t, levels), j), 0.0)
    return packed


def side_rows(fresh, east, solved, row, level, dims):
    tracers, levels, width = dims
    for t in range(tracers):
        line = solved[pl.ds(t * levels + level, 1), :]
        fresh = fresh + jnp.where(row == t * width + side_of(east, width), line, 0.0)
    return fresh


def west_kernel(dims, strips, nu, weights, spread, edge_lanes, rows, guide, own, other, from_west, solved, incr, half_lanes, surface):
    tracers, levels, width = dims
    total = tracers * width
    lane = lanes_of(levels)
    terms = side_terms(from_west, False, strips, nu, dims)
    result = product(weights[...], jnp.concatenate(terms, axis=1))
    flux = increments(own[...], other[...], guide, tracers, width)
    incr[...] = flux
    for t in range(tracers):
        solved[t * levels:(t + 1) * levels, :] = result[:, t * 128:(t + 1) * 128]
    row = lax.broadcasted_iota(jnp.int32, (total, 128), 0)
    rows_lane = lax.broadcasted_iota(jnp.int32, (total, 128), 1)
    turned = pltpu.roll(flux, 1, 1, stride=2, stride_axis=0)
    turned = jnp.sum(jnp.where(rows_lane // 2 == row, turned, 0.0), axis=0, keepdims=True)
    half_lanes[...] = side_lanes(edge_lanes[...] + spread[...] * turned, False, solved, lane, dims)
    level = surface_level(levels)
    fresh = rows[...] + spread[pl.ds(level, 1), :] * flux
    surface[...] = side_rows(fresh, False, solved, row, level, dims)


def east_kernel(dims, strips, nu, weights, half_lanes, half_surface, from_west, from_east, solved, surface, outside, *send_mer):
    tracers, levels, width = dims
    total = tracers * width
    lane = lanes_of(levels)
    result = product(weights[...], jnp.concatenate(side_terms(from_east, True, strips, nu, dims), axis=1))
    for t in range(tracers):
        solved[t * levels:(t + 1) * levels, :] = result[:, t * 128:(t + 1) * 128]
    packed = side_lanes(half_lanes[...], True, solved, lane, dims)
    place = lax.axis_index("mer")
    for r, ref in enumerate(send_mer):
        up = lax.rem(place + 1 + r, 2)
        message = packed
        for s, cells in enumerate((from_west, from_east)):
            for t in range(tracers):
                at = s * tracers + t
                moved = pltpu.roll(part(cells, t, levels), 2 * at + 2 * up, 1)
                message = jnp.where(lane == 2 * at + up, moved, message)
        ref[:levels // 2, :] = fold(message)
        ref[levels // 2:, :] = jnp.zeros((ref.shape[0] - levels // 2, 128), f32)
    row = lax.broadcasted_iota(jnp.int32, (total, 128), 0)
    level = surface_level(levels)
    surface[...] = side_rows(half_surface[...], True, solved, row, level, dims)
    outside[...] = jnp.zeros(outside.shape, f32)
    for s, cells in enumerate((from_west, from_east)):
        for t in range(tracers):
            outside[s * tracers + t:s * tracers + t + 1, :] = cells[pl.ds(t * levels + level, 1), :]


def meet_kernel(dims, mer_count, weights, own_mer, half_surface, *rest):
    tracers, levels, width = dims
    total = tracers * width
    rounds = len(rest) - 3
    recv_mer, (lanes, beyond, surface) = [ref[...] for ref in rest[:rounds]], rest[rounds:]
    lane = lanes_of(levels)
    edge = jnp.where(lane < 64, own_mer[...], 0.0)
    gain = jnp.where(lane < 64, pltpu.roll(own_mer[...], 64, 1), 0.0)
    here = gain * mer_halo(recv_mer, levels, mer_count)
    there = edge * mer_halo([pltpu.roll(value, 64, 1) for value in recv_mer], levels, mer_count)
    result = product(weights[...], jnp.concatenate([here, there], axis=1))
    lanes[...] = result[:, :128]
    beyond[...] = result[:, 128:]
    row = lax.broadcasted_iota(jnp.int32, (total, 128), 0)
    rows_lane = lax.broadcasted_iota(jnp.int32, (total, 128), 1)
    line = jnp.broadcast_to(lanes[pl.ds(surface_level(levels), 1), :], (total, 128))
    line = jnp.take_along_axis(line, 2 * row + (rows_lane == 0).astype(jnp.int32), axis=1)
    rim = jnp.logical_or(rows_lane == 127, rows_lane == 0)
    surface[...] = half_surface[...] + jnp.where(rim, line, 0.0)


def again_kernel(dims, partial, strips, nu, weights, spread, west_solved, east_solved, lanes, incr, again, fresh):
    tracers, levels, width = dims
    lane = lanes_of(levels)
    rim = jnp.logical_or(lane == 127, lane == 0)
    for t in range(tracers):
        for x in range(width):
            j = t * width + x
            value = part(partial, j, levels) + spread[...] * incr[j:j + 1, :]
            value = value + jnp.where(rim, at_edges(lanes[...], j), 0.0)
            if x in (0, width - 1):
                value = value + part(west_solved if x == 0 else east_solved, t, levels)
            fresh[j * levels:(j + 1) * levels, :] = value

    def store(t, x, value):
        again[pl.ds((t * width + x) * levels, levels), :] = value

    column = lambda t, x: part(fresh, t * width + x, levels)
    strip = lambda k, x: part(strips, k * width + x, levels)
    interior(column, strip, nu, weights, store, dims)


def sides_kernel(dims, columns, strips, nu, weights, guide, own, other, outside, other_outside, from_west, from_east, edges, flux, inner_gain, outer_gain):
    tracers, levels, width = dims
    total = tracers * width
    lane = lanes_of(levels)
    flux[...] = increments(own[...], other[...], guide, tracers, width)
    extra = increments(outside[...], other_outside[...], guide, tracers, 1)
    at_level = lax.broadcasted_iota(jnp.int32, (levels, 128), 0) == surface_level(levels)
    terms, gains = [], []
    first = jnp.zeros((levels, 128), f32)
    later = jnp.zeros((levels, 128), f32)
    for s, ref in enumerate((from_west, from_east)):
        x = side_of(s == 1, width)
        c, d = (part(ref, 2 * tracers + k, levels) for k in range(2))
        own_c = part(strips, x, levels)
        for t in range(tracers):
            mine, beyond = part(columns, t * width + x, levels), part(ref, tracers + t, levels)
            west, east = (mine, beyond) if s == 1 else (beyond, mine)
            value = horizontal(part(ref, t, levels), east, west, c, d, part(nu, t, levels), lane)
            value = value + jnp.where(at_level, jnp.broadcast_to(extra[s * tracers + t:s * tracers + t + 1, :], value.shape), 0.0)
            terms.append(value)
            gain = part(nu, t, levels) + (-own_c if s == 1 else own_c)
            gains.append(gain)
            j = t * width + x
            here = lane // 2 == j
            packed = both_edges(d, j)
            first = jnp.where(here, part(nu, t, levels) + jnp.where(lane % 2 == 0, -packed, packed), first)
            later = jnp.where(here, both_edges(gain, j), later)
    inner_gain[...] = first
    outer_gain[...] = later
    result = product(weights[...], jnp.concatenate(terms, axis=1))
    result = product(weights[...], result * jnp.concatenate(gains, axis=1))
    for i in range(2 * tracers):
        edges[i * levels:(i + 1) * levels, :] = result[:, i * 128:(i + 1) * 128]


def last_kernel(dims, mer_count, partial, edges, incr, weights, spread, own_mer, beyond, inner_gain, outer_gain, *rest):
    tracers, levels, width = dims
    rounds = len(rest) - 3
    recv_mer, (out, done, sems) = [unfold(ref[:levels // 2, :]) for ref in rest[:rounds]], rest[rounds:]
    lane = lanes_of(levels)
    halo = mer_halo(recv_mer, levels, mer_count) + beyond[...]
    gain = jnp.where(lane < 64, pltpu.roll(own_mer[...], 64, 1), 0.0)
    lanes = product(weights[...], gain * halo)
    corner = jnp.zeros((levels, 128), f32)
    for value, north, inside in mer_sides(recv_mer, mer_count):
        for s in range(2):
            for t in range(tracers):
                j = t * width + side_of(s == 1, width)
                moved = pltpu.roll(value, 2 * (j - s * tracers - t) % 128, 1)
                corner = jnp.where(jnp.logical_and(lane == 2 * j + 1 - north, inside), moved, corner)
    corner = outer_gain[...] * product(weights[...], inner_gain[...] * corner)
    corner = product(weights[...], corner) + lanes
    rim = jnp.logical_or(lane == 127, lane == 0)
    copies = []
    for x in list(range(1, width - 1)) + [0, width - 1]:
        for t in range(tracers):
            j = t * width + x
            value = part(partial, j, levels) + spread[...] * incr[j:j + 1, :]
            value = value + jnp.where(rim, at_edges(corner if x in (0, width - 1) else lanes, j), 0.0)
            if x in (0, width - 1):
                value = value + part(edges, (0 if x == 0 else tracers) + t, levels)
            done[j] = value
            copy = pltpu.make_async_copy(done.at[j], out.at[t, :, x, :], sems.at[j])
            copy.start()
            copies.append(copy)
    for copy in copies:
        copy.wait()


VM = pl.BlockSpec(memory_space=pltpu.VMEM)
HB = pl.BlockSpec(memory_space=pltpu.HBM)


def call(body, name, in_specs, out_shape, flops, out_specs=None, scratch=(), touched=2 << 20):
    many = isinstance(out_shape, list)
    return pl.pallas_call(
        body,
        out_shape=out_shape,
        in_specs=in_specs,
        out_specs=out_specs or ([VM] * len(out_shape) if many else VM),
        scratch_shapes=scratch,
        name=name,
        cost_estimate=pl.CostEstimate(flops=flops, bytes_accessed=touched, transcendentals=0),
        compiler_params=pltpu.CompilerParams(vmem_limit_bytes=32 * 1024 * 1024),
    )


def on_device(state, flow, diffusion, column_solve, exchange_rate, block_map, ice_mask):
    _, tracers, levels, width, wide = state.shape
    mer_count, zon_count = lax.axis_size("mer"), lax.axis_size("zon")
    rounds = 1 if mer_count == 2 else 2
    dims = (tracers, levels, width)
    size, total = levels * width, tracers * width
    shape = lambda rows, dtype=f32: jax.ShapeDtypeStruct((rows, wide), dtype)
    message = shape((2 * tracers + 2) * levels)
    packed = shape(levels)
    folded = shape(levels // 2 + 8)
    kept = shape(tracers * size)
    halved = shape(tracers * levels)
    sided = shape(2 * tracers * levels)

    def swap_mer(pieces):
        return [lax.ppermute(piece, "mer", pairs(mer_count, r == 1)) for r, piece in enumerate(pieces)]

    def shift_zonal(piece, ahead):
        return lax.ppermute(piece, "zon", ring(zon_count, ahead))

    def widen(piece):
        return piece.astype(f32) * (1.0 / SCALE)

    def swap_fluid(piece):
        return lax.ppermute(piece, "fluid", [(0, 1), (1, 0)])

    params = (diffusion[0], column_solve[0], exchange_rate, block_map[None], ice_mask[None])
    in_hbm = [pltpu.with_memory_space_constraint(value, pltpu.HBM) for value in (state[0], flow[0]) + params]
    east_bound, west_bound, surface, frame, *params = call(
        functools.partial(pack_kernel, dims), "pack", [HB] * len(in_hbm),
        [message, message, shape(total), shape(2 * size)] + [jax.ShapeDtypeStruct(p.shape, p.dtype) for p in params], 1 << 20,
        scratch=[pltpu.VMEM((2, levels, width, wide), bf16),
                 pltpu.SemaphoreType.DMA((5 * tracers + 2 + len(params),))],
    )(*in_hbm)
    east_bound, west_bound = lax.optimization_barrier(((east_bound * SCALE).astype(jnp.float16), (west_bound * SCALE).astype(jnp.float16)))
    from_west = widen(shift_zonal(east_bound, 1))
    columns, own_mer, nu, weights, spread, guide = call(
        functools.partial(lanes_kernel, dims), "lanes", [VM] * 7,
        [kept, packed, shape(tracers * levels), jax.ShapeDtypeStruct((levels, 3 * levels), bf16), packed, shape(8)], 1 << 20,
    )(state.reshape(tracers * size, wide), frame, *params)
    recv_mer = swap_mer([own_mer] * rounds)
    other = swap_fluid(surface)
    from_east = shift_zonal(west_bound, -1)
    partial, strips, edge_lanes, rows = call(
        functools.partial(inner_kernel, dims), "inner", [VM] * 4, [kept, shape(2 * size), packed, shape(total)], 1 << 30,
    )(columns, frame, nu, weights)
    west_solved, incr, half_lanes, half_surface = call(
        functools.partial(west_kernel, dims), "west", [VM] * 10,
        [halved, shape(total), packed, shape(total)], 1 << 33,
    )(strips, nu, weights, spread, edge_lanes, rows, guide, surface, other, from_west)
    from_east, half_lanes = lax.optimization_barrier((from_east, half_lanes))
    from_east = widen(from_east)
    east_solved, half_surface, outside, *send_mer = call(
        functools.partial(east_kernel, dims), "east", [VM] * 7, [halved, shape(total), shape(8)] + [folded] * rounds, 1 << 26,
    )(strips, nu, weights, half_lanes, half_surface, from_west, from_east)
    recv_again = swap_mer(send_mer)
    other_outside = swap_fluid(outside)
    lanes, beyond, fresh_surface = call(
        functools.partial(meet_kernel, dims, mer_count), "meet", [VM] * (3 + rounds), [packed, packed, shape(total)], 1 << 33,
    )(weights, own_mer, half_surface, *recv_mer)
    fresh_other = swap_fluid(fresh_surface)
    again = call(
        functools.partial(again_kernel, dims), "again", [VM] * 9, kept, 1 << 10, touched=1 << 10, scratch=[pltpu.VMEM((tracers * size, wide), f32)],
    )(partial, strips, nu, weights, spread, west_solved, east_solved, lanes, incr)
    edges, flux, inner_gain, outer_gain = call(
        functools.partial(sides_kernel, dims), "sides", [VM] * 11, [sided, shape(total), packed, packed], 1 << 10, touched=1 << 10,
    )(columns, strips, nu, weights, guide, fresh_surface, fresh_other, outside, other_outside, from_west, from_east)
    done = call(
        functools.partial(last_kernel, dims, mer_count), "last", [VM] * (9 + rounds),
        jax.ShapeDtypeStruct(state.shape[1:], f32), 1 << 26,
        out_specs=pl.BlockSpec(memory_space=pl.ANY),
        scratch=[pltpu.VMEM((total, levels, wide), f32), pltpu.SemaphoreType.DMA((total,))],
    )(again, edges, flux, weights, spread, own_mer, beyond, inner_gain, outer_gain, *recv_again)
    return done[None]


def solution(mesh):
    return jax.shard_map(
        on_device,
        mesh=mesh,
        in_specs=(
            P("fluid", None, None, "zon", "mer"),
            P("fluid", None, None, "zon", "mer"),
            P("fluid", None, None),
            P("fluid", None, None),
            P("fluid", None),
            P("mer"),
            P("mer"),
        ),
        out_specs=P("fluid", None, None, "zon", "mer"),
        check_vma=False,
    )
```

```python
import functools

import jax
import jax.numpy as jnp
from jax import lax
from jax.experimental import pallas as pl
from jax.experimental.pallas import tpu as pltpu
from jax.sharding import PartitionSpec as P

f32, bf16 = jnp.float32, jnp.bfloat16


SCALE = 8192.0


def ring(count, ahead):
    return [(i, (i + ahead) % count) for i in range(count)]


def pairs(count, odd):
    if odd:
        return [(i, ((i + 1) ^ 1) - 1) for i in range(1, count - 1)] + [(0, count - 1), (count - 1, 0)]
    return [(i, i ^ 1) for i in range(count)]


def side_of(east, width):
    return width - 1 if east else 0


def surface_level(levels):
    return jnp.where(lax.axis_index("fluid") == 0, levels - 1, 0)


def lanes_of(levels):
    return lax.broadcasted_iota(jnp.int32, (levels, 128), 1)


def split(value):
    high = value.astype(bf16)
    return high, (value - high.astype(f32)).astype(bf16)


def product(weights, value):
    high, low = split(value)
    return jnp.dot(weights, jnp.concatenate([high, low, high], axis=0), preferred_element_type=f32)


def part(ref, index, levels):
    return ref[index * levels:(index + 1) * levels, :]


def fold(value):
    half = value.shape[0] // 2
    lane = lanes_of(half)
    return jnp.where(lane < 64, value[:half], pltpu.roll(value[half:], 64, 1))


def unfold(value):
    return jnp.concatenate([value, pltpu.roll(value, 64, 1)], axis=0)


def mer_sides(recv_mer, mer_count):
    place = lax.axis_index("mer")
    even = 1 - lax.rem(place, 2)
    for r, value in enumerate(recv_mer):
        north = even if r == 0 else 1 - even
        yield value, north, jnp.where(north == 1, place + 1 < mer_count, place > 0)


def mer_halo(recv_mer, levels, mer_count):
    lane = lanes_of(levels)
    total = jnp.zeros((levels, 128), f32)
    for value, north, inside in mer_sides(recv_mer, mer_count):
        keep = jnp.logical_and(jnp.logical_and(lane % 2 == 1 - north, lane < 64), inside)
        total = total + jnp.where(keep, pltpu.roll(value, jnp.where(north == 1, 127, 1), 1), 0.0)
    return total


def both_edges(cells, j):
    return pltpu.roll(cells, 2 * j + 1, 1)


def at_edges(packed, j):
    return pltpu.roll(packed, (127 - 2 * j) % 128, 1)


def increments(own, other, guide, tracers, per_tracer):
    is_atm = lax.axis_index("fluid") == 0
    pick = lambda row: jnp.broadcast_to(guide[row:row + 1, :].astype(jnp.int32), own.shape)
    atm = jnp.where(is_atm, own, other)
    ocean = jnp.where(is_atm, other, own)
    flux = (jnp.take_along_axis(atm, pick(0), axis=1) - ocean) * guide[2:3, :]
    returned = jnp.take_along_axis(flux, pick(1), axis=1)
    tracer = lax.broadcasted_iota(jnp.int32, own.shape, 0) // per_tracer % tracers
    scale = jnp.broadcast_to(guide[3:4, :], own.shape)
    for t in range(1, tracers):
        scale = jnp.where(tracer == t, guide[3 + t:4 + t, :], scale)
    return jnp.where(is_atm, -returned, flux) * scale


def fill_guide(guide, rate, block_map, ice_mask, tracers):
    blocks = block_map.shape[1]
    lane = lax.broadcasted_iota(jnp.int32, (1, 128), 1)
    wide = 128 // blocks
    block, within = lane // wide, lane % wide
    first = lax.axis_index("mer") * blocks
    mapped = jnp.zeros((1, 128), jnp.int32)
    returned = jnp.zeros((1, 128), jnp.int32)
    is_open = jnp.zeros((1, 128), jnp.int32)
    for b in range(blocks):
        above = block_map[:, b:b + 1] - first
        mapped = jnp.where(block == b, above, mapped)
        returned = jnp.where(block == above, b, returned)
        is_open = jnp.where(block == b, 1 - ice_mask[:, b:b + 1], is_open)
    guide[...] = jnp.zeros(guide.shape, f32)
    guide[0:1, :] = (mapped * wide + within).astype(f32)
    guide[1:2, :] = (returned * wide + within).astype(f32)
    guide[2:3, :] = is_open.astype(f32)
    for t in range(tracers):
        guide[3 + t:4 + t, :] = jnp.broadcast_to(rate[:, t:t + 1], (1, 128))


def horizontal(q, east, west, c, d, nu, lane):
    north = jnp.where(lane == 127, 0.0, pltpu.roll(q, 127, 1))
    south = jnp.where(lane == 0, 0.0, pltpu.roll(q, 1, 1))
    return q - c * (east - west) - d * (north - south) + nu * ((east + west) + (north + south) - 4.0 * q)


def interior(column, strip, nu, weights, store, dims):
    tracers, levels, width = dims
    lane = lanes_of(levels)
    zero = jnp.zeros((levels, 128), f32)
    for x in range(width):
        c, d = strip(0, x), strip(1, x)
        terms = []
        for t in range(tracers):
            west = zero if x == 0 else column(t, x - 1)
            east = zero if x == width - 1 else column(t, x + 1)
            terms.append(horizontal(column(t, x), east, west, c, d, part(nu, t, levels), lane))
        solved = product(weights[...], jnp.concatenate(terms, axis=1))
        for t in range(tracers):
            store(t, x, solved[:, t * 128:(t + 1) * 128])


def pack_kernel(dims, state, flow, *rest):
    tracers, levels, width = dims
    size = levels * width
    fixed = len(rest) - 6 >> 1
    east_bound, west_bound, surface, frame = rest[fixed:fixed + 4]
    raw, sems = rest[2 * fixed + 4:]
    level = surface_level(levels)
    wait_flow, copies = [], []
    for k in range(2):
        wait_flow.append(pltpu.make_async_copy(flow.at[k], raw.at[k], sems.at[k]))
    for ref, places in ((east_bound, (width - 1, width - 2)), (west_bound, (0, 1))):
        for i, x in enumerate(places):
            for t in range(tracers):
                target = ref.at[pl.ds((i * tracers + t) * levels, levels), :]
                copies.append(pltpu.make_async_copy(state.at[t, :, x, :], target, sems.at[2 + len(copies)]))
    for t in range(tracers):
        target = surface.at[pl.ds(t * width, width), :]
        copies.append(pltpu.make_async_copy(state.at[t, level], target, sems.at[2 + len(copies)]))
    for i in range(fixed):
        copies.append(pltpu.make_async_copy(rest[i], rest[fixed + 4 + i], sems.at[2 + len(copies)]))
    for copy in wait_flow + copies:
        copy.start()
    for k, copy in enumerate(wait_flow):
        copy.wait()
        frame[k * size:(k + 1) * size, :] = raw[k].reshape(size, 128).astype(f32) * 0.5
        for ref, x in ((east_bound, width - 1), (west_bound, 0)):
            strip = frame[pl.ds(k * size + x, levels, stride=width), :]
            ref[(2 * tracers + k) * levels:(2 * tracers + k + 1) * levels, :] = strip
    for copy in copies:
        copy.wait()


def lanes_kernel(dims, cells, frame, diffusion, solve, rate, block_map, ice_mask, columns, send_mer, nu, weights, spread, guide):
    tracers, levels, width = dims
    size = levels * width
    lane = lanes_of(levels)
    packed = jnp.zeros((levels, 128), f32)
    merid = jnp.zeros((levels, 128), f32)
    gain = jnp.zeros((levels, 128), f32)
    for x in range(width):
        strip = frame[pl.ds(size + x, levels, stride=width), :]
        merid = jnp.where(lane // 2 == x, both_edges(strip, x), merid)
    for t in range(tracers):
        for x in range(width):
            j = t * width + x
            value = cells[pl.ds(t * size + x, levels, stride=width), :]
            columns[j * levels:(j + 1) * levels, :] = value
            packed = jnp.where(lane // 2 == j, both_edges(value, j), packed)
        mine = jnp.transpose(jnp.broadcast_to(diffusion[t:t + 1, :], (128, levels)))
        nu[t * levels:(t + 1) * levels, :] = mine
        turned = merid if t == 0 else pltpu.roll(merid, 2 * t * width, 1)
        mine = mine + jnp.where(lane % 2 == 0, -turned, turned)
        gain = jnp.where(lane // (2 * width) == t, mine, gain)
    send_mer[...] = jnp.where(lane < 64, packed, pltpu.roll(gain, 64, 1))
    high, low = split(solve[...])
    weights[...] = jnp.concatenate([high, high, low], axis=1)
    at_level = lax.broadcasted_iota(jnp.int32, (levels, levels), 1) == surface_level(levels)
    fill_guide(guide, rate, block_map, ice_mask, tracers)
    spread[...] = jnp.broadcast_to(jnp.sum(jnp.where(at_level, solve[...], 0.0), axis=1, keepdims=True), (levels, 128))


def inner_kernel(dims, columns, frame, nu, weights, partial, strips, edge_lanes, rows):
    tracers, levels, width = dims
    lane = lanes_of(levels)
    for k in range(2):
        for x in range(width):
            value = frame[pl.ds((k * levels * width) + x, levels, stride=width), :]
            strips[(k * width + x) * levels:(k * width + x + 1) * levels, :] = value

    def store(t, x, value):
        j = t * width + x
        partial[j * levels:(j + 1) * levels, :] = value

    column = lambda t, x: part(columns, t * width + x, levels)
    strip = lambda k, x: part(strips, k * width + x, levels)
    interior(column, strip, nu, weights, store, dims)
    packed = jnp.zeros((levels, 128), f32)
    for j in range(tracers * width):
        packed = jnp.where(lane // 2 == j, both_edges(part(partial, j, levels), j), packed)
    edge_lanes[...] = packed
    rows[...] = partial[pl.ds(surface_level(levels), tracers * width, stride=levels), :]


def side_terms(ref, east, strips, nu, dims):
    tracers, levels, width = dims
    c = part(strips, side_of(east, width), levels)
    return [(part(nu, t, levels) + (-c if east else c)) * part(ref, t, levels) for t in range(tracers)]


def side_lanes(packed, east, solved, lane, dims):
    tracers, levels, width = dims
    for t in range(tracers):
        j = t * width + side_of(east, width)
        packed = packed + jnp.where(lane // 2 == j, both_edges(part(solved, t, levels), j), 0.0)
    return packed


def side_rows(fresh, east, solved, row, level, dims):
    tracers, levels, width = dims
    for t in range(tracers):
        line = solved[pl.ds(t * levels + level, 1), :]
        fresh = fresh + jnp.where(row == t * width + side_of(east, width), line, 0.0)
    return fresh


def west_kernel(dims, strips, nu, weights, spread, edge_lanes, rows, guide, own, other, from_west, solved, incr, half_lanes, surface):
    tracers, levels, width = dims
    total = tracers * width
    lane = lanes_of(levels)
    terms = side_terms(from_west, False, strips, nu, dims)
    result = product(weights[...], jnp.concatenate(terms, axis=1))
    flux = increments(own[...], other[...], guide, tracers, width)
    incr[...] = flux
    for t in range(tracers):
        solved[t * levels:(t + 1) * levels, :] = result[:, t * 128:(t + 1) * 128]
    row = lax.broadcasted_iota(jnp.int32, (total, 128), 0)
    rows_lane = lax.broadcasted_iota(jnp.int32, (total, 128), 1)
    turned = pltpu.roll(flux, 1, 1, stride=2, stride_axis=0)
    turned = jnp.sum(jnp.where(rows_lane // 2 == row, turned, 0.0), axis=0, keepdims=True)
    half_lanes[...] = side_lanes(edge_lanes[...] + spread[...] * turned, False, solved, lane, dims)
    level = surface_level(levels)
    fresh = rows[...] + spread[pl.ds(level, 1), :] * flux
    surface[...] = side_rows(fresh, False, solved, row, level, dims)


def east_kernel(dims, strips, nu, weights, half_lanes, half_surface, from_west, from_east, solved, surface, *send_mer):
    tracers, levels, width = dims
    total = tracers * width
    lane = lanes_of(levels)
    result = product(weights[...], jnp.concatenate(side_terms(from_east, True, strips, nu, dims), axis=1))
    for t in range(tracers):
        solved[t * levels:(t + 1) * levels, :] = result[:, t * 128:(t + 1) * 128]
    packed = side_lanes(half_lanes[...], True, solved, lane, dims)
    place = lax.axis_index("mer")
    for r, ref in enumerate(send_mer):
        up = lax.rem(place + 1 + r, 2)
        message = packed
        for s, cells in enumerate((from_west, from_east)):
            for t in range(tracers):
                at = s * tracers + t
                moved = pltpu.roll(part(cells, t, levels), 2 * at + 2 * up, 1)
                message = jnp.where(lane == 2 * at + up, moved, message)
        ref[:levels // 2, :] = fold(message)
        ref[levels // 2:, :] = jnp.zeros((ref.shape[0] - levels // 2, 128), f32)
    row = lax.broadcasted_iota(jnp.int32, (total, 128), 0)
    surface[...] = side_rows(half_surface[...], True, solved, row, surface_level(levels), dims)


def meet_kernel(dims, mer_count, weights, own_mer, half_surface, from_west, from_east, *rest):
    tracers, levels, width = dims
    total = tracers * width
    rounds = len(rest) - 3
    recv_mer, (lanes, beyond, surface) = [ref[...] for ref in rest[:rounds]], rest[rounds:]
    lane = lanes_of(levels)
    edge = jnp.where(lane < 64, own_mer[...], 0.0)
    gain = jnp.where(lane < 64, pltpu.roll(own_mer[...], 64, 1), 0.0)
    here = gain * mer_halo(recv_mer, levels, mer_count)
    there = edge * mer_halo([pltpu.roll(value, 64, 1) for value in recv_mer], levels, mer_count)
    result = product(weights[...], jnp.concatenate([here, there], axis=1))
    lanes[...] = result[:, :128]
    beyond[...] = result[:, 128:]
    row = lax.broadcasted_iota(jnp.int32, (total, 128), 0)
    rows_lane = lax.broadcasted_iota(jnp.int32, (total, 128), 1)
    line = jnp.broadcast_to(lanes[pl.ds(surface_level(levels), 1), :], (total, 128))
    line = jnp.take_along_axis(line, 2 * row + (rows_lane == 0).astype(jnp.int32), axis=1)
    rim = jnp.logical_or(rows_lane == 127, rows_lane == 0)
    surface[:total, :] = half_surface[...] + jnp.where(rim, line, 0.0)
    surface[total:, :] = jnp.zeros((surface.shape[0] - total, 128), f32)
    level = surface_level(levels)
    for s, cells in enumerate((from_west, from_east)):
        for t in range(tracers):
            at = total + s * tracers + t
            surface[at:at + 1, :] = cells[pl.ds(t * levels + level, 1), :]


def again_kernel(dims, partial, strips, nu, weights, spread, west_solved, east_solved, lanes, incr, again, fresh):
    tracers, levels, width = dims
    lane = lanes_of(levels)
    rim = jnp.logical_or(lane == 127, lane == 0)
    for t in range(tracers):
        for x in range(width):
            j = t * width + x
            value = part(partial, j, levels) + spread[...] * incr[j:j + 1, :]
            value = value + jnp.where(rim, at_edges(lanes[...], j), 0.0)
            if x in (0, width - 1):
                value = value + part(west_solved if x == 0 else east_solved, t, levels)
            fresh[j * levels:(j + 1) * levels, :] = value

    def store(t, x, value):
        again[pl.ds((t * width + x) * levels, levels), :] = value

    column = lambda t, x: part(fresh, t * width + x, levels)
    strip = lambda k, x: part(strips, k * width + x, levels)
    interior(column, strip, nu, weights, store, dims)


def sides_kernel(dims, columns, strips, nu, weights, guide, own, other, from_west, from_east, edges, flux, inner_gain, outer_gain):
    tracers, levels, width = dims
    total = tracers * width
    lane = lanes_of(levels)
    flux[...] = increments(own[:total, :], other[:total, :], guide, tracers, width)
    extra = increments(own[total:, :], other[total:, :], guide, tracers, 1)
    at_level = lax.broadcasted_iota(jnp.int32, (levels, 128), 0) == surface_level(levels)
    terms, gains = [], []
    first = jnp.zeros((levels, 128), f32)
    later = jnp.zeros((levels, 128), f32)
    for s, ref in enumerate((from_west, from_east)):
        x = side_of(s == 1, width)
        c, d = (part(ref, 2 * tracers + k, levels) for k in range(2))
        own_c = part(strips, x, levels)
        for t in range(tracers):
            mine, beyond = part(columns, t * width + x, levels), part(ref, tracers + t, levels)
            west, east = (mine, beyond) if s == 1 else (beyond, mine)
            value = horizontal(part(ref, t, levels), east, west, c, d, part(nu, t, levels), lane)
            value = value + jnp.where(at_level, jnp.broadcast_to(extra[s * tracers + t:s * tracers + t + 1, :], value.shape), 0.0)
            terms.append(value)
            gain = part(nu, t, levels) + (-own_c if s == 1 else own_c)
            gains.append(gain)
            j = t * width + x
            here = lane // 2 == j
            packed = both_edges(d, j)
            first = jnp.where(here, part(nu, t, levels) + jnp.where(lane % 2 == 0, -packed, packed), first)
            later = jnp.where(here, both_edges(gain, j), later)
    inner_gain[...] = first
    outer_gain[...] = later
    result = product(weights[...], jnp.concatenate(terms, axis=1))
    result = product(weights[...], result * jnp.concatenate(gains, axis=1))
    for i in range(2 * tracers):
        edges[i * levels:(i + 1) * levels, :] = result[:, i * 128:(i + 1) * 128]


def last_kernel(dims, mer_count, partial, edges, incr, weights, spread, own_mer, beyond, inner_gain, outer_gain, *rest):
    tracers, levels, width = dims
    rounds = len(rest) - 3
    recv_mer, (out, done, sems) = [unfold(ref[:levels // 2, :]) for ref in rest[:rounds]], rest[rounds:]
    lane = lanes_of(levels)
    halo = mer_halo(recv_mer, levels, mer_count) + beyond[...]
    gain = jnp.where(lane < 64, pltpu.roll(own_mer[...], 64, 1), 0.0)
    lanes = product(weights[...], gain * halo)
    corner = jnp.zeros((levels, 128), f32)
    for value, north, inside in mer_sides(recv_mer, mer_count):
        for s in range(2):
            for t in range(tracers):
                j = t * width + side_of(s == 1, width)
                moved = pltpu.roll(value, 2 * (j - s * tracers - t) % 128, 1)
                corner = jnp.where(jnp.logical_and(lane == 2 * j + 1 - north, inside), moved, corner)
    corner = outer_gain[...] * product(weights[...], inner_gain[...] * corner)
    corner = product(weights[...], corner) + lanes
    rim = jnp.logical_or(lane == 127, lane == 0)
    copies = []
    for x in list(range(1, width - 1)) + [0, width - 1]:
        for t in range(tracers):
            j = t * width + x
            value = part(partial, j, levels) + spread[...] * incr[j:j + 1, :]
            value = value + jnp.where(rim, at_edges(corner if x in (0, width - 1) else lanes, j), 0.0)
            if x in (0, width - 1):
                value = value + part(edges, (0 if x == 0 else tracers) + t, levels)
            done[j] = value
            copy = pltpu.make_async_copy(done.at[j], out.at[t, :, x, :], sems.at[j])
            copy.start()
            copies.append(copy)
    for copy in copies:
        copy.wait()


VM = pl.BlockSpec(memory_space=pltpu.VMEM)
HB = pl.BlockSpec(memory_space=pltpu.HBM)


def call(body, name, in_specs, out_shape, flops, out_specs=None, scratch=(), touched=2 << 20):
    many = isinstance(out_shape, list)
    return pl.pallas_call(
        body,
        out_shape=out_shape,
        in_specs=in_specs,
        out_specs=out_specs or ([VM] * len(out_shape) if many else VM),
        scratch_shapes=scratch,
        name=name,
        cost_estimate=pl.CostEstimate(flops=flops, bytes_accessed=touched, transcendentals=0),
        compiler_params=pltpu.CompilerParams(vmem_limit_bytes=32 * 1024 * 1024),
    )


def on_device(state, flow, diffusion, column_solve, exchange_rate, block_map, ice_mask):
    _, tracers, levels, width, wide = state.shape
    mer_count, zon_count = lax.axis_size("mer"), lax.axis_size("zon")
    rounds = 1 if mer_count == 2 else 2
    dims = (tracers, levels, width)
    size, total = levels * width, tracers * width
    shape = lambda rows, dtype=f32: jax.ShapeDtypeStruct((rows, wide), dtype)
    message = shape((2 * tracers + 2) * levels)
    packed = shape(levels)
    folded = shape(levels // 2 + 16)
    kept = shape(tracers * size)
    halved = shape(tracers * levels)
    sided = shape(2 * tracers * levels)

    def swap_mer(pieces):
        return [lax.ppermute(piece, "mer", pairs(mer_count, r == 1)) for r, piece in enumerate(pieces)]

    def shift_zonal(piece, ahead):
        return lax.ppermute(piece, "zon", ring(zon_count, ahead))

    def widen(piece):
        return piece.astype(f32) * (1.0 / SCALE)

    def swap_fluid(piece):
        return lax.ppermute(piece, "fluid", [(0, 1), (1, 0)])

    params = (diffusion[0], column_solve[0], exchange_rate, block_map[None], ice_mask[None])
    in_hbm = [pltpu.with_memory_space_constraint(value, pltpu.HBM) for value in (state[0], flow[0]) + params]
    east_bound, west_bound, surface, frame, *params = call(
        functools.partial(pack_kernel, dims), "pack", [HB] * len(in_hbm),
        [message, message, shape(total), shape(2 * size)] + [jax.ShapeDtypeStruct(p.shape, p.dtype) for p in params], 1 << 20,
        scratch=[pltpu.VMEM((2, levels, width, wide), bf16),
                 pltpu.SemaphoreType.DMA((5 * tracers + 2 + len(params),))],
    )(*in_hbm)
    east_bound, west_bound = lax.optimization_barrier(((east_bound * SCALE).astype(jnp.float16), (west_bound * SCALE).astype(jnp.float16)))
    from_west = widen(shift_zonal(east_bound, 1))
    columns, own_mer, nu, weights, spread, guide = call(
        functools.partial(lanes_kernel, dims), "lanes", [VM] * 7,
        [kept, packed, shape(tracers * levels), jax.ShapeDtypeStruct((levels, 3 * levels), bf16), packed, shape(8)], 1 << 20,
    )(state.reshape(tracers * size, wide), frame, *params)
    recv_mer = swap_mer([own_mer] * rounds)
    other = swap_fluid(surface)
    from_east = shift_zonal(west_bound, -1)
    partial, strips, edge_lanes, rows = call(
        functools.partial(inner_kernel, dims), "inner", [VM] * 4, [kept, shape(2 * size), packed, shape(total)], 1 << 30,
    )(columns, frame, nu, weights)
    west_solved, incr, half_lanes, half_surface = call(
        functools.partial(west_kernel, dims), "west", [VM] * 10,
        [halved, shape(total), packed, shape(total)], 1 << 33,
    )(strips, nu, weights, spread, edge_lanes, rows, guide, surface, other, from_west)
    from_east, half_lanes = lax.optimization_barrier((from_east, half_lanes))
    from_east = widen(from_east)
    east_solved, half_surface, *send_mer = call(
        functools.partial(east_kernel, dims), "east", [VM] * 7, [halved, shape(total)] + [folded] * rounds, 1 << 26,
    )(strips, nu, weights, half_lanes, half_surface, from_west, from_east)
    recv_again = swap_mer(send_mer)
    lanes, beyond, fresh_surface = call(
        functools.partial(meet_kernel, dims, mer_count), "meet", [VM] * (5 + rounds), [packed, packed, shape(total + 8)], 1 << 33,
    )(weights, own_mer, half_surface, from_west, from_east, *recv_mer)
    fresh_other = swap_fluid(fresh_surface)
    again = call(
        functools.partial(again_kernel, dims), "again", [VM] * 9, kept, 1 << 10, touched=1 << 10, scratch=[pltpu.VMEM((tracers * size, wide), f32)],
    )(partial, strips, nu, weights, spread, west_solved, east_solved, lanes, incr)
    edges, flux, inner_gain, outer_gain = call(
        functools.partial(sides_kernel, dims), "sides", [VM] * 9, [sided, shape(total), packed, packed], 1 << 10, touched=1 << 10,
    )(columns, strips, nu, weights, guide, fresh_surface, fresh_other, from_west, from_east)
    done = call(
        functools.partial(last_kernel, dims, mer_count), "last", [VM] * (9 + rounds),
        jax.ShapeDtypeStruct(state.shape[1:], f32), 1 << 26,
        out_specs=pl.BlockSpec(memory_space=pl.ANY),
        scratch=[pltpu.VMEM((total, levels, wide), f32), pltpu.SemaphoreType.DMA((total,))],
    )(again, edges, flux, weights, spread, own_mer, beyond, inner_gain, outer_gain, *recv_again)
    return done[None]


def solution(mesh):
    return jax.shard_map(
        on_device,
        mesh=mesh,
        in_specs=(
            P("fluid", None, None, "zon", "mer"),
            P("fluid", None, None, "zon", "mer"),
            P("fluid", None, None),
            P("fluid", None, None),
            P("fluid", None),
            P("mer"),
            P("mer"),
        ),
        out_specs=P("fluid", None, None, "zon", "mer"),
        check_vma=False,
    )
```

```python
import functools

import jax
import jax.numpy as jnp
from jax import lax
from jax.experimental import pallas as pl
from jax.experimental.pallas import tpu as pltpu
from jax.sharding import PartitionSpec as P

f32, bf16 = jnp.float32, jnp.bfloat16


SCALE = 4096.0


def ring(count, ahead):
    return [(i, (i + ahead) % count) for i in range(count)]


def pairs(count, odd):
    if odd:
        return [(i, ((i + 1) ^ 1) - 1) for i in range(1, count - 1)] + [(0, count - 1), (count - 1, 0)]
    return [(i, i ^ 1) for i in range(count)]


def side_of(east, width):
    return width - 1 if east else 0


def surface_level(levels):
    return jnp.where(lax.axis_index("fluid") == 0, levels - 1, 0)


def lanes_of(levels):
    return lax.broadcasted_iota(jnp.int32, (levels, 128), 1)


def split(value):
    high = value.astype(bf16)
    return high, (value - high.astype(f32)).astype(bf16)


def product(weights, value):
    high, low = split(value)
    return jnp.dot(weights, jnp.concatenate([high, low, high], axis=0), preferred_element_type=f32)


def part(ref, index, levels):
    return ref[index * levels:(index + 1) * levels, :]


def fold(value):
    half = value.shape[0] // 2
    lane = lanes_of(half)
    return jnp.where(lane < 64, value[:half], pltpu.roll(value[half:], 64, 1))


def unfold(value):
    return jnp.concatenate([value, pltpu.roll(value, 64, 1)], axis=0)


def mer_sides(recv_mer, mer_count):
    place = lax.axis_index("mer")
    even = 1 - lax.rem(place, 2)
    for r, value in enumerate(recv_mer):
        north = even if r == 0 else 1 - even
        yield value, north, jnp.where(north == 1, place + 1 < mer_count, place > 0)


def mer_halo(recv_mer, levels, mer_count):
    lane = lanes_of(levels)
    total = jnp.zeros((levels, 128), f32)
    for value, north, inside in mer_sides(recv_mer, mer_count):
        keep = jnp.logical_and(jnp.logical_and(lane % 2 == 1 - north, lane < 64), inside)
        total = total + jnp.where(keep, pltpu.roll(value, jnp.where(north == 1, 127, 1), 1), 0.0)
    return total


def both_edges(cells, j):
    return pltpu.roll(cells, 2 * j + 1, 1)


def at_edges(packed, j):
    return pltpu.roll(packed, (127 - 2 * j) % 128, 1)


def increments(own, other, guide, tracers, per_tracer):
    is_atm = lax.axis_index("fluid") == 0
    pick = lambda row: jnp.broadcast_to(guide[row:row + 1, :].astype(jnp.int32), own.shape)
    atm = jnp.where(is_atm, own, other)
    ocean = jnp.where(is_atm, other, own)
    flux = (jnp.take_along_axis(atm, pick(0), axis=1) - ocean) * guide[2:3, :]
    returned = jnp.take_along_axis(flux, pick(1), axis=1)
    tracer = lax.broadcasted_iota(jnp.int32, own.shape, 0) // per_tracer % tracers
    scale = jnp.broadcast_to(guide[3:4, :], own.shape)
    for t in range(1, tracers):
        scale = jnp.where(tracer == t, guide[3 + t:4 + t, :], scale)
    return jnp.where(is_atm, -returned, flux) * scale


def fill_guide(guide, rate, block_map, ice_mask, tracers):
    blocks = block_map.shape[1]
    lane = lax.broadcasted_iota(jnp.int32, (1, 128), 1)
    wide = 128 // blocks
    block, within = lane // wide, lane % wide
    first = lax.axis_index("mer") * blocks
    mapped = jnp.zeros((1, 128), jnp.int32)
    returned = jnp.zeros((1, 128), jnp.int32)
    is_open = jnp.zeros((1, 128), jnp.int32)
    for b in range(blocks):
        above = block_map[:, b:b + 1] - first
        mapped = jnp.where(block == b, above, mapped)
        returned = jnp.where(block == above, b, returned)
        is_open = jnp.where(block == b, 1 - ice_mask[:, b:b + 1], is_open)
    guide[...] = jnp.zeros(guide.shape, f32)
    guide[0:1, :] = (mapped * wide + within).astype(f32)
    guide[1:2, :] = (returned * wide + within).astype(f32)
    guide[2:3, :] = is_open.astype(f32)
    for t in range(tracers):
        guide[3 + t:4 + t, :] = jnp.broadcast_to(rate[:, t:t + 1], (1, 128))


def horizontal(q, east, west, c, d, nu, lane):
    north = jnp.where(lane == 127, 0.0, pltpu.roll(q, 127, 1))
    south = jnp.where(lane == 0, 0.0, pltpu.roll(q, 1, 1))
    return q - c * (east - west) - d * (north - south) + nu * ((east + west) + (north + south) - 4.0 * q)


def interior(column, strip, nu, weights, store, dims):
    tracers, levels, width = dims
    lane = lanes_of(levels)
    zero = jnp.zeros((levels, 128), f32)
    for x in range(width):
        c, d = strip(0, x), strip(1, x)
        terms = []
        for t in range(tracers):
            west = zero if x == 0 else column(t, x - 1)
            east = zero if x == width - 1 else column(t, x + 1)
            terms.append(horizontal(column(t, x), east, west, c, d, part(nu, t, levels), lane))
        solved = product(weights[...], jnp.concatenate(terms, axis=1))
        for t in range(tracers):
            store(t, x, solved[:, t * 128:(t + 1) * 128])


def pack_kernel(dims, state, flow, *rest):
    tracers, levels, width = dims
    size = levels * width
    fixed = len(rest) - 7 >> 1
    east_bound, west_bound, surface, frame = rest[fixed:fixed + 4]
    raw, inner, sems = rest[2 * fixed + 4:]
    level = surface_level(levels)
    wait_flow, copies = [], []
    for k in range(2):
        wait_flow.append(pltpu.make_async_copy(flow.at[k], raw.at[k], sems.at[k]))
    for i in range(fixed):
        copies.append(pltpu.make_async_copy(rest[i], rest[fixed + 4 + i], sems.at[2 + len(copies)]))
    sides = ((east_bound, width - 1, width - 2), (west_bound, 0, 1))
    for s, (ref, edge, second) in enumerate(sides):
        for t in range(tracers):
            target = ref.at[pl.ds(t * levels, levels), :]
            copies.append(pltpu.make_async_copy(state.at[t, :, edge, :], target, sems.at[2 + len(copies)]))
            copies.append(pltpu.make_async_copy(state.at[t, :, second, :], inner.at[s * tracers + t], sems.at[2 + len(copies)]))
    for t in range(tracers):
        target = surface.at[pl.ds(t * width, width), :]
        copies.append(pltpu.make_async_copy(state.at[t, level], target, sems.at[2 + len(copies)]))
    for copy in wait_flow + copies:
        copy.start()
    for copy in copies:
        copy.wait()
    diffusion = rest[fixed + 4]
    lane = lanes_of(levels)
    row = lax.broadcasted_iota(jnp.int32, (levels, 128), 0)
    nu = [jnp.transpose(jnp.broadcast_to(diffusion[t:t + 1, :], (128, levels))) for t in range(tracers)]
    for k in range(2):
        wait_flow[k].wait()
        frame[k * size:(k + 1) * size, :] = raw[k].reshape(size, 128).astype(f32) * 0.5
    for s, (ref, edge, _) in enumerate(sides):
        c, d = (frame[pl.ds(k * size + edge, levels, stride=width), :] for k in range(2))
        toward = c if s == 0 else -c
        for t in range(tracers):
            q = ref[t * levels:(t + 1) * levels, :]
            north = jnp.where(lane == 127, 0.0, pltpu.roll(q, 127, 1))
            south = jnp.where(lane == 0, 0.0, pltpu.roll(q, 1, 1))
            value = (1.0 - 4.0 * nu[t]) * q + (nu[t] + toward) * inner[s * tracers + t] + (nu[t] - d) * north + (nu[t] + d) * south
            ref[(tracers + t) * levels:(tracers + t + 1) * levels, :] = value
        ref[2 * tracers * levels:(2 * tracers + 1) * levels, :] = c
        rims = jnp.where(lane == row, d[:, 127:128], 0.0) + jnp.where(lane == row + 64, d[:, 0:1], 0.0)
        ref[(2 * tracers + 1) * levels:, :] = jnp.broadcast_to(jnp.sum(rims, axis=0, keepdims=True), (16, 128))


def lanes_kernel(dims, cells, frame, diffusion, solve, rate, block_map, ice_mask, columns, send_mer, nu, weights, spread, guide):
    tracers, levels, width = dims
    size = levels * width
    lane = lanes_of(levels)
    packed = jnp.zeros((levels, 128), f32)
    merid = jnp.zeros((levels, 128), f32)
    gain = jnp.zeros((levels, 128), f32)
    for x in range(width):
        strip = frame[pl.ds(size + x, levels, stride=width), :]
        merid = jnp.where(lane // 2 == x, both_edges(strip, x), merid)
    for t in range(tracers):
        for x in range(width):
            j = t * width + x
            value = cells[pl.ds(t * size + x, levels, stride=width), :]
            columns[j * levels:(j + 1) * levels, :] = value
            packed = jnp.where(lane // 2 == j, both_edges(value, j), packed)
        mine = jnp.transpose(jnp.broadcast_to(diffusion[t:t + 1, :], (128, levels)))
        nu[t * levels:(t + 1) * levels, :] = mine
        turned = merid if t == 0 else pltpu.roll(merid, 2 * t * width, 1)
        mine = mine + jnp.where(lane % 2 == 0, -turned, turned)
        gain = jnp.where(lane // (2 * width) == t, mine, gain)
    send_mer[...] = jnp.where(lane < 64, packed, pltpu.roll(gain, 64, 1))
    high, low = split(solve[...])
    weights[...] = jnp.concatenate([high, high, low], axis=1)
    at_level = lax.broadcasted_iota(jnp.int32, (levels, levels), 1) == surface_level(levels)
    fill_guide(guide, rate, block_map, ice_mask, tracers)
    spread[...] = jnp.broadcast_to(jnp.sum(jnp.where(at_level, solve[...], 0.0), axis=1, keepdims=True), (levels, 128))


def inner_kernel(dims, columns, frame, nu, weights, partial, strips, edge_lanes, rows):
    tracers, levels, width = dims
    lane = lanes_of(levels)
    for k in range(2):
        for x in range(width):
            value = frame[pl.ds((k * levels * width) + x, levels, stride=width), :]
            strips[(k * width + x) * levels:(k * width + x + 1) * levels, :] = value

    def store(t, x, value):
        j = t * width + x
        partial[j * levels:(j + 1) * levels, :] = value

    column = lambda t, x: part(columns, t * width + x, levels)
    strip = lambda k, x: part(strips, k * width + x, levels)
    interior(column, strip, nu, weights, store, dims)
    packed = jnp.zeros((levels, 128), f32)
    for j in range(tracers * width):
        packed = jnp.where(lane // 2 == j, both_edges(part(partial, j, levels), j), packed)
    edge_lanes[...] = packed
    rows[...] = partial[pl.ds(surface_level(levels), tracers * width, stride=levels), :]


def side_terms(ref, east, strips, nu, dims):
    tracers, levels, width = dims
    c = part(strips, side_of(east, width), levels)
    return [(part(nu, t, levels) + (-c if east else c)) * part(ref, t, levels) for t in range(tracers)]


def side_lanes(packed, east, solved, lane, dims):
    tracers, levels, width = dims
    for t in range(tracers):
        j = t * width + side_of(east, width)
        packed = packed + jnp.where(lane // 2 == j, both_edges(part(solved, t, levels), j), 0.0)
    return packed


def side_rows(fresh, east, solved, row, level, dims):
    tracers, levels, width = dims
    for t in range(tracers):
        line = solved[pl.ds(t * levels + level, 1), :]
        fresh = fresh + jnp.where(row == t * width + side_of(east, width), line, 0.0)
    return fresh


def west_kernel(dims, strips, nu, weights, spread, edge_lanes, rows, guide, own, other, from_west, solved, incr, half_lanes, surface):
    tracers, levels, width = dims
    total = tracers * width
    lane = lanes_of(levels)
    terms = side_terms(from_west, False, strips, nu, dims)
    result = product(weights[...], jnp.concatenate(terms, axis=1))
    flux = increments(own[...], other[...], guide, tracers, width)
    incr[...] = flux
    for t in range(tracers):
        solved[t * levels:(t + 1) * levels, :] = result[:, t * 128:(t + 1) * 128]
    row = lax.broadcasted_iota(jnp.int32, (total, 128), 0)
    rows_lane = lax.broadcasted_iota(jnp.int32, (total, 128), 1)
    turned = pltpu.roll(flux, 1, 1, stride=2, stride_axis=0)
    turned = jnp.sum(jnp.where(rows_lane // 2 == row, turned, 0.0), axis=0, keepdims=True)
    half_lanes[...] = side_lanes(edge_lanes[...] + spread[...] * turned, False, solved, lane, dims)
    level = surface_level(levels)
    fresh = rows[...] + spread[pl.ds(level, 1), :] * flux
    surface[...] = side_rows(fresh, False, solved, row, level, dims)


def east_kernel(dims, strips, nu, weights, half_lanes, half_surface, from_west, from_east, solved, surface, *send_mer):
    tracers, levels, width = dims
    total = tracers * width
    lane = lanes_of(levels)
    result = product(weights[...], jnp.concatenate(side_terms(from_east, True, strips, nu, dims), axis=1))
    for t in range(tracers):
        solved[t * levels:(t + 1) * levels, :] = result[:, t * 128:(t + 1) * 128]
    packed = side_lanes(half_lanes[...], True, solved, lane, dims)
    place = lax.axis_index("mer")
    for r, ref in enumerate(send_mer):
        up = lax.rem(place + 1 + r, 2)
        message = packed
        for s, cells in enumerate((from_west, from_east)):
            for t in range(tracers):
                at = s * tracers + t
                moved = pltpu.roll(part(cells, t, levels), 2 * at + 2 * up, 1)
                message = jnp.where(lane == 2 * at + up, moved, message)
        ref[:levels // 2, :] = fold(message)
        ref[levels // 2:, :] = jnp.zeros((ref.shape[0] - levels // 2, 128), f32)
    row = lax.broadcasted_iota(jnp.int32, (total, 128), 0)
    surface[...] = side_rows(half_surface[...], True, solved, row, surface_level(levels), dims)


def meet_kernel(dims, mer_count, weights, own_mer, half_surface, from_west, from_east, *rest):
    tracers, levels, width = dims
    total = tracers * width
    rounds = len(rest) - 3
    recv_mer, (lanes, beyond, surface) = [ref[...] for ref in rest[:rounds]], rest[rounds:]
    lane = lanes_of(levels)
    edge = jnp.where(lane < 64, own_mer[...], 0.0)
    gain = jnp.where(lane < 64, pltpu.roll(own_mer[...], 64, 1), 0.0)
    here = gain * mer_halo(recv_mer, levels, mer_count)
    there = edge * mer_halo([pltpu.roll(value, 64, 1) for value in recv_mer], levels, mer_count)
    result = product(weights[...], jnp.concatenate([here, there], axis=1))
    lanes[...] = result[:, :128]
    beyond[...] = result[:, 128:]
    row = lax.broadcasted_iota(jnp.int32, (total, 128), 0)
    rows_lane = lax.broadcasted_iota(jnp.int32, (total, 128), 1)
    line = jnp.broadcast_to(lanes[pl.ds(surface_level(levels), 1), :], (total, 128))
    line = jnp.take_along_axis(line, 2 * row + (rows_lane == 0).astype(jnp.int32), axis=1)
    rim = jnp.logical_or(rows_lane == 127, rows_lane == 0)
    surface[:total, :] = half_surface[...] + jnp.where(rim, line, 0.0)
    surface[total:, :] = jnp.zeros((surface.shape[0] - total, 128), f32)
    level = surface_level(levels)
    for s, cells in enumerate((from_west, from_east)):
        for t in range(tracers):
            at = total + s * tracers + t
            surface[at:at + 1, :] = cells[pl.ds(t * levels + level, 1), :]


def again_kernel(dims, partial, strips, nu, weights, spread, west_solved, east_solved, lanes, incr, again, fresh):
    tracers, levels, width = dims
    lane = lanes_of(levels)
    rim = jnp.logical_or(lane == 127, lane == 0)
    for t in range(tracers):
        for x in range(width):
            j = t * width + x
            value = part(partial, j, levels) + spread[...] * incr[j:j + 1, :]
            value = value + jnp.where(rim, at_edges(lanes[...], j), 0.0)
            if x in (0, width - 1):
                value = value + part(west_solved if x == 0 else east_solved, t, levels)
            fresh[j * levels:(j + 1) * levels, :] = value

    def store(t, x, value):
        again[pl.ds((t * width + x) * levels, levels), :] = value

    column = lambda t, x: part(fresh, t * width + x, levels)
    strip = lambda k, x: part(strips, k * width + x, levels)
    interior(column, strip, nu, weights, store, dims)


def sides_kernel(dims, columns, strips, nu, weights, guide, own, other, from_west, from_east, edges, flux, inner_gain, outer_gain):
    tracers, levels, width = dims
    total = tracers * width
    lane = lanes_of(levels)
    flux[...] = increments(own[:total, :], other[:total, :], guide, tracers, width)
    extra = increments(own[total:, :], other[total:, :], guide, tracers, 1)
    level_row = lax.broadcasted_iota(jnp.int32, (levels, 128), 0)
    at_level = level_row == surface_level(levels)
    terms, gains = [], []
    first = jnp.zeros((levels, 128), f32)
    later = jnp.zeros((levels, 128), f32)
    for s, ref in enumerate((from_west, from_east)):
        x = side_of(s == 1, width)
        c = part(ref, 2 * tracers, levels)
        rims = ref[(2 * tracers + 1) * levels:(2 * tracers + 1) * levels + 1, :]
        d_north = jnp.sum(jnp.where(lane == level_row, rims, 0.0), axis=1, keepdims=True)
        d_south = jnp.sum(jnp.where(lane == level_row + 64, rims, 0.0), axis=1, keepdims=True)
        own_c = part(strips, x, levels)
        for t in range(tracers):
            mine = part(columns, t * width + x, levels)
            value = part(ref, tracers + t, levels) + (part(nu, t, levels) + (c if s == 1 else -c)) * mine
            value = value + jnp.where(at_level, jnp.broadcast_to(extra[s * tracers + t:s * tracers + t + 1, :], value.shape), 0.0)
            terms.append(value)
            gain = part(nu, t, levels) + (-own_c if s == 1 else own_c)
            gains.append(gain)
            here = lane // 2 == t * width + x
            first = jnp.where(here, part(nu, t, levels) + jnp.where(lane % 2 == 0, -d_north, d_south), first)
            later = jnp.where(here, both_edges(gain, t * width + x), later)
    inner_gain[...] = first
    outer_gain[...] = later
    result = product(weights[...], jnp.concatenate(terms, axis=1))
    result = product(weights[...], result * jnp.concatenate(gains, axis=1))
    for i in range(2 * tracers):
        edges[i * levels:(i + 1) * levels, :] = result[:, i * 128:(i + 1) * 128]


def last_kernel(dims, mer_count, partial, edges, incr, weights, spread, own_mer, beyond, inner_gain, outer_gain, *rest):
    tracers, levels, width = dims
    rounds = len(rest) - 3
    recv_mer, (out, done, sems) = [unfold(ref[:levels // 2, :]) for ref in rest[:rounds]], rest[rounds:]
    lane = lanes_of(levels)
    halo = mer_halo(recv_mer, levels, mer_count) + beyond[...]
    gain = jnp.where(lane < 64, pltpu.roll(own_mer[...], 64, 1), 0.0)
    lanes = product(weights[...], gain * halo)
    corner = jnp.zeros((levels, 128), f32)
    for value, north, inside in mer_sides(recv_mer, mer_count):
        for s in range(2):
            for t in range(tracers):
                j = t * width + side_of(s == 1, width)
                moved = pltpu.roll(value, 2 * (j - s * tracers - t) % 128, 1)
                corner = jnp.where(jnp.logical_and(lane == 2 * j + 1 - north, inside), moved, corner)
    corner = outer_gain[...] * product(weights[...], inner_gain[...] * corner)
    corner = product(weights[...], corner) + lanes
    rim = jnp.logical_or(lane == 127, lane == 0)
    copies = []
    for x in list(range(1, width - 1)) + [0, width - 1]:
        for t in range(tracers):
            j = t * width + x
            value = part(partial, j, levels) + spread[...] * incr[j:j + 1, :]
            value = value + jnp.where(rim, at_edges(corner if x in (0, width - 1) else lanes, j), 0.0)
            if x in (0, width - 1):
                value = value + part(edges, (0 if x == 0 else tracers) + t, levels)
            done[j] = value
            copy = pltpu.make_async_copy(done.at[j], out.at[t, :, x, :], sems.at[j])
            copy.start()
            copies.append(copy)
    for copy in copies:
        copy.wait()


VM = pl.BlockSpec(memory_space=pltpu.VMEM)
HB = pl.BlockSpec(memory_space=pltpu.HBM)


def call(body, name, in_specs, out_shape, flops, out_specs=None, scratch=(), touched=2 << 20):
    many = isinstance(out_shape, list)
    return pl.pallas_call(
        body,
        out_shape=out_shape,
        in_specs=in_specs,
        out_specs=out_specs or ([VM] * len(out_shape) if many else VM),
        scratch_shapes=scratch,
        name=name,
        cost_estimate=pl.CostEstimate(flops=flops, bytes_accessed=touched, transcendentals=0),
        compiler_params=pltpu.CompilerParams(vmem_limit_bytes=32 * 1024 * 1024),
    )


def on_device(state, flow, diffusion, column_solve, exchange_rate, block_map, ice_mask):
    _, tracers, levels, width, wide = state.shape
    mer_count, zon_count = lax.axis_size("mer"), lax.axis_size("zon")
    rounds = 1 if mer_count == 2 else 2
    dims = (tracers, levels, width)
    size, total = levels * width, tracers * width
    shape = lambda rows, dtype=f32: jax.ShapeDtypeStruct((rows, wide), dtype)
    message = shape((2 * tracers + 1) * levels + 16)
    packed = shape(levels)
    folded = shape(levels // 2 + 16)
    kept = shape(tracers * size)
    halved = shape(tracers * levels)
    sided = shape(2 * tracers * levels)

    def swap_mer(pieces):
        return [lax.ppermute(piece, "mer", pairs(mer_count, r == 1)) for r, piece in enumerate(pieces)]

    def shift_zonal(piece, ahead):
        return lax.ppermute(piece, "zon", ring(zon_count, ahead))

    def widen(piece):
        return piece.astype(f32) * (1.0 / SCALE)

    def swap_fluid(piece):
        return lax.ppermute(piece, "fluid", [(0, 1), (1, 0)])

    params = (diffusion[0], column_solve[0], exchange_rate, block_map[None], ice_mask[None])
    in_hbm = [pltpu.with_memory_space_constraint(value, pltpu.HBM) for value in (state[0], flow[0]) + params]
    east_bound, west_bound, surface, frame, *params = call(
        functools.partial(pack_kernel, dims), "pack", [HB] * len(in_hbm),
        [message, message, shape(total), shape(2 * size)] + [jax.ShapeDtypeStruct(p.shape, p.dtype) for p in params], 1 << 20,
        scratch=[pltpu.VMEM((2, levels, width, wide), bf16), pltpu.VMEM((2 * tracers, levels, wide), f32),
                 pltpu.SemaphoreType.DMA((5 * tracers + 2 + len(params),))],
    )(*in_hbm)
    east_bound, west_bound = lax.optimization_barrier(((east_bound * SCALE).astype(jnp.float16), (west_bound * SCALE).astype(jnp.float16)))
    from_west = widen(shift_zonal(east_bound, 1))
    columns, own_mer, nu, weights, spread, guide = call(
        functools.partial(lanes_kernel, dims), "lanes", [VM] * 7,
        [kept, packed, shape(tracers * levels), jax.ShapeDtypeStruct((levels, 3 * levels), bf16), packed, shape(8)], 1 << 20,
    )(state.reshape(tracers * size, wide), frame, *params)
    recv_mer = swap_mer([own_mer] * rounds)
    other = swap_fluid(surface)
    from_east = shift_zonal(west_bound, -1)
    partial, strips, edge_lanes, rows = call(
        functools.partial(inner_kernel, dims), "inner", [VM] * 4, [kept, shape(2 * size), packed, shape(total)], 1 << 30,
    )(columns, frame, nu, weights)
    west_solved, incr, half_lanes, half_surface = call(
        functools.partial(west_kernel, dims), "west", [VM] * 10,
        [halved, shape(total), packed, shape(total)], 1 << 33,
    )(strips, nu, weights, spread, edge_lanes, rows, guide, surface, other, from_west)
    from_east, half_lanes = lax.optimization_barrier((from_east, half_lanes))
    from_east = widen(from_east)
    east_solved, half_surface, *send_mer = call(
        functools.partial(east_kernel, dims), "east", [VM] * 7, [halved, shape(total)] + [folded] * rounds, 1 << 26,
    )(strips, nu, weights, half_lanes, half_surface, from_west, from_east)
    recv_again = swap_mer(send_mer)
    lanes, beyond, fresh_surface = call(
        functools.partial(meet_kernel, dims, mer_count), "meet", [VM] * (5 + rounds), [packed, packed, shape(total + 8)], 1 << 33,
    )(weights, own_mer, half_surface, from_west, from_east, *recv_mer)
    fresh_other = swap_fluid(fresh_surface)
    again = call(
        functools.partial(again_kernel, dims), "again", [VM] * 9, kept, 1 << 10, touched=1 << 10, scratch=[pltpu.VMEM((tracers * size, wide), f32)],
    )(partial, strips, nu, weights, spread, west_solved, east_solved, lanes, incr)
    edges, flux, inner_gain, outer_gain = call(
        functools.partial(sides_kernel, dims), "sides", [VM] * 9, [sided, shape(total), packed, packed], 1 << 10, touched=1 << 10,
    )(columns, strips, nu, weights, guide, fresh_surface, fresh_other, from_west, from_east)
    done = call(
        functools.partial(last_kernel, dims, mer_count), "last", [VM] * (9 + rounds),
        jax.ShapeDtypeStruct(state.shape[1:], f32), 1 << 26,
        out_specs=pl.BlockSpec(memory_space=pl.ANY),
        scratch=[pltpu.VMEM((total, levels, wide), f32), pltpu.SemaphoreType.DMA((total,))],
    )(again, edges, flux, weights, spread, own_mer, beyond, inner_gain, outer_gain, *recv_again)
    return done[None]


def solution(mesh):
    return jax.shard_map(
        on_device,
        mesh=mesh,
        in_specs=(
            P("fluid", None, None, "zon", "mer"),
            P("fluid", None, None, "zon", "mer"),
            P("fluid", None, None),
            P("fluid", None, None),
            P("fluid", None),
            P("mer"),
            P("mer"),
        ),
        out_specs=P("fluid", None, None, "zon", "mer"),
        check_vma=False,
    )
```

```python
import functools

import jax
import jax.numpy as jnp
from jax import lax
from jax.experimental import pallas as pl
from jax.experimental.pallas import tpu as pltpu
from jax.sharding import PartitionSpec as P

f32, bf16 = jnp.float32, jnp.bfloat16


SCALE = 8192.0


def ring(count, ahead):
    return [(i, (i + ahead) % count) for i in range(count)]


def pairs(count, odd):
    if odd:
        return [(i, ((i + 1) ^ 1) - 1) for i in range(1, count - 1)] + [(0, count - 1), (count - 1, 0)]
    return [(i, i ^ 1) for i in range(count)]


def side_of(east, width):
    return width - 1 if east else 0


def surface_level(levels):
    return jnp.where(lax.axis_index("fluid") == 0, levels - 1, 0)


def lanes_of(levels):
    return lax.broadcasted_iota(jnp.int32, (levels, 128), 1)


def split(value):
    high = value.astype(bf16)
    return high, (value - high.astype(f32)).astype(bf16)


def product(weights, value):
    high, low = split(value)
    return jnp.dot(weights, jnp.concatenate([high, low, high], axis=0), preferred_element_type=f32)


def part(ref, index, levels):
    return ref[index * levels:(index + 1) * levels, :]


def fold(value):
    half = value.shape[0] // 2
    lane = lanes_of(half)
    return jnp.where(lane < 64, value[:half], pltpu.roll(value[half:], 64, 1))


def unfold(value):
    return jnp.concatenate([value, pltpu.roll(value, 64, 1)], axis=0)


def mer_sides(recv_mer, mer_count):
    place = lax.axis_index("mer")
    even = 1 - lax.rem(place, 2)
    for r, value in enumerate(recv_mer):
        north = even if r == 0 else 1 - even
        yield value, north, jnp.where(north == 1, place + 1 < mer_count, place > 0)


def mer_halo(recv_mer, levels, mer_count):
    lane = lanes_of(levels)
    total = jnp.zeros((levels, 128), f32)
    for value, north, inside in mer_sides(recv_mer, mer_count):
        keep = jnp.logical_and(jnp.logical_and(lane % 2 == 1 - north, lane < 64), inside)
        total = total + jnp.where(keep, pltpu.roll(value, jnp.where(north == 1, 127, 1), 1), 0.0)
    return total


def both_edges(cells, j):
    return pltpu.roll(cells, 2 * j + 1, 1)


def at_edges(packed, j):
    return pltpu.roll(packed, (127 - 2 * j) % 128, 1)


def increments(own, other, guide, tracers, per_tracer):
    is_atm = lax.axis_index("fluid") == 0
    pick = lambda row: jnp.broadcast_to(guide[row:row + 1, :].astype(jnp.int32), own.shape)
    atm = jnp.where(is_atm, own, other)
    ocean = jnp.where(is_atm, other, own)
    flux = (jnp.take_along_axis(atm, pick(0), axis=1) - ocean) * guide[2:3, :]
    returned = jnp.take_along_axis(flux, pick(1), axis=1)
    tracer = lax.broadcasted_iota(jnp.int32, own.shape, 0) // per_tracer % tracers
    scale = jnp.broadcast_to(guide[3:4, :], own.shape)
    for t in range(1, tracers):
        scale = jnp.where(tracer == t, guide[3 + t:4 + t, :], scale)
    return jnp.where(is_atm, -returned, flux) * scale


def fill_guide(guide, rate, block_map, ice_mask, tracers):
    blocks = block_map.shape[1]
    lane = lax.broadcasted_iota(jnp.int32, (1, 128), 1)
    wide = 128 // blocks
    block, within = lane // wide, lane % wide
    first = lax.axis_index("mer") * blocks
    mapped = jnp.zeros((1, 128), jnp.int32)
    returned = jnp.zeros((1, 128), jnp.int32)
    is_open = jnp.zeros((1, 128), jnp.int32)
    for b in range(blocks):
        above = block_map[:, b:b + 1] - first
        mapped = jnp.where(block == b, above, mapped)
        returned = jnp.where(block == above, b, returned)
        is_open = jnp.where(block == b, 1 - ice_mask[:, b:b + 1], is_open)
    guide[...] = jnp.zeros(guide.shape, f32)
    guide[0:1, :] = (mapped * wide + within).astype(f32)
    guide[1:2, :] = (returned * wide + within).astype(f32)
    guide[2:3, :] = is_open.astype(f32)
    for t in range(tracers):
        guide[3 + t:4 + t, :] = jnp.broadcast_to(rate[:, t:t + 1], (1, 128))


def horizontal(q, east, west, c, d, nu, lane):
    north = jnp.where(lane == 127, 0.0, pltpu.roll(q, 127, 1))
    south = jnp.where(lane == 0, 0.0, pltpu.roll(q, 1, 1))
    return q - c * (east - west) - d * (north - south) + nu * ((east + west) + (north + south) - 4.0 * q)


def interior(column, strip, nu, weights, store, dims):
    tracers, levels, width = dims
    lane = lanes_of(levels)
    zero = jnp.zeros((levels, 128), f32)
    for x in range(width):
        c, d = strip(0, x), strip(1, x)
        terms = []
        for t in range(tracers):
            west = zero if x == 0 else column(t, x - 1)
            east = zero if x == width - 1 else column(t, x + 1)
            terms.append(horizontal(column(t, x), east, west, c, d, part(nu, t, levels), lane))
        solved = product(weights[...], jnp.concatenate(terms, axis=1))
        for t in range(tracers):
            store(t, x, solved[:, t * 128:(t + 1) * 128])


def pack_kernel(dims, state, flow, *rest):
    tracers, levels, width = dims
    size = levels * width
    fixed = len(rest) - 6 >> 1
    east_bound, west_bound, surface, frame = rest[fixed:fixed + 4]
    raw, sems = rest[2 * fixed + 4:]
    level = surface_level(levels)
    transfers = [(flow.at[k], raw.at[k]) for k in range(2)]
    for ref, places in ((east_bound, (width - 1, width - 2)), (west_bound, (0, 1))):
        for i, x in enumerate(places):
            transfers.append((state.at[:, :, x, :], ref.at[pl.ds(i * tracers, tracers)]))
    transfers.append((state.at[:, level], surface))
    transfers += [(rest[i], rest[fixed + 4 + i]) for i in range(fixed)]
    copies = [pltpu.make_async_copy(source, target, sems.at[i]) for i, (source, target) in enumerate(transfers)]
    for copy in copies:
        copy.start()
    wait_flow, copies = copies[:2], copies[2:]
    for k, copy in enumerate(wait_flow):
        copy.wait()
        frame[k * size:(k + 1) * size, :] = raw[k].reshape(size, 128).astype(f32) * 0.5
        for ref, x in ((east_bound, width - 1), (west_bound, 0)):
            strip = frame[pl.ds(k * size + x, levels, stride=width), :]
            ref[2 * tracers + k] = strip
    for copy in copies:
        copy.wait()


def lanes_kernel(dims, cells, frame, diffusion, solve, rate, block_map, ice_mask, columns, send_mer, nu, weights, spread, guide):
    tracers, levels, width = dims
    size = levels * width
    lane = lanes_of(levels)
    packed = jnp.zeros((levels, 128), f32)
    merid = jnp.zeros((levels, 128), f32)
    gain = jnp.zeros((levels, 128), f32)
    for x in range(width):
        strip = frame[pl.ds(size + x, levels, stride=width), :]
        merid = jnp.where(lane // 2 == x, both_edges(strip, x), merid)
    for t in range(tracers):
        for x in range(width):
            j = t * width + x
            value = cells[pl.ds(t * size + x, levels, stride=width), :]
            columns[j * levels:(j + 1) * levels, :] = value
            packed = jnp.where(lane // 2 == j, both_edges(value, j), packed)
        mine = jnp.transpose(jnp.broadcast_to(diffusion[t:t + 1, :], (128, levels)))
        nu[t * levels:(t + 1) * levels, :] = mine
        turned = merid if t == 0 else pltpu.roll(merid, 2 * t * width, 1)
        mine = mine + jnp.where(lane % 2 == 0, -turned, turned)
        gain = jnp.where(lane // (2 * width) == t, mine, gain)
    send_mer[...] = jnp.where(lane < 64, packed, pltpu.roll(gain, 64, 1))
    high, low = split(solve[...])
    weights[...] = jnp.concatenate([high, high, low], axis=1)
    at_level = lax.broadcasted_iota(jnp.int32, (levels, levels), 1) == surface_level(levels)
    fill_guide(guide, rate, block_map, ice_mask, tracers)
    spread[...] = jnp.broadcast_to(jnp.sum(jnp.where(at_level, solve[...], 0.0), axis=1, keepdims=True), (levels, 128))


def inner_kernel(dims, columns, frame, nu, weights, guide, own, other, partial, strips, edge_lanes, rows, incr):
    tracers, levels, width = dims
    lane = lanes_of(levels)
    for k in range(2):
        for x in range(width):
            value = frame[pl.ds((k * levels * width) + x, levels, stride=width), :]
            strips[(k * width + x) * levels:(k * width + x + 1) * levels, :] = value

    def store(t, x, value):
        j = t * width + x
        partial[j * levels:(j + 1) * levels, :] = value

    column = lambda t, x: part(columns, t * width + x, levels)
    strip = lambda k, x: part(strips, k * width + x, levels)
    interior(column, strip, nu, weights, store, dims)
    packed = jnp.zeros((levels, 128), f32)
    for j in range(tracers * width):
        packed = jnp.where(lane // 2 == j, both_edges(part(partial, j, levels), j), packed)
    edge_lanes[...] = packed
    rows[...] = partial[pl.ds(surface_level(levels), tracers * width, stride=levels), :]
    incr[...] = increments(own[...], other[...], guide, tracers, width)


def side_terms(ref, east, strips, nu, dims):
    tracers, levels, width = dims
    c = part(strips, side_of(east, width), levels)
    return [(part(nu, t, levels) + (-c if east else c)) * part(ref, t, levels) for t in range(tracers)]


def side_lanes(packed, east, solved, lane, dims):
    tracers, levels, width = dims
    for t in range(tracers):
        j = t * width + side_of(east, width)
        packed = packed + jnp.where(lane // 2 == j, both_edges(part(solved, t, levels), j), 0.0)
    return packed


def side_rows(fresh, east, solved, row, level, dims):
    tracers, levels, width = dims
    for t in range(tracers):
        line = solved[pl.ds(t * levels + level, 1), :]
        fresh = fresh + jnp.where(row == t * width + side_of(east, width), line, 0.0)
    return fresh


def west_kernel(dims, strips, nu, weights, spread, edge_lanes, rows, incr, from_west, solved, half_lanes, surface):
    tracers, levels, width = dims
    total = tracers * width
    lane = lanes_of(levels)
    terms = side_terms(from_west, False, strips, nu, dims)
    result = product(weights[...], jnp.concatenate(terms, axis=1))
    flux = incr[...]
    for t in range(tracers):
        solved[t * levels:(t + 1) * levels, :] = result[:, t * 128:(t + 1) * 128]
    row = lax.broadcasted_iota(jnp.int32, (total, 128), 0)
    rows_lane = lax.broadcasted_iota(jnp.int32, (total, 128), 1)
    turned = pltpu.roll(flux, 1, 1, stride=2, stride_axis=0)
    turned = jnp.sum(jnp.where(rows_lane // 2 == row, turned, 0.0), axis=0, keepdims=True)
    half_lanes[...] = side_lanes(edge_lanes[...] + spread[...] * turned, False, solved, lane, dims)
    level = surface_level(levels)
    fresh = rows[...] + spread[pl.ds(level, 1), :] * flux
    surface[...] = side_rows(fresh, False, solved, row, level, dims)


def east_kernel(dims, strips, nu, weights, half_lanes, half_surface, from_west, from_east, solved, surface, *send_mer):
    tracers, levels, width = dims
    total = tracers * width
    lane = lanes_of(levels)
    result = product(weights[...], jnp.concatenate(side_terms(from_east, True, strips, nu, dims), axis=1))
    for t in range(tracers):
        solved[t * levels:(t + 1) * levels, :] = result[:, t * 128:(t + 1) * 128]
    packed = side_lanes(half_lanes[...], True, solved, lane, dims)
    place = lax.axis_index("mer")
    for r, ref in enumerate(send_mer):
        up = lax.rem(place + 1 + r, 2)
        message = packed
        for s, cells in enumerate((from_west, from_east)):
            for t in range(tracers):
                at = s * tracers + t
                moved = pltpu.roll(part(cells, t, levels), 2 * at + 2 * up, 1)
                message = jnp.where(lane == 2 * at + up, moved, message)
        ref[:levels // 2, :] = fold(message)
        ref[levels // 2:, :] = jnp.zeros((ref.shape[0] - levels // 2, 128), f32)
    row = lax.broadcasted_iota(jnp.int32, (total, 128), 0)
    surface[...] = side_rows(half_surface[...], True, solved, row, surface_level(levels), dims)


def meet_kernel(dims, mer_count, weights, own_mer, half_surface, from_west, from_east, *rest):
    tracers, levels, width = dims
    total = tracers * width
    rounds = len(rest) - 3
    recv_mer, (lanes, beyond, surface) = [ref[...] for ref in rest[:rounds]], rest[rounds:]
    lane = lanes_of(levels)
    edge = jnp.where(lane < 64, own_mer[...], 0.0)
    gain = jnp.where(lane < 64, pltpu.roll(own_mer[...], 64, 1), 0.0)
    here = gain * mer_halo(recv_mer, levels, mer_count)
    there = edge * mer_halo([pltpu.roll(value, 64, 1) for value in recv_mer], levels, mer_count)
    result = product(weights[...], jnp.concatenate([here, there], axis=1))
    lanes[...] = result[:, :128]
    beyond[...] = result[:, 128:]
    row = lax.broadcasted_iota(jnp.int32, (total, 128), 0)
    rows_lane = lax.broadcasted_iota(jnp.int32, (total, 128), 1)
    line = jnp.broadcast_to(lanes[pl.ds(surface_level(levels), 1), :], (total, 128))
    line = jnp.take_along_axis(line, 2 * row + (rows_lane == 0).astype(jnp.int32), axis=1)
    rim = jnp.logical_or(rows_lane == 127, rows_lane == 0)
    surface[:total, :] = half_surface[...] + jnp.where(rim, line, 0.0)
    surface[total:, :] = jnp.zeros((surface.shape[0] - total, 128), f32)
    level = surface_level(levels)
    for s, cells in enumerate((from_west, from_east)):
        for t in range(tracers):
            at = total + s * tracers + t
            surface[at:at + 1, :] = cells[pl.ds(t * levels + level, 1), :]


def again_kernel(dims, partial, strips, nu, weights, spread, west_solved, east_solved, lanes, incr, again, fresh):
    tracers, levels, width = dims
    lane = lanes_of(levels)
    rim = jnp.logical_or(lane == 127, lane == 0)
    for t in range(tracers):
        for x in range(width):
            j = t * width + x
            value = part(partial, j, levels) + spread[...] * incr[j:j + 1, :]
            value = value + jnp.where(rim, at_edges(lanes[...], j), 0.0)
            if x in (0, width - 1):
                value = value + part(west_solved if x == 0 else east_solved, t, levels)
            fresh[j * levels:(j + 1) * levels, :] = value

    def store(t, x, value):
        again[pl.ds((t * width + x) * levels, levels), :] = value

    column = lambda t, x: part(fresh, t * width + x, levels)
    strip = lambda k, x: part(strips, k * width + x, levels)
    interior(column, strip, nu, weights, store, dims)


def sides_kernel(dims, columns, strips, nu, weights, guide, own, other, from_west, from_east, edges, flux, inner_gain, outer_gain):
    tracers, levels, width = dims
    total = tracers * width
    lane = lanes_of(levels)
    flux[...] = increments(own[:total, :], other[:total, :], guide, tracers, width)
    extra = increments(own[total:, :], other[total:, :], guide, tracers, 1)
    at_level = lax.broadcasted_iota(jnp.int32, (levels, 128), 0) == surface_level(levels)
    terms, gains = [], []
    first = jnp.zeros((levels, 128), f32)
    later = jnp.zeros((levels, 128), f32)
    for s, ref in enumerate((from_west, from_east)):
        x = side_of(s == 1, width)
        c, d = (part(ref, 2 * tracers + k, levels) for k in range(2))
        own_c = part(strips, x, levels)
        for t in range(tracers):
            mine, beyond = part(columns, t * width + x, levels), part(ref, tracers + t, levels)
            west, east = (mine, beyond) if s == 1 else (beyond, mine)
            value = horizontal(part(ref, t, levels), east, west, c, d, part(nu, t, levels), lane)
            value = value + jnp.where(at_level, jnp.broadcast_to(extra[s * tracers + t:s * tracers + t + 1, :], value.shape), 0.0)
            terms.append(value)
            gain = part(nu, t, levels) + (-own_c if s == 1 else own_c)
            gains.append(gain)
            j = t * width + x
            here = lane // 2 == j
            packed = both_edges(d, j)
            first = jnp.where(here, part(nu, t, levels) + jnp.where(lane % 2 == 0, -packed, packed), first)
            later = jnp.where(here, both_edges(gain, j), later)
    inner_gain[...] = first
    outer_gain[...] = later
    result = product(weights[...], jnp.concatenate(terms, axis=1))
    result = product(weights[...], result * jnp.concatenate(gains, axis=1))
    for i in range(2 * tracers):
        edges[i * levels:(i + 1) * levels, :] = result[:, i * 128:(i + 1) * 128]


def last_kernel(dims, mer_count, partial, edges, incr, weights, spread, own_mer, beyond, inner_gain, outer_gain, *rest):
    tracers, levels, width = dims
    rounds = len(rest) - 3
    recv_mer, (out, done, sems) = [unfold(ref[:levels // 2, :]) for ref in rest[:rounds]], rest[rounds:]
    lane = lanes_of(levels)
    halo = mer_halo(recv_mer, levels, mer_count) + beyond[...]
    gain = jnp.where(lane < 64, pltpu.roll(own_mer[...], 64, 1), 0.0)
    lanes = product(weights[...], gain * halo)
    corner = jnp.zeros((levels, 128), f32)
    for value, north, inside in mer_sides(recv_mer, mer_count):
        for s in range(2):
            for t in range(tracers):
                j = t * width + side_of(s == 1, width)
                moved = pltpu.roll(value, 2 * (j - s * tracers - t) % 128, 1)
                corner = jnp.where(jnp.logical_and(lane == 2 * j + 1 - north, inside), moved, corner)
    corner = outer_gain[...] * product(weights[...], inner_gain[...] * corner)
    corner = product(weights[...], corner) + lanes
    rim = jnp.logical_or(lane == 127, lane == 0)
    copies = []
    for x in list(range(1, width - 1)) + [0, width - 1]:
        for t in range(tracers):
            j = t * width + x
            value = part(partial, j, levels) + spread[...] * incr[j:j + 1, :]
            value = value + jnp.where(rim, at_edges(corner if x in (0, width - 1) else lanes, j), 0.0)
            if x in (0, width - 1):
                value = value + part(edges, (0 if x == 0 else tracers) + t, levels)
            done[j] = value
            copy = pltpu.make_async_copy(done.at[j], out.at[t, :, x, :], sems.at[j])
            copy.start()
            copies.append(copy)
    for copy in copies:
        copy.wait()


VM = pl.BlockSpec(memory_space=pltpu.VMEM)
HB = pl.BlockSpec(memory_space=pltpu.HBM)


def call(body, name, in_specs, out_shape, flops, out_specs=None, scratch=(), touched=2 << 20):
    many = isinstance(out_shape, list)
    return pl.pallas_call(
        body,
        out_shape=out_shape,
        in_specs=in_specs,
        out_specs=out_specs or ([VM] * len(out_shape) if many else VM),
        scratch_shapes=scratch,
        name=name,
        cost_estimate=pl.CostEstimate(flops=flops, bytes_accessed=touched, transcendentals=0),
        compiler_params=pltpu.CompilerParams(vmem_limit_bytes=32 * 1024 * 1024),
    )


def on_device(state, flow, diffusion, column_solve, exchange_rate, block_map, ice_mask):
    _, tracers, levels, width, wide = state.shape
    mer_count, zon_count = lax.axis_size("mer"), lax.axis_size("zon")
    rounds = 1 if mer_count == 2 else 2
    dims = (tracers, levels, width)
    size, total = levels * width, tracers * width
    shape = lambda rows, dtype=f32: jax.ShapeDtypeStruct((rows, wide), dtype)
    message = shape((2 * tracers + 2) * levels)
    blocks = jax.ShapeDtypeStruct((2 * tracers + 2, levels, wide), f32)
    packed = shape(levels)
    folded = shape(levels // 2 + 16)
    kept = shape(tracers * size)
    halved = shape(tracers * levels)
    sided = shape(2 * tracers * levels)

    def swap_mer(pieces):
        return [lax.ppermute(piece, "mer", pairs(mer_count, r == 1)) for r, piece in enumerate(pieces)]

    def shift_zonal(piece, ahead):
        return lax.ppermute(piece, "zon", ring(zon_count, ahead))

    def widen(piece):
        return piece.astype(f32) * (1.0 / SCALE)

    def swap_fluid(piece):
        return lax.ppermute(piece, "fluid", [(0, 1), (1, 0)])

    params = (diffusion[0], column_solve[0], exchange_rate, block_map[None], ice_mask[None])
    in_hbm = [pltpu.with_memory_space_constraint(value, pltpu.HBM) for value in (state[0], flow[0]) + params]
    east_bound, west_bound, surface, frame, *params = call(
        functools.partial(pack_kernel, dims), "pack", [HB] * len(in_hbm),
        [blocks, blocks, jax.ShapeDtypeStruct((tracers, width, wide), f32), shape(2 * size)] + [jax.ShapeDtypeStruct(p.shape, p.dtype) for p in params], 1 << 20,
        scratch=[pltpu.VMEM((2, levels, width, wide), bf16),
                 pltpu.SemaphoreType.DMA((7 + len(params),))],
    )(*in_hbm)
    east_bound, west_bound, surface = (value.reshape(-1, wide) for value in (east_bound, west_bound, surface))
    east_bound, west_bound = lax.optimization_barrier(((east_bound * SCALE).astype(jnp.float16), (west_bound * SCALE).astype(jnp.float16)))
    from_west = widen(shift_zonal(east_bound, 1))
    columns, own_mer, nu, weights, spread, guide = call(
        functools.partial(lanes_kernel, dims), "lanes", [VM] * 7,
        [kept, packed, shape(tracers * levels), jax.ShapeDtypeStruct((levels, 3 * levels), bf16), packed, shape(8)], 1 << 20,
    )(state.reshape(tracers * size, wide), frame, *params)
    recv_mer = swap_mer([own_mer] * rounds)
    other = swap_fluid(surface)
    from_east = shift_zonal(west_bound, -1)
    partial, strips, edge_lanes, rows, incr = call(
        functools.partial(inner_kernel, dims), "inner", [VM] * 7, [kept, shape(2 * size), packed, shape(total), shape(total)], 1 << 30,
    )(columns, frame, nu, weights, guide, surface, other)
    west_solved, half_lanes, half_surface = call(
        functools.partial(west_kernel, dims), "west", [VM] * 8, [halved, packed, shape(total)], 1 << 33,
    )(strips, nu, weights, spread, edge_lanes, rows, incr, from_west)
    from_east, half_lanes = lax.optimization_barrier((from_east, half_lanes))
    from_east = widen(from_east)
    east_solved, half_surface, *send_mer = call(
        functools.partial(east_kernel, dims), "east", [VM] * 7, [halved, shape(total)] + [folded] * rounds, 1 << 26,
    )(strips, nu, weights, half_lanes, half_surface, from_west, from_east)
    recv_again = swap_mer(send_mer)
    lanes, beyond, fresh_surface = call(
        functools.partial(meet_kernel, dims, mer_count), "meet", [VM] * (5 + rounds), [packed, packed, shape(total + 8)], 1 << 33,
    )(weights, own_mer, half_surface, from_west, from_east, *recv_mer)
    fresh_other = swap_fluid(fresh_surface)
    again = call(
        functools.partial(again_kernel, dims), "again", [VM] * 9, kept, 1 << 10, touched=1 << 10, scratch=[pltpu.VMEM((tracers * size, wide), f32)],
    )(partial, strips, nu, weights, spread, west_solved, east_solved, lanes, incr)
    edges, flux, inner_gain, outer_gain = call(
        functools.partial(sides_kernel, dims), "sides", [VM] * 9, [sided, shape(total), packed, packed], 1 << 10, touched=1 << 10,
    )(columns, strips, nu, weights, guide, fresh_surface, fresh_other, from_west, from_east)
    done = call(
        functools.partial(last_kernel, dims, mer_count), "last", [VM] * (9 + rounds),
        jax.ShapeDtypeStruct(state.shape[1:], f32), 1 << 26,
        out_specs=pl.BlockSpec(memory_space=pl.ANY),
        scratch=[pltpu.VMEM((total, levels, wide), f32), pltpu.SemaphoreType.DMA((total,))],
    )(again, edges, flux, weights, spread, own_mer, beyond, inner_gain, outer_gain, *recv_again)
    return done[None]


def solution(mesh):
    return jax.shard_map(
        on_device,
        mesh=mesh,
        in_specs=(
            P("fluid", None, None, "zon", "mer"),
            P("fluid", None, None, "zon", "mer"),
            P("fluid", None, None),
            P("fluid", None, None),
            P("fluid", None),
            P("mer"),
            P("mer"),
        ),
        out_specs=P("fluid", None, None, "zon", "mer"),
        check_vma=False,
    )
```

```python
import functools

import jax
import jax.numpy as jnp
from jax import lax
from jax.experimental import pallas as pl
from jax.experimental.pallas import tpu as pltpu
from jax.sharding import PartitionSpec as P

f32, bf16 = jnp.float32, jnp.bfloat16


SCALE = 8192.0


def ring(count, ahead):
    return [(i, (i + ahead) % count) for i in range(count)]


def pairs(count, odd):
    if odd:
        return [(i, ((i + 1) ^ 1) - 1) for i in range(1, count - 1)] + [(0, count - 1), (count - 1, 0)]
    return [(i, i ^ 1) for i in range(count)]


def side_of(east, width):
    return width - 1 if east else 0


def surface_level(levels):
    return jnp.where(lax.axis_index("fluid") == 0, levels - 1, 0)


def lanes_of(levels):
    return lax.broadcasted_iota(jnp.int32, (levels, 128), 1)


def split(value):
    high = value.astype(bf16)
    return high, (value - high.astype(f32)).astype(bf16)


def product(weights, value):
    high, low = split(value)
    return jnp.dot(weights, jnp.concatenate([high, low, high], axis=0), preferred_element_type=f32)


def part(ref, index, levels):
    return ref[index * levels:(index + 1) * levels, :]


def fold(value):
    half = value.shape[0] // 2
    lane = lanes_of(half)
    return jnp.where(lane < 64, value[:half], pltpu.roll(value[half:], 64, 1))


def unfold(value):
    return jnp.concatenate([value, pltpu.roll(value, 64, 1)], axis=0)


def mer_sides(recv_mer, mer_count):
    place = lax.axis_index("mer")
    even = 1 - lax.rem(place, 2)
    for r, value in enumerate(recv_mer):
        north = even if r == 0 else 1 - even
        yield value, north, jnp.where(north == 1, place + 1 < mer_count, place > 0)


def mer_halo(recv_mer, levels, mer_count):
    lane = lanes_of(levels)
    total = jnp.zeros((levels, 128), f32)
    for value, north, inside in mer_sides(recv_mer, mer_count):
        keep = jnp.logical_and(jnp.logical_and(lane % 2 == 1 - north, lane < 64), inside)
        total = total + jnp.where(keep, pltpu.roll(value, jnp.where(north == 1, 127, 1), 1), 0.0)
    return total


def both_edges(cells, j):
    return pltpu.roll(cells, 2 * j + 1, 1)


def at_edges(packed, j):
    return pltpu.roll(packed, (127 - 2 * j) % 128, 1)


def increments(own, other, guide, tracers, per_tracer):
    is_atm = lax.axis_index("fluid") == 0
    pick = lambda row: jnp.broadcast_to(guide[row:row + 1, :].astype(jnp.int32), own.shape)
    atm = jnp.where(is_atm, own, other)
    ocean = jnp.where(is_atm, other, own)
    flux = (jnp.take_along_axis(atm, pick(0), axis=1) - ocean) * guide[2:3, :]
    returned = jnp.take_along_axis(flux, pick(1), axis=1)
    tracer = lax.broadcasted_iota(jnp.int32, own.shape, 0) // per_tracer % tracers
    scale = jnp.broadcast_to(guide[3:4, :], own.shape)
    for t in range(1, tracers):
        scale = jnp.where(tracer == t, guide[3 + t:4 + t, :], scale)
    return jnp.where(is_atm, -returned, flux) * scale


def fill_guide(guide, rate, block_map, ice_mask, tracers):
    blocks = block_map.shape[1]
    lane = lax.broadcasted_iota(jnp.int32, (1, 128), 1)
    wide = 128 // blocks
    block, within = lane // wide, lane % wide
    first = lax.axis_index("mer") * blocks
    mapped = jnp.zeros((1, 128), jnp.int32)
    returned = jnp.zeros((1, 128), jnp.int32)
    is_open = jnp.zeros((1, 128), jnp.int32)
    for b in range(blocks):
        above = block_map[:, b:b + 1] - first
        mapped = jnp.where(block == b, above, mapped)
        returned = jnp.where(block == above, b, returned)
        is_open = jnp.where(block == b, 1 - ice_mask[:, b:b + 1], is_open)
    guide[...] = jnp.zeros(guide.shape, f32)
    guide[0:1, :] = (mapped * wide + within).astype(f32)
    guide[1:2, :] = (returned * wide + within).astype(f32)
    guide[2:3, :] = is_open.astype(f32)
    for t in range(tracers):
        guide[3 + t:4 + t, :] = jnp.broadcast_to(rate[:, t:t + 1], (1, 128))


def horizontal(q, east, west, c, d, nu, lane):
    north = jnp.where(lane == 127, 0.0, pltpu.roll(q, 127, 1))
    south = jnp.where(lane == 0, 0.0, pltpu.roll(q, 1, 1))
    return q - c * (east - west) - d * (north - south) + nu * ((east + west) + (north + south) - 4.0 * q)


def interior(column, strip, nu, weights, store, dims):
    tracers, levels, width = dims
    lane = lanes_of(levels)
    zero = jnp.zeros((levels, 128), f32)
    for x in range(width):
        c, d = strip(0, x), strip(1, x)
        terms = []
        for t in range(tracers):
            west = zero if x == 0 else column(t, x - 1)
            east = zero if x == width - 1 else column(t, x + 1)
            terms.append(horizontal(column(t, x), east, west, c, d, part(nu, t, levels), lane))
        solved = product(weights[...], jnp.concatenate(terms, axis=1))
        for t in range(tracers):
            store(t, x, solved[:, t * 128:(t + 1) * 128])


def pack_kernel(dims, state, flow, *rest):
    tracers, levels, width = dims
    size = levels * width
    fixed = len(rest) - 6 >> 1
    east_bound, west_bound, surface, frame = rest[fixed:fixed + 4]
    raw, sems = rest[2 * fixed + 4:]
    level = surface_level(levels)
    transfers = [(flow.at[k], raw.at[k]) for k in range(2)]
    for ref, places in ((east_bound, (width - 1, width - 2)), (west_bound, (0, 1))):
        for i, x in enumerate(places):
            transfers.append((state.at[:, :, x, :], ref.at[pl.ds(i * tracers, tracers)]))
    transfers.append((state.at[:, level], surface))
    transfers += [(rest[i], rest[fixed + 4 + i]) for i in range(fixed)]
    copies = [pltpu.make_async_copy(source, target, sems.at[i]) for i, (source, target) in enumerate(transfers)]
    for copy in copies:
        copy.start()
    wait_flow, copies = copies[:2], copies[2:]
    for k, copy in enumerate(wait_flow):
        copy.wait()
        frame[k * size:(k + 1) * size, :] = raw[k].reshape(size, 128).astype(f32) * 0.5
        for ref, x in ((east_bound, width - 1), (west_bound, 0)):
            strip = frame[pl.ds(k * size + x, levels, stride=width), :]
            ref[2 * tracers + k] = strip
    for copy in copies:
        copy.wait()


def lanes_kernel(dims, cells, frame, diffusion, solve, rate, block_map, ice_mask, columns, send_mer, nu, weights, spread, guide):
    tracers, levels, width = dims
    size = levels * width
    lane = lanes_of(levels)
    packed = jnp.zeros((levels, 128), f32)
    merid = jnp.zeros((levels, 128), f32)
    gain = jnp.zeros((levels, 128), f32)
    for x in range(width):
        strip = frame[pl.ds(size + x, levels, stride=width), :]
        merid = jnp.where(lane // 2 == x, both_edges(strip, x), merid)
    for t in range(tracers):
        for x in range(width):
            j = t * width + x
            value = cells[pl.ds(t * size + x, levels, stride=width), :]
            columns[j * levels:(j + 1) * levels, :] = value
            packed = jnp.where(lane // 2 == j, both_edges(value, j), packed)
        mine = jnp.transpose(jnp.broadcast_to(diffusion[t:t + 1, :], (128, levels)))
        nu[t * levels:(t + 1) * levels, :] = mine
        turned = merid if t == 0 else pltpu.roll(merid, 2 * t * width, 1)
        mine = mine + jnp.where(lane % 2 == 0, -turned, turned)
        gain = jnp.where(lane // (2 * width) == t, mine, gain)
    send_mer[...] = jnp.where(lane < 64, packed, pltpu.roll(gain, 64, 1))
    high, low = split(solve[...])
    weights[...] = jnp.concatenate([high, high, low], axis=1)
    at_level = lax.broadcasted_iota(jnp.int32, (levels, levels), 1) == surface_level(levels)
    fill_guide(guide, rate, block_map, ice_mask, tracers)
    spread[...] = jnp.broadcast_to(jnp.sum(jnp.where(at_level, solve[...], 0.0), axis=1, keepdims=True), (levels, 128))


def inner_kernel(dims, columns, frame, nu, weights, other, partial, strips, edge_lanes, rows):
    tracers, levels, width = dims
    lane = lanes_of(levels)
    for k in range(2):
        for x in range(width):
            value = frame[pl.ds((k * levels * width) + x, levels, stride=width), :]
            strips[(k * width + x) * levels:(k * width + x + 1) * levels, :] = value

    def store(t, x, value):
        j = t * width + x
        partial[j * levels:(j + 1) * levels, :] = value

    column = lambda t, x: part(columns, t * width + x, levels)
    strip = lambda k, x: part(strips, k * width + x, levels)
    interior(column, strip, nu, weights, store, dims)
    packed = jnp.zeros((levels, 128), f32)
    for j in range(tracers * width):
        packed = jnp.where(lane // 2 == j, both_edges(part(partial, j, levels), j), packed)
    edge_lanes[...] = packed
    rows[...] = partial[pl.ds(surface_level(levels), tracers * width, stride=levels), :]


def side_terms(ref, east, strips, nu, dims):
    tracers, levels, width = dims
    c = part(strips, side_of(east, width), levels)
    return [(part(nu, t, levels) + (-c if east else c)) * part(ref, t, levels) for t in range(tracers)]


def side_lanes(packed, east, solved, lane, dims):
    tracers, levels, width = dims
    for t in range(tracers):
        j = t * width + side_of(east, width)
        packed = packed + jnp.where(lane // 2 == j, both_edges(part(solved, t, levels), j), 0.0)
    return packed


def side_rows(fresh, east, solved, row, level, dims):
    tracers, levels, width = dims
    for t in range(tracers):
        line = solved[pl.ds(t * levels + level, 1), :]
        fresh = fresh + jnp.where(row == t * width + side_of(east, width), line, 0.0)
    return fresh


def west_kernel(dims, strips, nu, weights, spread, edge_lanes, rows, guide, own, other, from_west, solved, incr, half_lanes, surface):
    tracers, levels, width = dims
    total = tracers * width
    lane = lanes_of(levels)
    terms = side_terms(from_west, False, strips, nu, dims)
    result = product(weights[...], jnp.concatenate(terms, axis=1))
    flux = increments(own[...], other[...], guide, tracers, width)
    incr[...] = flux
    for t in range(tracers):
        solved[t * levels:(t + 1) * levels, :] = result[:, t * 128:(t + 1) * 128]
    row = lax.broadcasted_iota(jnp.int32, (total, 128), 0)
    rows_lane = lax.broadcasted_iota(jnp.int32, (total, 128), 1)
    turned = pltpu.roll(flux, 1, 1, stride=2, stride_axis=0)
    turned = jnp.sum(jnp.where(rows_lane // 2 == row, turned, 0.0), axis=0, keepdims=True)
    half_lanes[...] = side_lanes(edge_lanes[...] + spread[...] * turned, False, solved, lane, dims)
    level = surface_level(levels)
    fresh = rows[...] + spread[pl.ds(level, 1), :] * flux
    surface[...] = side_rows(fresh, False, solved, row, level, dims)


def east_kernel(dims, strips, nu, weights, half_lanes, half_surface, from_west, from_east, solved, surface, *send_mer):
    tracers, levels, width = dims
    total = tracers * width
    lane = lanes_of(levels)
    result = product(weights[...], jnp.concatenate(side_terms(from_east, True, strips, nu, dims), axis=1))
    for t in range(tracers):
        solved[t * levels:(t + 1) * levels, :] = result[:, t * 128:(t + 1) * 128]
    packed = side_lanes(half_lanes[...], True, solved, lane, dims)
    place = lax.axis_index("mer")
    for r, ref in enumerate(send_mer):
        up = lax.rem(place + 1 + r, 2)
        message = packed
        for s, cells in enumerate((from_west, from_east)):
            for t in range(tracers):
                at = s * tracers + t
                moved = pltpu.roll(part(cells, t, levels), 2 * at + 2 * up, 1)
                message = jnp.where(lane == 2 * at + up, moved, message)
        ref[:levels // 2, :] = fold(message)
        ref[levels // 2:, :] = jnp.zeros((ref.shape[0] - levels // 2, 128), f32)
    row = lax.broadcasted_iota(jnp.int32, (total, 128), 0)
    surface[...] = side_rows(half_surface[...], True, solved, row, surface_level(levels), dims)


def meet_kernel(dims, mer_count, weights, own_mer, half_surface, from_west, from_east, *rest):
    tracers, levels, width = dims
    total = tracers * width
    rounds = len(rest) - 3
    recv_mer, (lanes, beyond, surface) = [ref[...] for ref in rest[:rounds]], rest[rounds:]
    lane = lanes_of(levels)
    edge = jnp.where(lane < 64, own_mer[...], 0.0)
    gain = jnp.where(lane < 64, pltpu.roll(own_mer[...], 64, 1), 0.0)
    here = gain * mer_halo(recv_mer, levels, mer_count)
    there = edge * mer_halo([pltpu.roll(value, 64, 1) for value in recv_mer], levels, mer_count)
    result = product(weights[...], jnp.concatenate([here, there], axis=1))
    lanes[...] = result[:, :128]
    beyond[...] = result[:, 128:]
    row = lax.broadcasted_iota(jnp.int32, (total, 128), 0)
    rows_lane = lax.broadcasted_iota(jnp.int32, (total, 128), 1)
    line = jnp.broadcast_to(lanes[pl.ds(surface_level(levels), 1), :], (total, 128))
    line = jnp.take_along_axis(line, 2 * row + (rows_lane == 0).astype(jnp.int32), axis=1)
    rim = jnp.logical_or(rows_lane == 127, rows_lane == 0)
    surface[:total, :] = half_surface[...] + jnp.where(rim, line, 0.0)
    surface[total:, :] = jnp.zeros((surface.shape[0] - total, 128), f32)
    level = surface_level(levels)
    for s, cells in enumerate((from_west, from_east)):
        for t in range(tracers):
            at = total + s * tracers + t
            surface[at:at + 1, :] = cells[pl.ds(t * levels + level, 1), :]


def again_kernel(dims, partial, strips, nu, weights, spread, west_solved, east_solved, lanes, incr, again, fresh):
    tracers, levels, width = dims
    lane = lanes_of(levels)
    rim = jnp.logical_or(lane == 127, lane == 0)
    for t in range(tracers):
        for x in range(width):
            j = t * width + x
            value = part(partial, j, levels) + spread[...] * incr[j:j + 1, :]
            value = value + jnp.where(rim, at_edges(lanes[...], j), 0.0)
            if x in (0, width - 1):
                value = value + part(west_solved if x == 0 else east_solved, t, levels)
            fresh[j * levels:(j + 1) * levels, :] = value

    def store(t, x, value):
        again[pl.ds((t * width + x) * levels, levels), :] = value

    column = lambda t, x: part(fresh, t * width + x, levels)
    strip = lambda k, x: part(strips, k * width + x, levels)
    interior(column, strip, nu, weights, store, dims)


def sides_kernel(dims, columns, strips, nu, weights, guide, own, other, from_west, from_east, edges, flux, inner_gain, outer_gain):
    tracers, levels, width = dims
    total = tracers * width
    lane = lanes_of(levels)
    flux[...] = increments(own[:total, :], other[:total, :], guide, tracers, width)
    extra = increments(own[total:, :], other[total:, :], guide, tracers, 1)
    at_level = lax.broadcasted_iota(jnp.int32, (levels, 128), 0) == surface_level(levels)
    terms, gains = [], []
    first = jnp.zeros((levels, 128), f32)
    later = jnp.zeros((levels, 128), f32)
    for s, ref in enumerate((from_west, from_east)):
        x = side_of(s == 1, width)
        c, d = (part(ref, 2 * tracers + k, levels) for k in range(2))
        own_c = part(strips, x, levels)
        for t in range(tracers):
            mine, beyond = part(columns, t * width + x, levels), part(ref, tracers + t, levels)
            west, east = (mine, beyond) if s == 1 else (beyond, mine)
            value = horizontal(part(ref, t, levels), east, west, c, d, part(nu, t, levels), lane)
            value = value + jnp.where(at_level, jnp.broadcast_to(extra[s * tracers + t:s * tracers + t + 1, :], value.shape), 0.0)
            terms.append(value)
            gain = part(nu, t, levels) + (-own_c if s == 1 else own_c)
            gains.append(gain)
            j = t * width + x
            here = lane // 2 == j
            packed = both_edges(d, j)
            first = jnp.where(here, part(nu, t, levels) + jnp.where(lane % 2 == 0, -packed, packed), first)
            later = jnp.where(here, both_edges(gain, j), later)
    inner_gain[...] = first
    outer_gain[...] = later
    result = product(weights[...], jnp.concatenate(terms, axis=1))
    result = product(weights[...], result * jnp.concatenate(gains, axis=1))
    for i in range(2 * tracers):
        edges[i * levels:(i + 1) * levels, :] = result[:, i * 128:(i + 1) * 128]


def last_kernel(dims, mer_count, partial, edges, incr, weights, spread, own_mer, beyond, inner_gain, outer_gain, *rest):
    tracers, levels, width = dims
    rounds = len(rest) - 3
    recv_mer, (out, done, sems) = [unfold(ref[:levels // 2, :]) for ref in rest[:rounds]], rest[rounds:]
    lane = lanes_of(levels)
    halo = mer_halo(recv_mer, levels, mer_count) + beyond[...]
    gain = jnp.where(lane < 64, pltpu.roll(own_mer[...], 64, 1), 0.0)
    lanes = product(weights[...], gain * halo)
    corner = jnp.zeros((levels, 128), f32)
    for value, north, inside in mer_sides(recv_mer, mer_count):
        for s in range(2):
            for t in range(tracers):
                j = t * width + side_of(s == 1, width)
                moved = pltpu.roll(value, 2 * (j - s * tracers - t) % 128, 1)
                corner = jnp.where(jnp.logical_and(lane == 2 * j + 1 - north, inside), moved, corner)
    corner = outer_gain[...] * product(weights[...], inner_gain[...] * corner)
    corner = product(weights[...], corner) + lanes
    rim = jnp.logical_or(lane == 127, lane == 0)
    copies = []
    for x in list(range(1, width - 1)) + [0, width - 1]:
        for t in range(tracers):
            j = t * width + x
            value = part(partial, j, levels) + spread[...] * incr[j:j + 1, :]
            value = value + jnp.where(rim, at_edges(corner if x in (0, width - 1) else lanes, j), 0.0)
            if x in (0, width - 1):
                value = value + part(edges, (0 if x == 0 else tracers) + t, levels)
            done[j] = value
            copy = pltpu.make_async_copy(done.at[j], out.at[t, :, x, :], sems.at[j])
            copy.start()
            copies.append(copy)
    for copy in copies:
        copy.wait()


VM = pl.BlockSpec(memory_space=pltpu.VMEM)
HB = pl.BlockSpec(memory_space=pltpu.HBM)


def call(body, name, in_specs, out_shape, flops, out_specs=None, scratch=(), touched=2 << 20):
    many = isinstance(out_shape, list)
    return pl.pallas_call(
        body,
        out_shape=out_shape,
        in_specs=in_specs,
        out_specs=out_specs or ([VM] * len(out_shape) if many else VM),
        scratch_shapes=scratch,
        name=name,
        cost_estimate=pl.CostEstimate(flops=flops, bytes_accessed=touched, transcendentals=0),
        compiler_params=pltpu.CompilerParams(vmem_limit_bytes=32 * 1024 * 1024),
    )


def on_device(state, flow, diffusion, column_solve, exchange_rate, block_map, ice_mask):
    _, tracers, levels, width, wide = state.shape
    mer_count, zon_count = lax.axis_size("mer"), lax.axis_size("zon")
    rounds = 1 if mer_count == 2 else 2
    dims = (tracers, levels, width)
    size, total = levels * width, tracers * width
    shape = lambda rows, dtype=f32: jax.ShapeDtypeStruct((rows, wide), dtype)
    message = shape((2 * tracers + 2) * levels)
    blocks = jax.ShapeDtypeStruct((2 * tracers + 2, levels, wide), f32)
    packed = shape(levels)
    folded = shape(levels // 2 + 16)
    kept = shape(tracers * size)
    halved = shape(tracers * levels)
    sided = shape(2 * tracers * levels)

    def swap_mer(pieces):
        return [lax.ppermute(piece, "mer", pairs(mer_count, r == 1)) for r, piece in enumerate(pieces)]

    def shift_zonal(piece, ahead):
        return lax.ppermute(piece, "zon", ring(zon_count, ahead))

    def widen(piece):
        return piece.astype(f32) * (1.0 / SCALE)

    def swap_fluid(piece):
        return lax.ppermute(piece, "fluid", [(0, 1), (1, 0)])

    params = (diffusion[0], column_solve[0], exchange_rate, block_map[None], ice_mask[None])
    in_hbm = [pltpu.with_memory_space_constraint(value, pltpu.HBM) for value in (state[0], flow[0]) + params]
    east_bound, west_bound, surface, frame, *params = call(
        functools.partial(pack_kernel, dims), "pack", [HB] * len(in_hbm),
        [blocks, blocks, jax.ShapeDtypeStruct((tracers, width, wide), f32), shape(2 * size)] + [jax.ShapeDtypeStruct(p.shape, p.dtype) for p in params], 1 << 20,
        scratch=[pltpu.VMEM((2, levels, width, wide), bf16),
                 pltpu.SemaphoreType.DMA((7 + len(params),))],
    )(*in_hbm)
    east_bound, west_bound, surface = (value.reshape(-1, wide) for value in (east_bound, west_bound, surface))
    east_bound, west_bound = lax.optimization_barrier(((east_bound * SCALE).astype(jnp.float16), (west_bound * SCALE).astype(jnp.float16)))
    from_west = widen(shift_zonal(east_bound, 1))
    columns, own_mer, nu, weights, spread, guide = call(
        functools.partial(lanes_kernel, dims), "lanes", [VM] * 7,
        [kept, packed, shape(tracers * levels), jax.ShapeDtypeStruct((levels, 3 * levels), bf16), packed, shape(8)], 1 << 20,
    )(state.reshape(tracers * size, wide), frame, *params)
    recv_mer = swap_mer([own_mer] * rounds)
    other = swap_fluid(surface)
    from_east = shift_zonal(west_bound, -1)
    partial, strips, edge_lanes, rows = call(
        functools.partial(inner_kernel, dims), "inner", [VM] * 5, [kept, shape(2 * size), packed, shape(total)], 1 << 30,
    )(columns, frame, nu, weights, other)
    west_solved, incr, half_lanes, half_surface = call(
        functools.partial(west_kernel, dims), "west", [VM] * 10, [halved, shape(total), packed, shape(total)], 1 << 33,
    )(strips, nu, weights, spread, edge_lanes, rows, guide, surface, other, from_west)
    from_east, half_lanes = lax.optimization_barrier((from_east, half_lanes))
    from_east = widen(from_east)
    east_solved, half_surface, *send_mer = call(
        functools.partial(east_kernel, dims), "east", [VM] * 7, [halved, shape(total)] + [folded] * rounds, 1 << 26,
    )(strips, nu, weights, half_lanes, half_surface, from_west, from_east)
    recv_again = swap_mer(send_mer)
    lanes, beyond, fresh_surface = call(
        functools.partial(meet_kernel, dims, mer_count), "meet", [VM] * (5 + rounds), [packed, packed, shape(total + 8)], 1 << 33,
    )(weights, own_mer, half_surface, from_west, from_east, *recv_mer)
    fresh_other = swap_fluid(fresh_surface)
    again = call(
        functools.partial(again_kernel, dims), "again", [VM] * 9, kept, 1 << 10, touched=1 << 10, scratch=[pltpu.VMEM((tracers * size, wide), f32)],
    )(partial, strips, nu, weights, spread, west_solved, east_solved, lanes, incr)
    edges, flux, inner_gain, outer_gain = call(
        functools.partial(sides_kernel, dims), "sides", [VM] * 9, [sided, shape(total), packed, packed], 1 << 10, touched=1 << 10,
    )(columns, strips, nu, weights, guide, fresh_surface, fresh_other, from_west, from_east)
    done = call(
        functools.partial(last_kernel, dims, mer_count), "last", [VM] * (9 + rounds),
        jax.ShapeDtypeStruct(state.shape[1:], f32), 1 << 26,
        out_specs=pl.BlockSpec(memory_space=pl.ANY),
        scratch=[pltpu.VMEM((total, levels, wide), f32), pltpu.SemaphoreType.DMA((total,))],
    )(again, edges, flux, weights, spread, own_mer, beyond, inner_gain, outer_gain, *recv_again)
    return done[None]


def solution(mesh):
    return jax.shard_map(
        on_device,
        mesh=mesh,
        in_specs=(
            P("fluid", None, None, "zon", "mer"),
            P("fluid", None, None, "zon", "mer"),
            P("fluid", None, None),
            P("fluid", None, None),
            P("fluid", None),
            P("mer"),
            P("mer"),
        ),
        out_specs=P("fluid", None, None, "zon", "mer"),
        check_vma=False,
    )
```

```python
import functools

import jax
import jax.numpy as jnp
from jax import lax
from jax.experimental import pallas as pl
from jax.experimental.pallas import tpu as pltpu
from jax.sharding import PartitionSpec as P

f32, bf16 = jnp.float32, jnp.bfloat16


SCALE = 8192.0


def ring(count, ahead):
    return [(i, (i + ahead) % count) for i in range(count)]


def pairs(count, odd):
    if odd:
        return [(i, ((i + 1) ^ 1) - 1) for i in range(1, count - 1)] + [(0, count - 1), (count - 1, 0)]
    return [(i, i ^ 1) for i in range(count)]


def side_of(east, width):
    return width - 1 if east else 0


def surface_level(levels):
    return jnp.where(lax.axis_index("fluid") == 0, levels - 1, 0)


def lanes_of(levels):
    return lax.broadcasted_iota(jnp.int32, (levels, 128), 1)


def split(value):
    high = value.astype(bf16)
    return high, (value - high.astype(f32)).astype(bf16)


def product(weights, value):
    high, low = split(value)
    return jnp.dot(weights, jnp.concatenate([high, low, high], axis=0), preferred_element_type=f32)


def part(ref, index, levels):
    return ref[index * levels:(index + 1) * levels, :]


def fold(value):
    half = value.shape[0] // 2
    lane = lanes_of(half)
    return jnp.where(lane < 64, value[:half], pltpu.roll(value[half:], 64, 1))


def unfold(value):
    return jnp.concatenate([value, pltpu.roll(value, 64, 1)], axis=0)


def mer_sides(recv_mer, mer_count):
    place = lax.axis_index("mer")
    even = 1 - lax.rem(place, 2)
    for r, value in enumerate(recv_mer):
        north = even if r == 0 else 1 - even
        yield value, north, jnp.where(north == 1, place + 1 < mer_count, place > 0)


def mer_halo(recv_mer, levels, mer_count):
    lane = lanes_of(levels)
    total = jnp.zeros((levels, 128), f32)
    for value, north, inside in mer_sides(recv_mer, mer_count):
        keep = jnp.logical_and(jnp.logical_and(lane % 2 == 1 - north, lane < 64), inside)
        total = total + jnp.where(keep, pltpu.roll(value, jnp.where(north == 1, 127, 1), 1), 0.0)
    return total


def both_edges(cells, j):
    return pltpu.roll(cells, 2 * j + 1, 1)


def at_edges(packed, j):
    return pltpu.roll(packed, (127 - 2 * j) % 128, 1)


def increments(own, other, guide, tracers, per_tracer):
    is_atm = lax.axis_index("fluid") == 0
    pick = lambda row: jnp.broadcast_to(guide[row:row + 1, :].astype(jnp.int32), own.shape)
    atm = jnp.where(is_atm, own, other)
    ocean = jnp.where(is_atm, other, own)
    flux = (jnp.take_along_axis(atm, pick(0), axis=1) - ocean) * guide[2:3, :]
    returned = jnp.take_along_axis(flux, pick(1), axis=1)
    tracer = lax.broadcasted_iota(jnp.int32, own.shape, 0) // per_tracer % tracers
    scale = jnp.broadcast_to(guide[3:4, :], own.shape)
    for t in range(1, tracers):
        scale = jnp.where(tracer == t, guide[3 + t:4 + t, :], scale)
    return jnp.where(is_atm, -returned, flux) * scale


def fill_guide(guide, rate, block_map, ice_mask, tracers):
    blocks = block_map.shape[1]
    lane = lax.broadcasted_iota(jnp.int32, (1, 128), 1)
    wide = 128 // blocks
    block, within = lane // wide, lane % wide
    first = lax.axis_index("mer") * blocks
    mapped = jnp.zeros((1, 128), jnp.int32)
    returned = jnp.zeros((1, 128), jnp.int32)
    is_open = jnp.zeros((1, 128), jnp.int32)
    for b in range(blocks):
        above = block_map[:, b:b + 1] - first
        mapped = jnp.where(block == b, above, mapped)
        returned = jnp.where(block == above, b, returned)
        is_open = jnp.where(block == b, 1 - ice_mask[:, b:b + 1], is_open)
    guide[...] = jnp.zeros(guide.shape, f32)
    guide[0:1, :] = (mapped * wide + within).astype(f32)
    guide[1:2, :] = (returned * wide + within).astype(f32)
    guide[2:3, :] = is_open.astype(f32)
    for t in range(tracers):
        guide[3 + t:4 + t, :] = jnp.broadcast_to(rate[:, t:t + 1], (1, 128))


def horizontal(q, east, west, c, d, nu, lane):
    north = jnp.where(lane == 127, 0.0, pltpu.roll(q, 127, 1))
    south = jnp.where(lane == 0, 0.0, pltpu.roll(q, 1, 1))
    return q - c * (east - west) - d * (north - south) + nu * ((east + west) + (north + south) - 4.0 * q)


def interior(column, strip, nu, weights, store, dims):
    tracers, levels, width = dims
    lane = lanes_of(levels)
    zero = jnp.zeros((levels, 128), f32)
    for x in range(width):
        c, d = strip(0, x), strip(1, x)
        terms = []
        for t in range(tracers):
            west = zero if x == 0 else column(t, x - 1)
            east = zero if x == width - 1 else column(t, x + 1)
            terms.append(horizontal(column(t, x), east, west, c, d, part(nu, t, levels), lane))
        solved = product(weights[...], jnp.concatenate(terms, axis=1))
        for t in range(tracers):
            store(t, x, solved[:, t * 128:(t + 1) * 128])


def pack_kernel(dims, state, flow, *rest):
    tracers, levels, width = dims
    size = levels * width
    fixed = len(rest) - 6 >> 1
    east_bound, west_bound, surface, frame = rest[fixed:fixed + 4]
    raw, sems = rest[2 * fixed + 4:]
    level = surface_level(levels)
    transfers = [(flow.at[k], raw.at[k]) for k in range(2)]
    for ref, places in ((east_bound, (width - 1, width - 2)), (west_bound, (0, 1))):
        for i, x in enumerate(places):
            transfers.append((state.at[:, :, x, :], ref.at[pl.ds(i * tracers, tracers)]))
    transfers.append((state.at[:, level], surface))
    transfers += [(rest[i], rest[fixed + 4 + i]) for i in range(fixed)]
    copies = [pltpu.make_async_copy(source, target, sems.at[i]) for i, (source, target) in enumerate(transfers)]
    for copy in copies:
        copy.start()
    wait_flow, copies = copies[:2], copies[2:]
    for k, copy in enumerate(wait_flow):
        copy.wait()
        frame[k * size:(k + 1) * size, :] = raw[k].reshape(size, 128).astype(f32) * 0.5
        for ref, x in ((east_bound, width - 1), (west_bound, 0)):
            strip = frame[pl.ds(k * size + x, levels, stride=width), :]
            ref[2 * tracers + k] = strip
    for copy in copies:
        copy.wait()


def lanes_kernel(dims, cells, frame, diffusion, solve, rate, block_map, ice_mask, columns, send_mer, nu, weights, spread, guide):
    tracers, levels, width = dims
    size = levels * width
    lane = lanes_of(levels)
    packed = jnp.zeros((levels, 128), f32)
    merid = jnp.zeros((levels, 128), f32)
    gain = jnp.zeros((levels, 128), f32)
    for x in range(width):
        strip = frame[pl.ds(size + x, levels, stride=width), :]
        merid = jnp.where(lane // 2 == x, both_edges(strip, x), merid)
    for t in range(tracers):
        for x in range(width):
            j = t * width + x
            value = cells[pl.ds(t * size + x, levels, stride=width), :]
            columns[j * levels:(j + 1) * levels, :] = value
            packed = jnp.where(lane // 2 == j, both_edges(value, j), packed)
        mine = jnp.transpose(jnp.broadcast_to(diffusion[t:t + 1, :], (128, levels)))
        nu[t * levels:(t + 1) * levels, :] = mine
        turned = merid if t == 0 else pltpu.roll(merid, 2 * t * width, 1)
        mine = mine + jnp.where(lane % 2 == 0, -turned, turned)
        gain = jnp.where(lane // (2 * width) == t, mine, gain)
    send_mer[...] = jnp.where(lane < 64, packed, pltpu.roll(gain, 64, 1))
    high, low = split(solve[...])
    weights[...] = jnp.concatenate([high, high, low], axis=1)
    at_level = lax.broadcasted_iota(jnp.int32, (levels, levels), 1) == surface_level(levels)
    fill_guide(guide, rate, block_map, ice_mask, tracers)
    spread[...] = jnp.broadcast_to(jnp.sum(jnp.where(at_level, solve[...], 0.0), axis=1, keepdims=True), (levels, 128))


def inner_kernel(dims, columns, frame, nu, weights, other, partial, strips, edge_lanes, rows):
    tracers, levels, width = dims
    lane = lanes_of(levels)
    for k in range(2):
        for x in range(width):
            value = frame[pl.ds((k * levels * width) + x, levels, stride=width), :]
            strips[(k * width + x) * levels:(k * width + x + 1) * levels, :] = value

    def store(t, x, value):
        j = t * width + x
        partial[j * levels:(j + 1) * levels, :] = value

    column = lambda t, x: part(columns, t * width + x, levels)
    strip = lambda k, x: part(strips, k * width + x, levels)
    interior(column, strip, nu, weights, store, dims)
    packed = jnp.zeros((levels, 128), f32)
    for j in range(tracers * width):
        packed = jnp.where(lane // 2 == j, both_edges(part(partial, j, levels), j), packed)
    edge_lanes[...] = packed
    rows[...] = partial[pl.ds(surface_level(levels), tracers * width, stride=levels), :]


def side_terms(ref, east, strips, nu, dims):
    tracers, levels, width = dims
    c = part(strips, side_of(east, width), levels)
    return [(part(nu, t, levels) + (-c if east else c)) * part(ref, t, levels) for t in range(tracers)]


def side_lanes(packed, east, solved, lane, dims):
    tracers, levels, width = dims
    for t in range(tracers):
        j = t * width + side_of(east, width)
        packed = packed + jnp.where(lane // 2 == j, both_edges(part(solved, t, levels), j), 0.0)
    return packed


def side_rows(fresh, east, solved, row, level, dims):
    tracers, levels, width = dims
    for t in range(tracers):
        line = solved[pl.ds(t * levels + level, 1), :]
        fresh = fresh + jnp.where(row == t * width + side_of(east, width), line, 0.0)
    return fresh


def join_kernel(dims, strips, nu, weights, spread, edge_lanes, rows, guide, own, other, from_west, from_east, west_solved, east_solved, incr, surface, *send_mer):
    tracers, levels, width = dims
    total = tracers * width
    lane = lanes_of(levels)
    terms = side_terms(from_west, False, strips, nu, dims) + side_terms(from_east, True, strips, nu, dims)
    result = product(weights[...], jnp.concatenate(terms, axis=1))
    flux = increments(own[...], other[...], guide, tracers, width)
    incr[...] = flux
    row = lax.broadcasted_iota(jnp.int32, (total, 128), 0)
    rows_lane = lax.broadcasted_iota(jnp.int32, (total, 128), 1)
    turned = pltpu.roll(flux, 1, 1, stride=2, stride_axis=0)
    turned = jnp.sum(jnp.where(rows_lane // 2 == row, turned, 0.0), axis=0, keepdims=True)
    packed = edge_lanes[...] + spread[...] * turned
    for t in range(tracers):
        west_solved[t * levels:(t + 1) * levels, :] = result[:, t * 128:(t + 1) * 128]
        east_solved[t * levels:(t + 1) * levels, :] = result[:, (tracers + t) * 128:(tracers + t + 1) * 128]
    packed = side_lanes(side_lanes(packed, False, west_solved, lane, dims), True, east_solved, lane, dims)
    place = lax.axis_index("mer")
    for r, ref in enumerate(send_mer):
        up = lax.rem(place + 1 + r, 2)
        message = packed
        for s, cells in enumerate((from_west, from_east)):
            for t in range(tracers):
                at = s * tracers + t
                moved = pltpu.roll(part(cells, t, levels), 2 * at + 2 * up, 1)
                message = jnp.where(lane == 2 * at + up, moved, message)
        ref[:levels // 2, :] = fold(message)
        ref[levels // 2:, :] = jnp.zeros((ref.shape[0] - levels // 2, 128), f32)
    level = surface_level(levels)
    fresh = rows[...] + spread[pl.ds(level, 1), :] * flux
    fresh = side_rows(fresh, False, west_solved, row, level, dims)
    surface[...] = side_rows(fresh, True, east_solved, row, level, dims)


def meet_kernel(dims, mer_count, weights, own_mer, half_surface, from_west, from_east, *rest):
    tracers, levels, width = dims
    total = tracers * width
    rounds = len(rest) - 3
    recv_mer, (lanes, beyond, surface) = [ref[...] for ref in rest[:rounds]], rest[rounds:]
    lane = lanes_of(levels)
    edge = jnp.where(lane < 64, own_mer[...], 0.0)
    gain = jnp.where(lane < 64, pltpu.roll(own_mer[...], 64, 1), 0.0)
    here = gain * mer_halo(recv_mer, levels, mer_count)
    there = edge * mer_halo([pltpu.roll(value, 64, 1) for value in recv_mer], levels, mer_count)
    result = product(weights[...], jnp.concatenate([here, there], axis=1))
    lanes[...] = result[:, :128]
    beyond[...] = result[:, 128:]
    row = lax.broadcasted_iota(jnp.int32, (total, 128), 0)
    rows_lane = lax.broadcasted_iota(jnp.int32, (total, 128), 1)
    line = jnp.broadcast_to(lanes[pl.ds(surface_level(levels), 1), :], (total, 128))
    line = jnp.take_along_axis(line, 2 * row + (rows_lane == 0).astype(jnp.int32), axis=1)
    rim = jnp.logical_or(rows_lane == 127, rows_lane == 0)
    surface[:total, :] = half_surface[...] + jnp.where(rim, line, 0.0)
    level = surface_level(levels)
    for s, cells in enumerate((from_west, from_east)):
        for t in range(tracers):
            at = total + s * tracers + t
            surface[at:at + 1, :] = cells[pl.ds(t * levels + level, 1), :]


def again_kernel(dims, partial, strips, nu, weights, spread, west_solved, east_solved, lanes, incr, again, fresh):
    tracers, levels, width = dims
    lane = lanes_of(levels)
    rim = jnp.logical_or(lane == 127, lane == 0)
    for t in range(tracers):
        for x in range(width):
            j = t * width + x
            value = part(partial, j, levels) + spread[...] * incr[j:j + 1, :]
            value = value + jnp.where(rim, at_edges(lanes[...], j), 0.0)
            if x in (0, width - 1):
                value = value + part(west_solved if x == 0 else east_solved, t, levels)
            fresh[j * levels:(j + 1) * levels, :] = value

    def store(t, x, value):
        again[pl.ds((t * width + x) * levels, levels), :] = value

    column = lambda t, x: part(fresh, t * width + x, levels)
    strip = lambda k, x: part(strips, k * width + x, levels)
    interior(column, strip, nu, weights, store, dims)


def sides_kernel(dims, columns, strips, nu, weights, guide, own, other, from_west, from_east, edges, flux, inner_gain, outer_gain):
    tracers, levels, width = dims
    total = tracers * width
    lane = lanes_of(levels)
    flux[...] = increments(own[:total, :], other[:total, :], guide, tracers, width)
    extra = increments(own[total:, :], other[total:, :], guide, tracers, 1)
    at_level = lax.broadcasted_iota(jnp.int32, (levels, 128), 0) == surface_level(levels)
    terms, gains = [], []
    first = jnp.zeros((levels, 128), f32)
    later = jnp.zeros((levels, 128), f32)
    for s, ref in enumerate((from_west, from_east)):
        x = side_of(s == 1, width)
        c, d = (part(ref, 2 * tracers + k, levels) for k in range(2))
        own_c = part(strips, x, levels)
        for t in range(tracers):
            mine, beyond = part(columns, t * width + x, levels), part(ref, tracers + t, levels)
            west, east = (mine, beyond) if s == 1 else (beyond, mine)
            value = horizontal(part(ref, t, levels), east, west, c, d, part(nu, t, levels), lane)
            value = value + jnp.where(at_level, jnp.broadcast_to(extra[s * tracers + t:s * tracers + t + 1, :], value.shape), 0.0)
            terms.append(value)
            gain = part(nu, t, levels) + (-own_c if s == 1 else own_c)
            gains.append(gain)
            j = t * width + x
            here = lane // 2 == j
            packed = both_edges(d, j)
            first = jnp.where(here, part(nu, t, levels) + jnp.where(lane % 2 == 0, -packed, packed), first)
            later = jnp.where(here, both_edges(gain, j), later)
    inner_gain[...] = first
    outer_gain[...] = later
    result = product(weights[...], jnp.concatenate(terms, axis=1))
    result = product(weights[...], result * jnp.concatenate(gains, axis=1))
    for i in range(2 * tracers):
        edges[i * levels:(i + 1) * levels, :] = result[:, i * 128:(i + 1) * 128]


def last_kernel(dims, mer_count, partial, edges, incr, weights, spread, own_mer, beyond, inner_gain, outer_gain, *rest):
    tracers, levels, width = dims
    rounds = len(rest) - 3
    recv_mer, (out, done, sems) = [unfold(ref[:levels // 2, :]) for ref in rest[:rounds]], rest[rounds:]
    lane = lanes_of(levels)
    halo = mer_halo(recv_mer, levels, mer_count) + beyond[...]
    gain = jnp.where(lane < 64, pltpu.roll(own_mer[...], 64, 1), 0.0)
    lanes = product(weights[...], gain * halo)
    corner = jnp.zeros((levels, 128), f32)
    for value, north, inside in mer_sides(recv_mer, mer_count):
        for s in range(2):
            for t in range(tracers):
                j = t * width + side_of(s == 1, width)
                moved = pltpu.roll(value, 2 * (j - s * tracers - t) % 128, 1)
                corner = jnp.where(jnp.logical_and(lane == 2 * j + 1 - north, inside), moved, corner)
    corner = outer_gain[...] * product(weights[...], inner_gain[...] * corner)
    corner = product(weights[...], corner) + lanes
    rim = jnp.logical_or(lane == 127, lane == 0)
    copies = []
    for x in list(range(1, width - 1)) + [0, width - 1]:
        for t in range(tracers):
            j = t * width + x
            value = part(partial, j, levels) + spread[...] * incr[j:j + 1, :]
            value = value + jnp.where(rim, at_edges(corner if x in (0, width - 1) else lanes, j), 0.0)
            if x in (0, width - 1):
                value = value + part(edges, (0 if x == 0 else tracers) + t, levels)
            done[j] = value
            copy = pltpu.make_async_copy(done.at[j], out.at[t, :, x, :], sems.at[j])
            copy.start()
            copies.append(copy)
    for copy in copies:
        copy.wait()


VM = pl.BlockSpec(memory_space=pltpu.VMEM)
HB = pl.BlockSpec(memory_space=pltpu.HBM)


def call(body, name, in_specs, out_shape, flops, out_specs=None, scratch=(), touched=2 << 20):
    many = isinstance(out_shape, list)
    return pl.pallas_call(
        body,
        out_shape=out_shape,
        in_specs=in_specs,
        out_specs=out_specs or ([VM] * len(out_shape) if many else VM),
        scratch_shapes=scratch,
        name=name,
        cost_estimate=pl.CostEstimate(flops=flops, bytes_accessed=touched, transcendentals=0),
        compiler_params=pltpu.CompilerParams(vmem_limit_bytes=32 * 1024 * 1024),
    )


def on_device(state, flow, diffusion, column_solve, exchange_rate, block_map, ice_mask):
    _, tracers, levels, width, wide = state.shape
    mer_count, zon_count = lax.axis_size("mer"), lax.axis_size("zon")
    rounds = 1 if mer_count == 2 else 2
    dims = (tracers, levels, width)
    size, total = levels * width, tracers * width
    shape = lambda rows, dtype=f32: jax.ShapeDtypeStruct((rows, wide), dtype)
    message = shape((2 * tracers + 2) * levels)
    blocks = jax.ShapeDtypeStruct((2 * tracers + 2, levels, wide), f32)
    packed = shape(levels)
    folded = shape(levels // 2 + 8)
    kept = shape(tracers * size)
    halved = shape(tracers * levels)
    sided = shape(2 * tracers * levels)

    def swap_mer(pieces):
        return [lax.ppermute(piece, "mer", pairs(mer_count, r == 1)) for r, piece in enumerate(pieces)]

    def shift_zonal(piece, ahead):
        return lax.ppermute(piece, "zon", ring(zon_count, ahead))

    def widen(piece):
        return piece.astype(f32) * (1.0 / SCALE)

    def swap_fluid(piece):
        return lax.ppermute(piece, "fluid", [(0, 1), (1, 0)])

    params = (diffusion[0], column_solve[0], exchange_rate, block_map[None], ice_mask[None])
    in_hbm = [pltpu.with_memory_space_constraint(value, pltpu.HBM) for value in (state[0], flow[0]) + params]
    east_bound, west_bound, surface, frame, *params = call(
        functools.partial(pack_kernel, dims), "pack", [HB] * len(in_hbm),
        [blocks, blocks, jax.ShapeDtypeStruct((tracers, width, wide), f32), shape(2 * size)] + [jax.ShapeDtypeStruct(p.shape, p.dtype) for p in params], 1 << 20,
        scratch=[pltpu.VMEM((2, levels, width, wide), bf16),
                 pltpu.SemaphoreType.DMA((7 + len(params),))],
    )(*in_hbm)
    east_bound, west_bound, surface = (value.reshape(-1, wide) for value in (east_bound, west_bound, surface))
    east_bound, west_bound = lax.optimization_barrier(((east_bound * SCALE).astype(jnp.float16), (west_bound * SCALE).astype(jnp.float16)))
    from_west = widen(shift_zonal(east_bound, 1))
    columns, own_mer, nu, weights, spread, guide = call(
        functools.partial(lanes_kernel, dims), "lanes", [VM] * 7,
        [kept, packed, shape(tracers * levels), jax.ShapeDtypeStruct((levels, 3 * levels), bf16), packed, shape(8)], 1 << 20,
    )(state.reshape(tracers * size, wide), frame, *params)
    recv_mer = swap_mer([own_mer] * rounds)
    other = swap_fluid(surface)
    from_east = shift_zonal(west_bound, -1)
    partial, strips, edge_lanes, rows = call(
        functools.partial(inner_kernel, dims), "inner", [VM] * 5, [kept, shape(2 * size), packed, shape(total)], 1 << 30,
    )(columns, frame, nu, weights, other)
    from_east, from_west = lax.optimization_barrier((from_east, from_west))
    from_east = widen(from_east)
    west_solved, east_solved, incr, half_surface, *send_mer = call(
        functools.partial(join_kernel, dims), "join", [VM] * 11, [halved, halved, shape(total), shape(total)] + [folded] * rounds, 1 << 33,
    )(strips, nu, weights, spread, edge_lanes, rows, guide, surface, other, from_west, from_east)
    recv_again = swap_mer(send_mer)
    lanes, beyond, fresh_surface = call(
        functools.partial(meet_kernel, dims, mer_count), "meet", [VM] * (5 + rounds), [packed, packed, shape(total + 2 * tracers)], 1 << 33,
    )(weights, own_mer, half_surface, from_west, from_east, *recv_mer)
    fresh_other = swap_fluid(fresh_surface)
    again = call(
        functools.partial(again_kernel, dims), "again", [VM] * 9, kept, 1 << 10, touched=1 << 10, scratch=[pltpu.VMEM((tracers * size, wide), f32)],
    )(partial, strips, nu, weights, spread, west_solved, east_solved, lanes, incr)
    edges, flux, inner_gain, outer_gain = call(
        functools.partial(sides_kernel, dims), "sides", [VM] * 9, [sided, shape(total), packed, packed], 1 << 10, touched=1 << 10,
    )(columns, strips, nu, weights, guide, fresh_surface, fresh_other, from_west, from_east)
    done = call(
        functools.partial(last_kernel, dims, mer_count), "last", [VM] * (9 + rounds),
        jax.ShapeDtypeStruct(state.shape[1:], f32), 1 << 26,
        out_specs=pl.BlockSpec(memory_space=pl.ANY),
        scratch=[pltpu.VMEM((total, levels, wide), f32), pltpu.SemaphoreType.DMA((total,))],
    )(again, edges, flux, weights, spread, own_mer, beyond, inner_gain, outer_gain, *recv_again)
    return done[None]


def solution(mesh):
    return jax.shard_map(
        on_device,
        mesh=mesh,
        in_specs=(
            P("fluid", None, None, "zon", "mer"),
            P("fluid", None, None, "zon", "mer"),
            P("fluid", None, None),
            P("fluid", None, None),
            P("fluid", None),
            P("mer"),
            P("mer"),
        ),
        out_specs=P("fluid", None, None, "zon", "mer"),
        check_vma=False,
    )
```

```python
import functools

import jax
import jax.numpy as jnp
from jax import lax
from jax.experimental import pallas as pl
from jax.experimental.pallas import tpu as pltpu
from jax.sharding import PartitionSpec as P

f32, bf16 = jnp.float32, jnp.bfloat16


SCALE = 8192.0


def ring(count, ahead):
    return [(i, (i + ahead) % count) for i in range(count)]


def pairs(count, odd):
    if odd:
        return [(i, ((i + 1) ^ 1) - 1) for i in range(1, count - 1)] + [(0, count - 1), (count - 1, 0)]
    return [(i, i ^ 1) for i in range(count)]


def side_of(east, width):
    return width - 1 if east else 0


def surface_level(levels):
    return jnp.where(lax.axis_index("fluid") == 0, levels - 1, 0)


def lanes_of(levels):
    return lax.broadcasted_iota(jnp.int32, (levels, 128), 1)


def split(value):
    high = value.astype(bf16)
    return high, (value - high.astype(f32)).astype(bf16)


def product(weights, value):
    high, low = split(value)
    return jnp.dot(weights, jnp.concatenate([high, low, high], axis=0), preferred_element_type=f32)


def part(ref, index, levels):
    return ref[index * levels:(index + 1) * levels, :]


def fold(value):
    half = value.shape[0] // 2
    lane = lanes_of(half)
    return jnp.where(lane < 64, value[:half], pltpu.roll(value[half:], 64, 1))


def unfold(value):
    return jnp.concatenate([value, pltpu.roll(value, 64, 1)], axis=0)


def mer_sides(recv_mer, mer_count):
    place = lax.axis_index("mer")
    even = 1 - lax.rem(place, 2)
    for r, value in enumerate(recv_mer):
        north = even if r == 0 else 1 - even
        yield value, north, jnp.where(north == 1, place + 1 < mer_count, place > 0)


def mer_halo(recv_mer, levels, mer_count):
    lane = lanes_of(levels)
    total = jnp.zeros((levels, 128), f32)
    for value, north, inside in mer_sides(recv_mer, mer_count):
        keep = jnp.logical_and(jnp.logical_and(lane % 2 == 1 - north, lane < 64), inside)
        total = total + jnp.where(keep, pltpu.roll(value, jnp.where(north == 1, 127, 1), 1), 0.0)
    return total


def both_edges(cells, j):
    return pltpu.roll(cells, 2 * j + 1, 1)


def at_edges(packed, j):
    return pltpu.roll(packed, (127 - 2 * j) % 128, 1)


def increments(own, other, guide, tracers, per_tracer):
    is_atm = lax.axis_index("fluid") == 0
    pick = lambda row: jnp.broadcast_to(guide[row:row + 1, :].astype(jnp.int32), own.shape)
    atm = jnp.where(is_atm, own, other)
    ocean = jnp.where(is_atm, other, own)
    flux = (jnp.take_along_axis(atm, pick(0), axis=1) - ocean) * guide[2:3, :]
    returned = jnp.take_along_axis(flux, pick(1), axis=1)
    tracer = lax.broadcasted_iota(jnp.int32, own.shape, 0) // per_tracer % tracers
    scale = jnp.broadcast_to(guide[3:4, :], own.shape)
    for t in range(1, tracers):
        scale = jnp.where(tracer == t, guide[3 + t:4 + t, :], scale)
    return jnp.where(is_atm, -returned, flux) * scale


def fill_guide(guide, rate, block_map, ice_mask, tracers):
    blocks = block_map.shape[1]
    lane = lax.broadcasted_iota(jnp.int32, (1, 128), 1)
    wide = 128 // blocks
    block, within = lane // wide, lane % wide
    first = lax.axis_index("mer") * blocks
    mapped = jnp.zeros((1, 128), jnp.int32)
    returned = jnp.zeros((1, 128), jnp.int32)
    is_open = jnp.zeros((1, 128), jnp.int32)
    for b in range(blocks):
        above = block_map[:, b:b + 1] - first
        mapped = jnp.where(block == b, above, mapped)
        returned = jnp.where(block == above, b, returned)
        is_open = jnp.where(block == b, 1 - ice_mask[:, b:b + 1], is_open)
    guide[...] = jnp.zeros(guide.shape, f32)
    guide[0:1, :] = (mapped * wide + within).astype(f32)
    guide[1:2, :] = (returned * wide + within).astype(f32)
    guide[2:3, :] = is_open.astype(f32)
    for t in range(tracers):
        guide[3 + t:4 + t, :] = jnp.broadcast_to(rate[:, t:t + 1], (1, 128))


def horizontal(q, east, west, c, d, nu, lane):
    north = jnp.where(lane == 127, 0.0, pltpu.roll(q, 127, 1))
    south = jnp.where(lane == 0, 0.0, pltpu.roll(q, 1, 1))
    return q - c * (east - west) - d * (north - south) + nu * ((east + west) + (north + south) - 4.0 * q)


def interior(column, strip, nu, weights, store, dims):
    tracers, levels, width = dims
    lane = lanes_of(levels)
    zero = jnp.zeros((levels, 128), f32)
    for x in range(width):
        c, d = strip(0, x), strip(1, x)
        terms = []
        for t in range(tracers):
            west = zero if x == 0 else column(t, x - 1)
            east = zero if x == width - 1 else column(t, x + 1)
            terms.append(horizontal(column(t, x), east, west, c, d, part(nu, t, levels), lane))
        solved = product(weights[...], jnp.concatenate(terms, axis=1))
        for t in range(tracers):
            store(t, x, solved[:, t * 128:(t + 1) * 128])


def pack_kernel(dims, state, flow, *rest):
    tracers, levels, width = dims
    size = levels * width
    fixed = len(rest) - 6 >> 1
    east_bound, west_bound, surface, frame = rest[fixed:fixed + 4]
    raw, sems = rest[2 * fixed + 4:]
    level = surface_level(levels)
    transfers = [(flow.at[k], raw.at[k]) for k in range(2)]
    for ref, places in ((east_bound, (width - 1, width - 2)), (west_bound, (0, 1))):
        for i, x in enumerate(places):
            transfers.append((state.at[:, :, x, :], ref.at[pl.ds(i * tracers, tracers)]))
    transfers.append((state.at[:, level], surface))
    transfers += [(rest[i], rest[fixed + 4 + i]) for i in range(fixed)]
    copies = [pltpu.make_async_copy(source, target, sems.at[i]) for i, (source, target) in enumerate(transfers)]
    for copy in copies:
        copy.start()
    wait_flow, copies = copies[:2], copies[2:]
    for k, copy in enumerate(wait_flow):
        copy.wait()
        frame[k * size:(k + 1) * size, :] = raw[k].reshape(size, 128).astype(f32) * 0.5
        for ref, x in ((east_bound, width - 1), (west_bound, 0)):
            strip = frame[pl.ds(k * size + x, levels, stride=width), :]
            ref[2 * tracers + k] = strip
    for copy in copies:
        copy.wait()


def lay_out(dims, frame, strips):
    tracers, levels, width = dims
    for k in range(2):
        for x in range(width):
            value = frame[pl.ds(k * levels * width + x, levels, stride=width), :]
            strips[(k * width + x) * levels:(k * width + x + 1) * levels, :] = value


def lanes_kernel(dims, cells, frame, diffusion, solve, rate, block_map, ice_mask, columns, send_mer, nu, weights, spread, guide, strips):
    tracers, levels, width = dims
    size = levels * width
    lane = lanes_of(levels)
    packed = jnp.zeros((levels, 128), f32)
    merid = jnp.zeros((levels, 128), f32)
    gain = jnp.zeros((levels, 128), f32)
    for x in range(width):
        strip = frame[pl.ds(size + x, levels, stride=width), :]
        merid = jnp.where(lane // 2 == x, both_edges(strip, x), merid)
    for t in range(tracers):
        for x in range(width):
            j = t * width + x
            value = cells[pl.ds(t * size + x, levels, stride=width), :]
            columns[j * levels:(j + 1) * levels, :] = value
            packed = jnp.where(lane // 2 == j, both_edges(value, j), packed)
        mine = jnp.transpose(jnp.broadcast_to(diffusion[t:t + 1, :], (128, levels)))
        nu[t * levels:(t + 1) * levels, :] = mine
        turned = merid if t == 0 else pltpu.roll(merid, 2 * t * width, 1)
        mine = mine + jnp.where(lane % 2 == 0, -turned, turned)
        gain = jnp.where(lane // (2 * width) == t, mine, gain)
    send_mer[...] = jnp.where(lane < 64, packed, pltpu.roll(gain, 64, 1))
    high, low = split(solve[...])
    weights[...] = jnp.concatenate([high, high, low], axis=1)
    at_level = lax.broadcasted_iota(jnp.int32, (levels, levels), 1) == surface_level(levels)
    fill_guide(guide, rate, block_map, ice_mask, tracers)
    spread[...] = jnp.broadcast_to(jnp.sum(jnp.where(at_level, solve[...], 0.0), axis=1, keepdims=True), (levels, 128))

    @pl.when(lax.rem(lax.axis_index("mer"), 2) == 0)
    def _():
        lay_out(dims, frame, strips)


def inner_kernel(dims, columns, frame, nu, weights, other, _, partial, strips, edge_lanes, rows):
    tracers, levels, width = dims
    lane = lanes_of(levels)

    @pl.when(lax.rem(lax.axis_index("mer"), 2) == 1)
    def _():
        lay_out(dims, frame, strips)

    def store(t, x, value):
        j = t * width + x
        partial[j * levels:(j + 1) * levels, :] = value

    column = lambda t, x: part(columns, t * width + x, levels)
    strip = lambda k, x: part(strips, k * width + x, levels)
    interior(column, strip, nu, weights, store, dims)
    packed = jnp.zeros((levels, 128), f32)
    for j in range(tracers * width):
        packed = jnp.where(lane // 2 == j, both_edges(part(partial, j, levels), j), packed)
    edge_lanes[...] = packed
    rows[...] = partial[pl.ds(surface_level(levels), tracers * width, stride=levels), :]


def side_terms(ref, east, strips, nu, dims):
    tracers, levels, width = dims
    c = part(strips, side_of(east, width), levels)
    return [(part(nu, t, levels) + (-c if east else c)) * part(ref, t, levels) for t in range(tracers)]


def side_lanes(packed, east, solved, lane, dims):
    tracers, levels, width = dims
    for t in range(tracers):
        j = t * width + side_of(east, width)
        packed = packed + jnp.where(lane // 2 == j, both_edges(part(solved, t, levels), j), 0.0)
    return packed


def side_rows(fresh, east, solved, row, level, dims):
    tracers, levels, width = dims
    for t in range(tracers):
        line = solved[pl.ds(t * levels + level, 1), :]
        fresh = fresh + jnp.where(row == t * width + side_of(east, width), line, 0.0)
    return fresh


def join_kernel(dims, strips, nu, weights, spread, edge_lanes, rows, guide, own, other, from_west, from_east, west_solved, east_solved, incr, surface, *send_mer):
    tracers, levels, width = dims
    total = tracers * width
    lane = lanes_of(levels)
    terms = side_terms(from_west, False, strips, nu, dims) + side_terms(from_east, True, strips, nu, dims)
    result = product(weights[...], jnp.concatenate(terms, axis=1))
    flux = increments(own[...], other[...], guide, tracers, width)
    incr[...] = flux
    row = lax.broadcasted_iota(jnp.int32, (total, 128), 0)
    rows_lane = lax.broadcasted_iota(jnp.int32, (total, 128), 1)
    turned = pltpu.roll(flux, 1, 1, stride=2, stride_axis=0)
    turned = jnp.sum(jnp.where(rows_lane // 2 == row, turned, 0.0), axis=0, keepdims=True)
    packed = edge_lanes[...] + spread[...] * turned
    for t in range(tracers):
        west_solved[t * levels:(t + 1) * levels, :] = result[:, t * 128:(t + 1) * 128]
        east_solved[t * levels:(t + 1) * levels, :] = result[:, (tracers + t) * 128:(tracers + t + 1) * 128]
    packed = side_lanes(side_lanes(packed, False, west_solved, lane, dims), True, east_solved, lane, dims)
    place = lax.axis_index("mer")
    for r, ref in enumerate(send_mer):
        up = lax.rem(place + 1 + r, 2)
        message = packed
        for s, cells in enumerate((from_west, from_east)):
            for t in range(tracers):
                at = s * tracers + t
                moved = pltpu.roll(part(cells, t, levels), 2 * at + 2 * up, 1)
                message = jnp.where(lane == 2 * at + up, moved, message)
        ref[:levels // 2, :] = fold(message)
        ref[levels // 2:, :] = jnp.zeros((ref.shape[0] - levels // 2, 128), f32)
    level = surface_level(levels)
    fresh = rows[...] + spread[pl.ds(level, 1), :] * flux
    fresh = side_rows(fresh, False, west_solved, row, level, dims)
    surface[...] = side_rows(fresh, True, east_solved, row, level, dims)


def meet_kernel(dims, mer_count, weights, own_mer, half_surface, from_west, from_east, *rest):
    tracers, levels, width = dims
    total = tracers * width
    rounds = len(rest) - 3
    recv_mer, (lanes, beyond, surface) = [ref[...] for ref in rest[:rounds]], rest[rounds:]
    lane = lanes_of(levels)
    edge = jnp.where(lane < 64, own_mer[...], 0.0)
    gain = jnp.where(lane < 64, pltpu.roll(own_mer[...], 64, 1), 0.0)
    here = gain * mer_halo(recv_mer, levels, mer_count)
    there = edge * mer_halo([pltpu.roll(value, 64, 1) for value in recv_mer], levels, mer_count)
    result = product(weights[...], jnp.concatenate([here, there], axis=1))
    lanes[...] = result[:, :128]
    beyond[...] = result[:, 128:]
    row = lax.broadcasted_iota(jnp.int32, (total, 128), 0)
    rows_lane = lax.broadcasted_iota(jnp.int32, (total, 128), 1)
    line = jnp.broadcast_to(lanes[pl.ds(surface_level(levels), 1), :], (total, 128))
    line = jnp.take_along_axis(line, 2 * row + (rows_lane == 0).astype(jnp.int32), axis=1)
    rim = jnp.logical_or(rows_lane == 127, rows_lane == 0)
    surface[:total, :] = half_surface[...] + jnp.where(rim, line, 0.0)
    level = surface_level(levels)
    for s, cells in enumerate((from_west, from_east)):
        for t in range(tracers):
            at = total + s * tracers + t
            surface[at:at + 1, :] = cells[pl.ds(t * levels + level, 1), :]


def again_kernel(dims, partial, strips, nu, weights, spread, west_solved, east_solved, lanes, incr, again, fresh):
    tracers, levels, width = dims
    lane = lanes_of(levels)
    rim = jnp.logical_or(lane == 127, lane == 0)
    for t in range(tracers):
        for x in range(width):
            j = t * width + x
            value = part(partial, j, levels) + spread[...] * incr[j:j + 1, :]
            value = value + jnp.where(rim, at_edges(lanes[...], j), 0.0)
            if x in (0, width - 1):
                value = value + part(west_solved if x == 0 else east_solved, t, levels)
            fresh[j * levels:(j + 1) * levels, :] = value

    def store(t, x, value):
        again[pl.ds((t * width + x) * levels, levels), :] = value

    column = lambda t, x: part(fresh, t * width + x, levels)
    strip = lambda k, x: part(strips, k * width + x, levels)
    interior(column, strip, nu, weights, store, dims)


def sides_kernel(dims, columns, strips, nu, weights, guide, own, other, from_west, from_east, edges, flux, inner_gain, outer_gain):
    tracers, levels, width = dims
    total = tracers * width
    lane = lanes_of(levels)
    flux[...] = increments(own[:total, :], other[:total, :], guide, tracers, width)
    extra = increments(own[total:, :], other[total:, :], guide, tracers, 1)
    at_level = lax.broadcasted_iota(jnp.int32, (levels, 128), 0) == surface_level(levels)
    terms, gains = [], []
    first = jnp.zeros((levels, 128), f32)
    later = jnp.zeros((levels, 128), f32)
    for s, ref in enumerate((from_west, from_east)):
        x = side_of(s == 1, width)
        c, d = (part(ref, 2 * tracers + k, levels) for k in range(2))
        own_c = part(strips, x, levels)
        for t in range(tracers):
            mine, beyond = part(columns, t * width + x, levels), part(ref, tracers + t, levels)
            west, east = (mine, beyond) if s == 1 else (beyond, mine)
            value = horizontal(part(ref, t, levels), east, west, c, d, part(nu, t, levels), lane)
            value = value + jnp.where(at_level, jnp.broadcast_to(extra[s * tracers + t:s * tracers + t + 1, :], value.shape), 0.0)
            terms.append(value)
            gain = part(nu, t, levels) + (-own_c if s == 1 else own_c)
            gains.append(gain)
            j = t * width + x
            here = lane // 2 == j
            packed = both_edges(d, j)
            first = jnp.where(here, part(nu, t, levels) + jnp.where(lane % 2 == 0, -packed, packed), first)
            later = jnp.where(here, both_edges(gain, j), later)
    inner_gain[...] = first
    outer_gain[...] = later
    result = product(weights[...], jnp.concatenate(terms, axis=1))
    result = product(weights[...], result * jnp.concatenate(gains, axis=1))
    for i in range(2 * tracers):
        edges[i * levels:(i + 1) * levels, :] = result[:, i * 128:(i + 1) * 128]


def last_kernel(dims, mer_count, partial, edges, incr, weights, spread, own_mer, beyond, inner_gain, outer_gain, *rest):
    tracers, levels, width = dims
    rounds = len(rest) - 3
    recv_mer, (out, done, sems) = [unfold(ref[:levels // 2, :]) for ref in rest[:rounds]], rest[rounds:]
    lane = lanes_of(levels)
    halo = mer_halo(recv_mer, levels, mer_count) + beyond[...]
    gain = jnp.where(lane < 64, pltpu.roll(own_mer[...], 64, 1), 0.0)
    lanes = product(weights[...], gain * halo)
    corner = jnp.zeros((levels, 128), f32)
    for value, north, inside in mer_sides(recv_mer, mer_count):
        for s in range(2):
            for t in range(tracers):
                j = t * width + side_of(s == 1, width)
                moved = pltpu.roll(value, 2 * (j - s * tracers - t) % 128, 1)
                corner = jnp.where(jnp.logical_and(lane == 2 * j + 1 - north, inside), moved, corner)
    corner = outer_gain[...] * product(weights[...], inner_gain[...] * corner)
    corner = product(weights[...], corner) + lanes
    rim = jnp.logical_or(lane == 127, lane == 0)
    copies = []
    for x in list(range(1, width - 1)) + [0, width - 1]:
        for t in range(tracers):
            j = t * width + x
            value = part(partial, j, levels) + spread[...] * incr[j:j + 1, :]
            value = value + jnp.where(rim, at_edges(corner if x in (0, width - 1) else lanes, j), 0.0)
            if x in (0, width - 1):
                value = value + part(edges, (0 if x == 0 else tracers) + t, levels)
            done[j] = value
            copy = pltpu.make_async_copy(done.at[j], out.at[t, :, x, :], sems.at[j])
            copy.start()
            copies.append(copy)
    for copy in copies:
        copy.wait()


VM = pl.BlockSpec(memory_space=pltpu.VMEM)
HB = pl.BlockSpec(memory_space=pltpu.HBM)


def call(body, name, in_specs, out_shape, flops, out_specs=None, scratch=(), touched=2 << 20, aliases=None):
    many = isinstance(out_shape, list)
    return pl.pallas_call(
        body,
        out_shape=out_shape,
        in_specs=in_specs,
        out_specs=out_specs or ([VM] * len(out_shape) if many else VM),
        scratch_shapes=scratch,
        name=name,
        input_output_aliases=aliases or {},
        cost_estimate=pl.CostEstimate(flops=flops, bytes_accessed=touched, transcendentals=0),
        compiler_params=pltpu.CompilerParams(vmem_limit_bytes=32 * 1024 * 1024),
    )


def on_device(state, flow, diffusion, column_solve, exchange_rate, block_map, ice_mask):
    _, tracers, levels, width, wide = state.shape
    mer_count, zon_count = lax.axis_size("mer"), lax.axis_size("zon")
    rounds = 1 if mer_count == 2 else 2
    dims = (tracers, levels, width)
    size, total = levels * width, tracers * width
    shape = lambda rows, dtype=f32: jax.ShapeDtypeStruct((rows, wide), dtype)
    message = shape((2 * tracers + 2) * levels)
    blocks = jax.ShapeDtypeStruct((2 * tracers + 2, levels, wide), f32)
    packed = shape(levels)
    folded = shape(levels // 2 + 8)
    kept = shape(tracers * size)
    halved = shape(tracers * levels)
    sided = shape(2 * tracers * levels)

    def swap_mer(pieces):
        return [lax.ppermute(piece, "mer", pairs(mer_count, r == 1)) for r, piece in enumerate(pieces)]

    def shift_zonal(piece, ahead):
        return lax.ppermute(piece, "zon", ring(zon_count, ahead))

    def widen(piece):
        return piece.astype(f32) * (1.0 / SCALE)

    def swap_fluid(piece):
        return lax.ppermute(piece, "fluid", [(0, 1), (1, 0)])

    params = (diffusion[0], column_solve[0], exchange_rate, block_map[None], ice_mask[None])
    in_hbm = [pltpu.with_memory_space_constraint(value, pltpu.HBM) for value in (state[0], flow[0]) + params]
    east_bound, west_bound, surface, frame, *params = call(
        functools.partial(pack_kernel, dims), "pack", [HB] * len(in_hbm),
        [blocks, blocks, jax.ShapeDtypeStruct((tracers, width, wide), f32), shape(2 * size)] + [jax.ShapeDtypeStruct(p.shape, p.dtype) for p in params], 1 << 20,
        scratch=[pltpu.VMEM((2, levels, width, wide), bf16),
                 pltpu.SemaphoreType.DMA((7 + len(params),))],
    )(*in_hbm)
    east_bound, west_bound, surface = (value.reshape(-1, wide) for value in (east_bound, west_bound, surface))
    east_bound, west_bound = lax.optimization_barrier(((east_bound * SCALE).astype(jnp.float16), (west_bound * SCALE).astype(jnp.float16)))
    from_west = widen(shift_zonal(east_bound, 1))
    columns, own_mer, nu, weights, spread, guide, strips = call(
        functools.partial(lanes_kernel, dims), "lanes", [VM] * 7,
        [kept, packed, shape(tracers * levels), jax.ShapeDtypeStruct((levels, 3 * levels), bf16), packed, shape(8), shape(2 * size)],
        1 << 20,
    )(state.reshape(tracers * size, wide), frame, *params)
    recv_mer = swap_mer([own_mer] * rounds)
    other = swap_fluid(surface)
    from_east = shift_zonal(west_bound, -1)
    partial, strips, edge_lanes, rows = call(
        functools.partial(inner_kernel, dims), "inner", [VM] * 6, [kept, shape(2 * size), packed, shape(total)], 1 << 30,
        aliases={5: 1},
    )(columns, frame, nu, weights, other, strips)
    from_east, from_west = lax.optimization_barrier((from_east, from_west))
    from_east = widen(from_east)
    west_solved, east_solved, incr, half_surface, *send_mer = call(
        functools.partial(join_kernel, dims), "join", [VM] * 11, [halved, halved, shape(total), shape(total)] + [folded] * rounds, 1 << 33,
    )(strips, nu, weights, spread, edge_lanes, rows, guide, surface, other, from_west, from_east)
    recv_again = swap_mer(send_mer)
    lanes, beyond, fresh_surface = call(
        functools.partial(meet_kernel, dims, mer_count), "meet", [VM] * (5 + rounds), [packed, packed, shape(total + 2 * tracers)], 1 << 33,
    )(weights, own_mer, half_surface, from_west, from_east, *recv_mer)
    fresh_other = swap_fluid(fresh_surface)
    again = call(
        functools.partial(again_kernel, dims), "again", [VM] * 9, kept, 1 << 10, touched=1 << 10, scratch=[pltpu.VMEM((tracers * size, wide), f32)],
    )(partial, strips, nu, weights, spread, west_solved, east_solved, lanes, incr)
    edges, flux, inner_gain, outer_gain = call(
        functools.partial(sides_kernel, dims), "sides", [VM] * 9, [sided, shape(total), packed, packed], 1 << 10, touched=1 << 10,
    )(columns, strips, nu, weights, guide, fresh_surface, fresh_other, from_west, from_east)
    done = call(
        functools.partial(last_kernel, dims, mer_count), "last", [VM] * (9 + rounds),
        jax.ShapeDtypeStruct(state.shape[1:], f32), 1 << 26,
        out_specs=pl.BlockSpec(memory_space=pl.ANY),
        scratch=[pltpu.VMEM((total, levels, wide), f32), pltpu.SemaphoreType.DMA((total,))],
    )(again, edges, flux, weights, spread, own_mer, beyond, inner_gain, outer_gain, *recv_again)
    return done[None]


def solution(mesh):
    return jax.shard_map(
        on_device,
        mesh=mesh,
        in_specs=(
            P("fluid", None, None, "zon", "mer"),
            P("fluid", None, None, "zon", "mer"),
            P("fluid", None, None),
            P("fluid", None, None),
            P("fluid", None),
            P("mer"),
            P("mer"),
        ),
        out_specs=P("fluid", None, None, "zon", "mer"),
        check_vma=False,
    )
```
